32 devices in a mesh: groups: 2 (over y), row: 4 (over z), col: 2 (over x), sub: 2 (over core).
Axes of the slice: x: 2, y: 2, z: 4, core: 2. Of those that a mesh axis runs over, the one named last changes fastest.
Arguments:
- student: bfloat16 [1024, 1024], P(('groups', 'row', 'col'), 'sub'), parts along dimension 0, may hold values from -0.1875 to 0.1875
- teacher: bfloat16 [1024, 4096], P(('groups', 'row', 'col'), 'sub'), parts along dimension 0, may hold values from -6 to 6
- scale: bfloat16 [1024], P(('groups', 'row', 'col')), parts along dimension 0, may hold values from 0.2 to 36, as said below
Outputs:
- student_grad: float32 [1024, 1024], P(('groups', 'row', 'col'), 'sub'), parts along dimension 0
The draws below stay inside these ranges and needn't reach their ends.
There are 2 independent parts, one for each index of `groups`. The reference program is written for one: setup_inputs(seed, part) draws one part's arguments, and reference() takes and returns one part's arrays. A program takes and returns all parts, laid end to end along the dimension named above; each array names one. Nothing has to cross between parts.
Inputs may be any that keep to these rules, and one draw needn't show every extreme that they name: `scale`: positive scales.
All inputs are finite; a program needn't handle non-finite values.
Results may differ from the reference program's by a relative error of at most 0.0075.
Values may be sent and summed in bfloat16 or wider, within the bound.
No kernel may reach another device: no remote copies, remote signals or barrier semaphores. Data moves between devices by JAX's collectives and lax.ppermute only.
A program may use at most 64 MiB of HBM per device.

```python
import math
import jax
import jax.numpy as jnp
from jax import lax

DS = 1024
DT = 4096
BATCH = 512


def draw_scale(key, part):
    key = jax.random.fold_in(key, 7)
    ramp = jnp.arange(BATCH, dtype=jnp.float32) / max(BATCH - 1, 1)
    base = jnp.exp(jax.random.uniform(key, (BATCH,), jnp.float32, jnp.log(0.3), jnp.log(3.0)))
    values = base * (1.0 + 2.0 * ramp)
    return values.astype(jnp.bfloat16)


def block_scale(rng, shape, pieces, smallest, top_value):
    gain, own = 1.0, jax.random.fold_in(rng, 6)
    for axis_at, blocks in pieces:
        steps = jnp.exp(jax.random.uniform(jax.random.fold_in(own, axis_at), (blocks,), jnp.float32, smallest / len(pieces), top_value / len(pieces)))
        gain = gain * jnp.repeat(steps, shape[axis_at] // blocks).reshape([-1 if axis == axis_at else 1 for axis in range(len(shape))])
    return gain


def centred(stream_key, shape, width, bound, split=(), kind=jnp.bfloat16):
    gain = block_scale(stream_key, shape, split, -0.22, 0.18) if split else 1.0
    result = jax.random.normal(stream_key, shape, jnp.float32) * width * gain
    return jnp.minimum(jnp.maximum(result, -bound), bound).astype(kind)


def setup_inputs(seed: int = 0, part: int = 0) -> dict:
    seeds = jax.random.split(jax.random.key(seed), 4)
    part_keys = jax.random.split(jax.random.fold_in(seeds[3], part), 4)
    return {
        "student": centred(part_keys[0], (BATCH, DS), 0.03125, 0.1875, ((0, 8), (1, 2))),
        "teacher": centred(part_keys[1], (BATCH, DT), 1.0, 6.0, ((0, 8), (1, 2))),
        "scale": draw_scale(jax.random.fold_in(jax.random.fold_in(seeds[3], part), 71), part),
    }


def reference(student, teacher, scale):
    xs = student.astype(jnp.float32)
    row_norm = jnp.sqrt(lax.optimization_barrier(jnp.sum(xs * xs, axis=1)))
    unit = xs / row_norm[:, None]
    unit_b = unit.astype(jnp.bfloat16)
    scales = scale.astype(jnp.float32)
    squares = lax.optimization_barrier(jnp.sum(jnp.square(teacher.astype(jnp.float32)), axis=1))
    mass = jnp.sum(scales * scales * squares) / BATCH
    block = math.gcd(512, BATCH)
    blocks = BATCH // block

    def one_block(index):
        begin = (index * block).astype(jnp.int32)
        rows_s = lax.dynamic_slice_in_dim(unit_b, begin, block, 0)
        rows_t = lax.dynamic_slice_in_dim(teacher, begin, block, 0)
        rows_c = lax.dynamic_slice_in_dim(scales, begin, block, 0)
        student_gram = jnp.dot(rows_s, unit_b.T, preferred_element_type=jnp.float32)
        teacher_gram = jnp.dot(rows_t, teacher.T, preferred_element_type=jnp.float32)
        error = student_gram - rows_c[:, None] * scales[None, :] * teacher_gram / mass
        error_b = error.astype(jnp.bfloat16)
        return 4.0 * jnp.dot(error_b, unit_b, preferred_element_type=jnp.float32)
    grads = lax.map(one_block, jnp.arange(blocks, dtype=jnp.int32)).reshape(BATCH, DS)
    along = lax.optimization_barrier(jnp.sum(grads * unit, axis=1))
    return (grads - along[:, None] * unit) / row_norm[:, None]
```

```python
import jax
import jax.numpy as jnp
from jax import lax
from jax.sharding import PartitionSpec as P

F32, BF16 = jnp.float32, jnp.bfloat16
INNER = (((1,), (1,)), ((), ()))


def shards(student, teacher, scale):
    rows, half = student.shape
    nrow, ncol = lax.axis_size("row"), lax.axis_size("col")
    batch = rows * nrow * ncol
    part = teacher.shape[1] // nrow

    scaled = (teacher.astype(F32) * scale.astype(F32)[:, None]).astype(BF16)
    by_feature = scaled.reshape(rows, nrow, part).transpose(1, 0, 2)
    spread = jnp.broadcast_to(student[None], (nrow, rows, half))
    packed = jnp.concatenate([by_feature, spread], axis=2)
    mine = lax.all_to_all(packed, "row", 0, 0, tiled=True).reshape(nrow * rows, part + half)
    pieces = [mine]
    for k in range(1, ncol):
        pieces.append(lax.ppermute(mine, "col", [(i, (i - k) % ncol) for i in range(ncol)]))
    every = jnp.concatenate(pieces, axis=0)
    teach, stud = every[:, :part], every[:, part:]

    partial = lax.dot_general(mine[:, :part], teach, INNER, preferred_element_type=F32)
    local_mass = jnp.sum(jnp.square(teach.astype(F32)))
    high = local_mass.astype(BF16)
    low = (local_mass - high.astype(F32)).astype(BF16)
    tail = jnp.concatenate([jnp.full((nrow, 8, batch), high), jnp.full((nrow, 8, batch), low)], axis=1)
    sent = jnp.concatenate([partial.reshape(nrow, rows, batch).astype(BF16), tail], axis=1)
    back = jnp.sum(lax.all_to_all(sent, "row", 0, 0, tiled=True).astype(F32), axis=0)
    teach_gram = back[:rows]
    mass_part = back[rows] + back[rows + 8]

    raw_gram = lax.dot_general(student, stud, INNER, preferred_element_type=F32)
    xs = stud.astype(F32)
    square_part = jnp.sum(xs * xs, axis=1)
    extra = jnp.concatenate([jnp.broadcast_to(square_part[None], (4, batch)), jnp.broadcast_to(mass_part[None], (4, batch))], axis=0)
    half_sums = jnp.concatenate([teach_gram, raw_gram, extra], axis=0)
    sums = half_sums + lax.ppermute(half_sums, "sub", [(0, 1), (1, 0)])
    norm = jnp.sqrt(sums[2 * rows])
    mass = sums[2 * rows + 4] / batch
    me = lax.axis_index("row") * rows
    own_norm = lax.dynamic_slice_in_dim(norm, me, rows)
    unit_b = (xs / norm[:, None]).astype(BF16)
    unit_gram = sums[rows : 2 * rows] / (own_norm[:, None] * norm[None, :])
    error_b = (unit_gram - sums[:rows] / mass[None, :]).astype(BF16)
    grads = 4.0 * jnp.dot(error_b, unit_b, preferred_element_type=F32)
    along = 4.0 * jnp.sum(error_b.astype(F32) * unit_gram, axis=1)
    unit = student.astype(F32) / own_norm[:, None]
    return (grads - along[:, None] * unit) / own_norm[:, None]


def solution(mesh):
    spec = P(("groups", "row", "col"), "sub")
    return jax.shard_map(
        shards,
        mesh=mesh,
        in_specs=(spec, spec, P(("groups", "row", "col"))),
        out_specs=spec,
        check_vma=False,
    )
```

```python
import functools

import jax
import jax.numpy as jnp
from jax import lax
from jax.experimental import pallas as pl
from jax.experimental.pallas import tpu as pltpu
from jax.sharding import PartitionSpec as P

F32, BF16 = jnp.float32, jnp.bfloat16
INNER = (((1,), (1,)), ((), ()))
TAIL = 16


def call(body, out_shape, operands, flops=0, space=pltpu.VMEM, scratch=()):
    outs = out_shape if isinstance(out_shape, (list, tuple)) else [out_shape]
    moved = sum(x.size * x.dtype.itemsize for x in list(operands) + list(outs))
    return pl.pallas_call(
        body,
        out_shape=out_shape,
        in_specs=[pl.BlockSpec(memory_space=space)] * len(operands),
        out_specs=jax.tree.map(lambda _: pl.BlockSpec(memory_space=space), out_shape),
        scratch_shapes=list(scratch),
        cost_estimate=pl.CostEstimate(flops=flops, bytes_accessed=moved, transcendentals=0),
        compiler_params=pltpu.CompilerParams(vmem_limit_bytes=min(56 << 20, (8 << 20) + 3 * moved)),
    )(*operands)


def column(row):
    n = row.shape[1]
    eye = lax.broadcasted_iota(jnp.int32, (n, n), 0) == lax.broadcasted_iota(jnp.int32, (n, n), 1)
    return jnp.sum(jnp.where(eye, row, 0.0), axis=1, keepdims=True)


def cut_kernel(nrow, teach, *refs):
    outs, sems = refs[:nrow], refs[nrow]
    part = teach.shape[1] // nrow
    z = lax.axis_index("row")
    copies = []
    for k in range(nrow):
        at = pl.multiple_of(lax.rem(z + k, nrow) * part, part)
        copies.append(pltpu.make_async_copy(teach.at[:, pl.ds(at, part)], outs[k], sems.at[k]))
    for c in copies:
        c.start()
    for c in copies:
        c.wait()


def square_kernel(stud, teach, scale, out):
    xs = stud[...].astype(F32)
    squares = jnp.sum(xs * xs, axis=1, keepdims=True)
    ts = teach[...].astype(F32)
    s = column(scale[...].astype(F32))
    mass = jnp.sum(s * s * jnp.sum(ts * ts, axis=1, keepdims=True), keepdims=True)
    lane = lax.broadcasted_iota(jnp.int32, out.shape, 1)
    out[...] = jnp.where(lane < 64, squares, mass)


def unit_kernel(stud, mine, other, scale, out):
    rows, half = stud.shape
    total = mine[...] + other[...]
    norm = jnp.sqrt(total[:, :1])
    out[:rows, :] = (stud[...].astype(F32) / norm).astype(BF16)
    mass = total[:1, 64:65]
    high = mass.astype(BF16).astype(F32)
    low = mass - high
    s = scale[...].astype(F32)
    twice = jnp.concatenate([s, s] + [jnp.zeros((1, half - 2 * rows), F32)], axis=1)
    at = lax.broadcasted_iota(jnp.int32, (TAIL, half), 0)
    tail = jnp.where(at == 0, twice, jnp.where(at == 1, high, low))
    out[rows:, :] = tail.astype(BF16)


def assemble(nrow, ncol, rows, pieces, held):
    z = lax.axis_index("row")
    for c in range(ncol):
        for j in range(nrow):
            owner = lax.rem(z - j + nrow, nrow)
            at = pl.multiple_of((owner * ncol + c) * rows, rows)
            held[pl.ds(at, rows), :] = pieces[c * nrow + j][:rows, :]


def gram_kernel(nrow, ncol, *refs):
    count = nrow * ncol
    pieces, outs, held = refs[:count], refs[count : count + nrow], refs[count + nrow]
    rows = pieces[0].shape[0]
    assemble(nrow, ncol, rows, pieces, held)
    for k in range(nrow):
        left = pieces[(nrow - k) % nrow][...]
        outs[k][...] = lax.dot_general(left, held[...], INNER, preferred_element_type=F32).astype(outs[k].dtype)


def unit_gram_kernel(nrow, ncol, rows, *refs):
    count = nrow * ncol
    pieces, (gram, vectors, units) = refs[:count], refs[count:]
    assemble(nrow, ncol, rows, pieces, units)
    gram[...] = lax.dot_general(pieces[0][:rows, :], units[...], INNER, preferred_element_type=F32)
    z = lax.axis_index("row")
    lane = lax.broadcasted_iota(jnp.int32, (TAIL, 2 * rows), 1)
    mass = jnp.zeros((TAIL, 2 * rows), F32)
    for j in range(nrow):
        owner = lax.rem(z - j + nrow, nrow)
        for c in range(0, ncol, 2):
            first = pieces[c * nrow + j][rows:, : 2 * rows].astype(F32)
            second = pieces[(c + 1) * nrow + j][rows:, : 2 * rows].astype(F32)
            at = pl.multiple_of((owner * ncol + c) * rows, 2 * rows)
            vectors[0:8, pl.ds(at, 2 * rows)] = jnp.where(lane < rows, first, second)[0:8]
            mass = mass + first + second
    total = mass[1:2, 0:1] + mass[2:3, 0:1]
    vectors[8:16, :] = jnp.broadcast_to(total, (8, vectors.shape[1]))


def sum_kernel(*refs):
    ins, out = refs[:-1], refs[-1]
    total = ins[0][...].astype(F32)
    for r in ins[1:]:
        total = total + r[...].astype(F32)
    out[...] = total


def final_kernel(nrow, ncol, batch, mine, other, gram_mine, gram_other, vectors, stud, sq_mine, sq_other, scale, *refs):
    if len(refs) > 2:
        pieces, out, units = refs[:-2], refs[-2], refs[-1]
        assemble(nrow, ncol, stud.shape[0], pieces, units)
    else:
        units, out = refs
    norm = jnp.sqrt(sq_mine[:, :1] + sq_other[:, :1])
    mass = vectors[8:9, 0:1] / batch
    unit_gram = gram_mine[...] + gram_other[...]
    outer = column(scale[...].astype(F32)) * vectors[0:1, :]
    error = unit_gram - outer * (mine[...] + other[...]) / mass
    error_b = error.astype(BF16)
    grads = 4.0 * jnp.dot(error_b, units[...], preferred_element_type=F32)
    along = 4.0 * jnp.sum(error_b.astype(F32) * unit_gram, axis=1, keepdims=True)
    unit = stud[...].astype(F32) / norm
    out[...] = (grads - along * unit) / norm


def shards(student, teacher, scale):
    rows, half = student.shape
    nrow, ncol = lax.axis_size("row"), lax.axis_size("col")
    batch = rows * nrow * ncol
    part = teacher.shape[1] // nrow
    sds = jax.ShapeDtypeStruct
    scale = scale.reshape(1, rows)

    def along_row(x, k):
        return lax.ppermute(x, "row", [(i, (i + k) % nrow) for i in range(nrow)])

    def along_col(x, c):
        return lax.ppermute(x, "col", [(i, (i - c) % ncol) for i in range(ncol)])

    def other_core(x):
        return lax.ppermute(x, "sub", [(0, 1), (1, 0)])

    cuts = call(
        functools.partial(cut_kernel, nrow),
        [sds((rows, part), BF16)] * nrow,
        [teacher],
        space=pl.ANY,
        scratch=[pltpu.SemaphoreType.DMA((nrow,))],
    )
    teach = [cuts[0]] + [along_row(cuts[k], k) for k in range(1, nrow)]
    teach += [along_col(t, c) for c in range(1, ncol) for t in teach[:nrow]]

    squares = call(square_kernel, sds((rows, 128), F32), [student, teacher, scale])
    squares_other = other_core(squares)
    unit = call(unit_kernel, sds((rows + TAIL, half), BF16), [student, squares, squares_other, scale])
    units = [unit] + [along_row(unit, k) for k in range(1, nrow)]
    units += [along_col(u, c) for c in range(1, ncol) for u in units[:nrow]]

    partial = call(
        functools.partial(gram_kernel, nrow, ncol),
        [sds((rows, batch), F32)] + [sds((rows, batch), BF16)] * (nrow - 1),
        teach,
        flops=2 * rows * nrow * batch * part,
        scratch=[pltpu.VMEM((batch, part), BF16)],
    )
    returned = [partial[0]] + [along_row(partial[k], k) for k in range(1, nrow)]
    teach_gram = call(sum_kernel, sds((rows, batch), F32), returned)
    teach_gram_other = other_core(teach_gram)

    keep = batch <= 2048
    held = [] if keep else [pltpu.VMEM((batch, half), BF16)]
    unit_gram, vectors, *all_units = call(
        functools.partial(unit_gram_kernel, nrow, ncol, rows),
        [sds((rows, batch), F32), sds((16, batch), F32)] + ([sds((batch, half), BF16)] if keep else []),
        units,
        flops=2 * rows * batch * half,
        scratch=held,
    )
    unit_gram_other = other_core(unit_gram)
    return call(
        functools.partial(final_kernel, nrow, ncol, batch),
        sds((rows, half), F32),
        [teach_gram, teach_gram_other, unit_gram, unit_gram_other, vectors, student, squares, squares_other, scale]
        + (all_units if keep else units),
        flops=2 * rows * batch * half,
        scratch=held,
    )


def solution(mesh):
    spec = P(("groups", "row", "col"), "sub")
    return jax.shard_map(
        shards,
        mesh=mesh,
        in_specs=(spec, spec, P(("groups", "row", "col"))),
        out_specs=spec,
        check_vma=False,
    )
```

```python
import functools

import jax
import jax.numpy as jnp
from jax import lax
from jax.experimental import pallas as pl
from jax.experimental.pallas import tpu as pltpu
from jax.sharding import PartitionSpec as P

F32, BF16 = jnp.float32, jnp.bfloat16
INNER = (((1,), (1,)), ((), ()))
TAIL = 16


def call(body, out_shape, operands, flops=0, space=pltpu.VMEM, scratch=(), after=()):
    outs = out_shape if isinstance(out_shape, (list, tuple)) else [out_shape]
    moved = sum(x.size * x.dtype.itemsize for x in list(operands) + list(outs))

    def run(*refs):
        body(*refs[: len(operands)], *refs[len(operands) + len(after) :])

    return pl.pallas_call(
        run,
        out_shape=out_shape,
        in_specs=[pl.BlockSpec(memory_space=space)] * len(operands) + [pl.BlockSpec(memory_space=pl.ANY)] * len(after),
        out_specs=jax.tree.map(lambda _: pl.BlockSpec(memory_space=space), out_shape),
        scratch_shapes=list(scratch),
        cost_estimate=pl.CostEstimate(flops=flops, bytes_accessed=moved, transcendentals=0),
        compiler_params=pltpu.CompilerParams(vmem_limit_bytes=min(56 << 20, (8 << 20) + 3 * moved)),
    )(*operands, *after)


def column(row, first=0, count=None):
    shape = (count or row.shape[1], row.shape[1])
    eye = lax.broadcasted_iota(jnp.int32, shape, 0) + first == lax.broadcasted_iota(jnp.int32, shape, 1)
    return jnp.sum(jnp.where(eye, row, 0.0), axis=1, keepdims=True)


def tags_of(scales, mass):
    shape = (TAIL, scales.shape[1])
    at = lax.broadcasted_iota(jnp.int32, shape, 0)
    high = mass.astype(BF16).astype(F32)
    return jnp.where(at < 8, scales, jnp.where(at < 12, high, mass - high)).astype(BF16)


def read_tags(tags):
    tags = tags.astype(F32)
    return tags[0:1, :], tags[8:9, 0:1] + tags[12:13, 0:1]


def cut_kernel(nrow, teach, *refs):
    outs, sems = refs[:nrow], refs[nrow]
    part = teach.shape[1] // nrow
    z = lax.axis_index("row")
    copies = []
    for k in range(nrow):
        at = pl.multiple_of((z ^ k) * part, part)
        copies.append(pltpu.make_async_copy(teach.at[:, pl.ds(at, part)], outs[k], sems.at[k]))
    for c in copies:
        c.start()
    for c in copies:
        c.wait()


def square_kernel(stud, teach, scale, out):
    xs = stud[...].astype(F32)
    squares = jnp.sum(xs * xs, axis=1, keepdims=True)
    ts = teach[...].astype(F32)
    s = column(scale[...].astype(F32))
    mass = jnp.sum(s * s * jnp.sum(ts * ts, axis=1, keepdims=True), keepdims=True)
    lane = lax.broadcasted_iota(jnp.int32, out.shape, 1)
    out[...] = jnp.where(lane < 64, squares, mass)


def unit_kernel(stud, mine, other, scale, teach, unit, tagged):
    rows, part = teach.shape
    total = mine[...] + other[...]
    norm = jnp.sqrt(total[:, :1])
    unit[...] = (stud[...].astype(F32) / norm).astype(BF16)
    s = scale[...].astype(F32)
    tagged[:rows, :] = teach[...]
    tags = tags_of(jnp.concatenate([s, s], axis=1), total[:1, 64:65])
    tagged[rows:, :] = jnp.concatenate([tags] * (part // (2 * rows)), axis=1)


def pack_kernel(*refs):
    out, at = refs[-1], 0
    for r in refs[:-1]:
        out[at : at + r.shape[0], :] = r[...]
        at += r.shape[0]


def place(nrow, ncol, rows, k, c):
    return pl.multiple_of(((lax.axis_index("row") ^ k) * ncol + c) * rows, rows)


def assemble(nrow, ncol, rows, blocks, held):
    for c in range(ncol):
        for k, (ref, at) in blocks[c].items():
            held[pl.ds(place(nrow, ncol, rows, k, c), rows), :] = ref[at : at + rows, :]


def split(refs, groups, step):
    refs, blocks = list(refs), []
    for stack in groups:
        found = {}
        for keys in stack:
            ref = refs.pop(0)
            for n, k in enumerate(keys):
                found[k] = (ref, n * step)
        blocks.append(found)
    return blocks, refs


def gram_kernel(nrow, ncol, rows, groups, order, *refs):
    blocks, (kept, given, tags, held, left) = split(refs, groups, rows)
    assemble(nrow, ncol, rows, blocks, held)
    sub, half = rows // 2, nrow * rows // 2
    core = lax.axis_index("sub")
    for n, k in enumerate(order):
        ref, at = blocks[0][k]
        for target, which in ((0, core), (half, 1 - core)):
            rows_at = pl.multiple_of(at + which * sub, sub)
            left[target + n * sub : target + (n + 1) * sub, :] = ref[pl.ds(rows_at, sub), :]
    given[...] = lax.dot_general(left[half:, :], held[...], INNER, preferred_element_type=F32).astype(given.dtype)
    kept[...] = lax.dot_general(left[:half, :], held[...], INNER, preferred_element_type=F32).astype(kept.dtype)
    lane = lax.broadcasted_iota(jnp.int32, (TAIL, 2 * rows), 1)
    found = [[blocks[c + d][0][0][rows:, : 2 * rows].astype(F32) for d in (0, 1)] for c in range(0, ncol, 2)]
    mass = sum(read_tags(tag)[1] for pair in found for tag in pair)
    tags[...] = tags_of(jnp.zeros((1, tags.shape[1]), F32), mass)
    for c, pair in zip(range(0, ncol, 2), found):
        spot = pl.multiple_of(place(nrow, ncol, rows, 0, c), 2 * rows)
        tags[:, pl.ds(spot, 2 * rows)] = tags_of(jnp.where(lane < rows, *pair)[0:1, :], mass)


def fold_tags(tags, came, rows):
    if came.shape[0] == rows:
        return tags[...]
    (scales, mass), (more_scales, more_mass) = read_tags(tags[...]), read_tags(came[rows:, :])
    return tags_of(scales + more_scales, mass + more_mass)


def fold_kernel(kept, came, tags, keep, give, tags_out):
    rows = kept.shape[0]
    half = rows // 2
    folded = fold_tags(tags, came, rows)
    tags_out[...] = folded
    give[:half, :] = (kept[half:, :].astype(F32) + came[half:rows, :].astype(F32)).astype(BF16)
    give[half:, :] = folded
    keep[...] = (kept[:half, :].astype(F32) + came[:half, :].astype(F32)).astype(keep.dtype)


def error_kernel(batch, kept, came, tags, gram_mine, gram_other, scale, out):
    sub = kept.shape[0]
    first = lax.axis_index("sub") * sub
    at = pl.ds(pl.multiple_of(first, sub), sub)
    scales, mass = read_tags(fold_tags(tags, came, sub))
    total = kept[...].astype(F32) + came[:sub, :].astype(F32)
    outer = column(scale[...].astype(F32), first, sub) * scales
    error = gram_mine[at, :] + gram_other[at, :] - outer * total / (mass / batch)
    out[...] = error.astype(BF16)


def unit_gram_kernel(nrow, ncol, rows, groups, *refs):
    blocks, (gram, units) = split(refs, groups, rows)
    assemble(nrow, ncol, rows, blocks, units)
    own = blocks[0][0][0][:rows, :]
    gram[...] = lax.dot_general(own, units[...], INNER, preferred_element_type=F32)


def final_kernel(nrow, ncol, groups, mine, other, gram_mine, gram_other, stud, sq_mine, sq_other, *refs):
    rows = stud.shape[0]
    if groups:
        blocks, (out, error_b, units) = split(refs, groups, rows)
        assemble(nrow, ncol, rows, blocks, units)
    else:
        units, out, error_b = refs
    sub = rows // 2
    core = lax.axis_index("sub")
    error_b[pl.ds(pl.multiple_of(core * sub, sub), sub), :] = mine[...]
    error_b[pl.ds(pl.multiple_of((1 - core) * sub, sub), sub), :] = other[...]
    norm = jnp.sqrt(sq_mine[:, :1] + sq_other[:, :1])
    grads = 4.0 * jnp.dot(error_b[...], units[...], preferred_element_type=F32)
    unit_gram = gram_mine[...] + gram_other[...]
    along = 4.0 * jnp.sum(error_b[...].astype(F32) * unit_gram, axis=1, keepdims=True)
    unit = stud[...].astype(F32) / norm
    out[...] = (grads - along * unit) / norm


def shards(student, teacher, scale):
    rows, half = student.shape
    nrow, ncol = lax.axis_size("row"), lax.axis_size("col")
    batch = rows * nrow * ncol
    part = teacher.shape[1] // nrow
    small = batch <= 2048
    sds = jax.ShapeDtypeStruct
    scale = scale.reshape(1, rows)

    def along_row(x, k):
        return lax.ppermute(x, "row", [(i, i ^ k) for i in range(nrow)])

    def along_col(x, c):
        return lax.ppermute(x, "col", [(i, (i - c) % ncol) for i in range(ncol)])

    def other_core(x):
        return lax.ppermute(x, "sub", [(0, 1), (1, 0)])

    def pack(xs, after=()):
        if len(xs) == 1:
            return xs[0]
        return call(pack_kernel, sds((sum(x.shape[0] for x in xs), xs[0].shape[1]), BF16), xs, after=after)

    cuts = call(
        functools.partial(cut_kernel, nrow),
        [sds((rows, part), BF16)] * nrow,
        [teacher],
        space=pl.ANY,
        scratch=[pltpu.SemaphoreType.DMA((nrow,))],
    )
    teach = [None] + [along_row(cuts[k], k) for k in range(1, nrow)]
    squares = call(square_kernel, sds((rows, 128), F32), [student, teacher, scale], after=[cuts[0]])
    squares_other = other_core(squares)
    unit, teach[0] = call(
        unit_kernel,
        [sds((rows, half), BF16), sds((rows + TAIL, part), BF16)],
        [student, squares, squares_other, scale, cuts[0]],
        after=[teach[1]],
    )

    direct = [[k] for k in range(nrow)]
    early = nrow // 2
    teach_groups, teach_refs = [direct], list(teach)
    passed = [[along_col(t, c) for t in teach[:early]] for c in range(1, ncol)]
    late = pack(teach[early:], after=sum(passed, []))
    for c in range(1, ncol):
        teach_groups.append(direct[:early] + [list(range(early, nrow))])
        teach_refs += passed[c - 1] + [along_col(late, c)]

    stack, keys, k = unit, [0], nrow // 2
    while k > 1:
        stack = pack([stack, along_row(stack, k)])
        keys = keys + [n ^ k for n in keys]
        k //= 2
    stacks = [stack, along_row(stack, 1)]
    unit_groups = [[keys, [n ^ 1 for n in keys]]] * ncol
    units = stacks + [along_col(u, c) for c in range(1, ncol) for u in stacks]

    order = [0]
    while len(order) < nrow:
        order = [2 * n for n in order] + [2 * n + 1 for n in order]
    kept, given, tags = call(
        functools.partial(gram_kernel, nrow, ncol, rows, teach_groups, order),
        [sds((nrow * rows // 2, batch), F32 if small else BF16), sds((nrow * rows // 2, batch), BF16), sds((TAIL, batch), BF16)],
        teach_refs,
        flops=2 * rows * nrow * batch * part,
        scratch=[pltpu.VMEM((batch, part), BF16), pltpu.VMEM((nrow * rows, part), BF16)],
    )
    came, k = other_core(given), 1
    while k < nrow:
        count = kept.shape[0] // 2
        kept, give, tags = call(
            fold_kernel,
            [sds((count, batch), kept.dtype), sds((count + TAIL, batch), BF16), sds((TAIL, batch), BF16)],
            [kept, came, tags],
        )
        came = along_row(give, k)
        k *= 2

    held = [] if small else [pltpu.VMEM((batch, half), BF16)]
    unit_gram, *all_units = call(
        functools.partial(unit_gram_kernel, nrow, ncol, rows, unit_groups),
        [sds((rows, batch), F32)] + ([sds((batch, half), BF16)] if small else []),
        units,
        flops=2 * rows * batch * half,
        scratch=held,
    )
    unit_gram_other = other_core(unit_gram)
    error_b = call(
        functools.partial(error_kernel, batch),
        sds((rows // 2, batch), BF16),
        [kept, came, tags, unit_gram, unit_gram_other, scale],
    )
    return call(
        functools.partial(final_kernel, nrow, ncol, None if small else unit_groups),
        sds((rows, half), F32),
        [error_b, other_core(error_b), unit_gram, unit_gram_other, student, squares, squares_other] + (all_units if small else units),
        flops=2 * rows * batch * half,
        scratch=[pltpu.VMEM((rows, batch), BF16)] + held,
    )


def solution(mesh):
    spec = P(("groups", "row", "col"), "sub")
    return jax.shard_map(
        shards,
        mesh=mesh,
        in_specs=(spec, spec, P(("groups", "row", "col"))),
        out_specs=spec,
        check_vma=False,
    )
```

```python
import functools

import jax
import jax.numpy as jnp
from jax import lax
from jax.experimental import pallas as pl
from jax.experimental.pallas import tpu as pltpu
from jax.sharding import PartitionSpec as P

F32, BF16 = jnp.float32, jnp.bfloat16
INNER = (((1,), (1,)), ((), ()))
TAIL = 16


def call(body, out_shape, operands, space=pltpu.VMEM, scratch=(), after=()):
    outs = out_shape if isinstance(out_shape, (list, tuple)) else [out_shape]
    moved = sum(x.size * x.dtype.itemsize for x in list(operands) + list(outs))

    def run(*refs):
        body(*refs[: len(operands)], *refs[len(operands) + len(after) :])

    return pl.pallas_call(
        run,
        out_shape=out_shape,
        in_specs=[pl.BlockSpec(memory_space=space)] * len(operands) + [pl.BlockSpec(memory_space=pl.ANY)] * len(after),
        out_specs=jax.tree.map(lambda _: pl.BlockSpec(memory_space=pltpu.VMEM), out_shape),
        scratch_shapes=list(scratch),
        cost_estimate=pl.CostEstimate(flops=0, bytes_accessed=0, transcendentals=0),
        compiler_params=pltpu.CompilerParams(vmem_limit_bytes=min(56 << 20, (8 << 20) + 3 * moved)),
    )(*operands, *after)


def column(row, first=0, count=None):
    shape = (count or row.shape[1], row.shape[1])
    eye = lax.broadcasted_iota(jnp.int32, shape, 0) + first == lax.broadcasted_iota(jnp.int32, shape, 1)
    return jnp.sum(jnp.where(eye, row, 0.0), axis=1, keepdims=True)


def tags_of(scales, mass):
    shape = (TAIL, scales.shape[1])
    at = lax.broadcasted_iota(jnp.int32, shape, 0)
    high = mass.astype(BF16).astype(F32)
    return jnp.where(at < 8, scales, jnp.where(at < 12, high, mass - high)).astype(BF16)


def read_tags(tags):
    tags = tags.astype(F32)
    return tags[0:1, :], tags[8:9, 0:1] + tags[12:13, 0:1]


def cut_kernel(nrow, teach, *outs):
    part = teach.shape[1] // nrow
    z = lax.axis_index("row")
    for k in range(nrow):
        at = pl.multiple_of((z ^ k) * part, part)
        outs[k][...] = teach[:, pl.ds(at, part)]


def tag_kernel(piece, scale, *refs):
    cuts, out = refs[:-1], refs[-1]
    rows, part = piece.shape
    out[:rows, :] = piece[...]
    squares = sum(jnp.sum(jnp.square(c[...].astype(F32)), axis=1, keepdims=True) for c in cuts)
    s = scale[...].astype(F32)
    mass = jnp.sum(jnp.square(column(s)) * squares, keepdims=True)
    tags = tags_of(jnp.concatenate([s, s], axis=1), mass)
    out[rows:, :] = jnp.concatenate([tags] * (part // (2 * rows)), axis=1)


def pack_kernel(*refs):
    out, at = refs[-1], 0
    for r in refs[:-1]:
        out[at : at + r.shape[0], :] = r[...]
        at += r.shape[0]


def place(nrow, ncol, rows, k, c):
    return pl.multiple_of(((lax.axis_index("row") ^ k) * ncol + c) * rows, rows)


def assemble(nrow, ncol, rows, blocks, held):
    for c in range(ncol):
        for k, (ref, at) in blocks[c].items():
            held[pl.ds(place(nrow, ncol, rows, k, c), rows), :] = ref[at : at + rows, :]


def split(refs, groups, step):
    refs, blocks = list(refs), []
    for stack in groups:
        found = {}
        for keys in stack:
            ref = refs.pop(0)
            for n, k in enumerate(keys):
                found[k] = (ref, n * step)
        blocks.append(found)
    return blocks, refs


def gram_kernel(nrow, ncol, rows, groups, order, *refs):
    blocks, (kept, given, tags, held, left) = split(refs, groups, rows)
    assemble(nrow, ncol, rows, blocks, held)
    sub, half = rows // 2, nrow * rows // 2
    core = lax.axis_index("sub")
    for n, k in enumerate(order):
        ref, at = blocks[0][k]
        for target, which in ((0, core), (half, 1 - core)):
            rows_at = pl.multiple_of(at + which * sub, sub)
            left[target + n * sub : target + (n + 1) * sub, :] = ref[pl.ds(rows_at, sub), :]
    given[:half, :] = lax.dot_general(left[half:, :], held[...], INNER, preferred_element_type=F32).astype(BF16)
    kept[...] = lax.dot_general(left[:half, :], held[...], INNER, preferred_element_type=F32).astype(kept.dtype)
    lane = lax.broadcasted_iota(jnp.int32, (TAIL, 2 * rows), 1)
    found = [[blocks[c + d][0][0][rows:, : 2 * rows].astype(F32) for d in (0, 1)] for c in range(0, ncol, 2)]
    mass = sum(read_tags(tag)[1] for pair in found for tag in pair)
    tags[...] = tags_of(jnp.zeros((1, tags.shape[1]), F32), mass)
    for c, pair in zip(range(0, ncol, 2), found):
        spot = pl.multiple_of(place(nrow, ncol, rows, 0, c), 2 * rows)
        tags[:, pl.ds(spot, 2 * rows)] = tags_of(jnp.where(lane < rows, *pair)[0:1, :], mass)
    given[half:, :] = tags[...]


def fold_tags(same, tags, came):
    (scales, mass), (more_scales, more_mass) = read_tags(tags[...]), read_tags(came[came.shape[0] - TAIL :, :])
    return tags_of(scales if same else scales + more_scales, mass + more_mass)


def fold_kernel(same, kept, came, tags, keep, give, tags_out):
    rows = kept.shape[0]
    half = rows // 2
    folded = fold_tags(same, tags, came)
    tags_out[...] = folded
    give[:half, :] = (kept[half:, :].astype(F32) + came[half:rows, :].astype(F32)).astype(BF16)
    give[half:, :] = folded
    keep[...] = (kept[:half, :].astype(F32) + came[:half, :].astype(F32)).astype(keep.dtype)


def raw_gram_kernel(nrow, ncol, rows, groups, *refs):
    blocks, (out, raw) = split(refs, groups, rows)
    assemble(nrow, ncol, rows, blocks, raw)
    out[:rows, :] = lax.dot_general(blocks[0][0][0][:rows, :], raw[...], INNER, preferred_element_type=F32)
    batch, half = raw.shape
    step = min(batch, 512)
    for at in range(0, batch, step):
        squares = jnp.square(raw[at : at + step, :].astype(F32))
        out[rows:, at : at + step] = lax.dot_general(
            jnp.ones((8, half), F32), squares, INNER, precision=lax.Precision.HIGHEST, preferred_element_type=F32
        )


def normalize(raw, squares, units):
    for at in range(0, raw.shape[0], 128):
        norm = jnp.sqrt(column(squares[:1, at : at + 128]))
        units[at : at + 128, :] = (raw[at : at + 128, :].astype(F32) / norm).astype(BF16)


def unit_gram_kernel(ncol, mine, other, *refs):
    rows = mine.shape[0] - 8
    gram, norms, squares = refs[-4:-1] if len(refs) > 3 else refs
    squares[...] = mine[rows:, :] + other[rows:, :]
    spot = pl.multiple_of(lax.axis_index("row") * ncol * rows, 2 * rows)
    norm = jnp.sqrt(column(squares[:1, pl.ds(spot, 2 * rows)][:, :rows]))
    norms[...] = jnp.broadcast_to(norm, norms.shape)
    gram[...] = (mine[:rows, :] + other[:rows, :]) / (norm * jnp.sqrt(squares[:1, :]))
    if len(refs) > 3:
        normalize(refs[0], squares, refs[-1])


def error_kernel(batch, kept, came, tags, gram, scale, out):
    sub = kept.shape[0]
    first = lax.axis_index("sub") * sub
    scales, mass = read_tags(fold_tags(False, tags, came))
    total = kept[...].astype(F32) + came[:sub, :].astype(F32)
    outer = column(scale[...].astype(F32), first, sub) * scales
    error = gram[pl.ds(pl.multiple_of(first, sub), sub), :] - outer * total / (mass / batch)
    out[...] = error.astype(BF16)


def final_kernel(nrow, ncol, groups, mine, other, gram, norms, squares, stud, *refs):
    rows = stud.shape[0]
    if groups:
        blocks, (out, error_b, units) = split(refs, groups, rows)
        assemble(nrow, ncol, rows, blocks, units)
        normalize(units, squares, units)
    else:
        units, out, error_b = refs
    sub = rows // 2
    core = lax.axis_index("sub")
    error_b[pl.ds(pl.multiple_of(core * sub, sub), sub), :] = mine[...]
    error_b[pl.ds(pl.multiple_of((1 - core) * sub, sub), sub), :] = other[...]
    norm = norms[:, :1]
    grads = 4.0 * jnp.dot(error_b[...], units[...], preferred_element_type=F32)
    along = 4.0 * jnp.sum(error_b[...].astype(F32) * gram[...], axis=1, keepdims=True)
    unit = stud[...].astype(F32) / norm
    out[...] = (grads - along * unit) / norm


def shards(student, teacher, scale):
    rows, half = student.shape
    nrow, ncol = lax.axis_size("row"), lax.axis_size("col")
    batch = rows * nrow * ncol
    part = teacher.shape[1] // nrow
    small = batch <= 2048
    sds = jax.ShapeDtypeStruct
    scale = scale.reshape(1, rows)

    def along_row(x, k):
        return lax.ppermute(x, "row", [(i, i ^ k) for i in range(nrow)])

    def along_col(x, c):
        return lax.ppermute(x, "col", [(i, (i - c) % ncol) for i in range(ncol)])

    def other_core(x):
        return lax.ppermute(x, "sub", [(0, 1), (1, 0)])

    def pack(xs, after=()):
        if len(xs) == 1:
            return xs[0]
        return call(pack_kernel, sds((sum(x.shape[0] for x in xs), xs[0].shape[1]), BF16), xs, after=after)

    def columns(x):
        return [along_col(x, c) for c in range(1, ncol)]

    stack, keys, k = student, [0], nrow // 2
    while k > 1:
        stack = pack([stack, along_row(stack, k)])
        keys, k = keys + [n ^ k for n in keys], k // 2
    raw = [stack, along_row(stack, 1)]
    raw_groups = [[keys, [n ^ 1 for n in keys]]] * ncol
    raw_passed = [columns(r) for r in raw]
    raw_refs = raw + [p[c] for c in range(ncol - 1) for p in raw_passed]

    cuts = call(functools.partial(cut_kernel, nrow), [sds((rows, part), BF16)] * nrow, [teacher])
    tagged = call(tag_kernel, sds((rows + TAIL, part), BF16), [cuts[0], scale] + list(cuts))
    pieces = [along_row(cuts[k], k) for k in range(1, nrow)]
    tagged_passed = columns(tagged)
    late = pack(pieces, after=tagged_passed[:1] + [stack])
    late_passed = columns(late)
    teach_groups = [[[0], list(range(1, nrow))]] * ncol
    teach_refs = [tagged, late] + [p[c] for c in range(ncol - 1) for p in (tagged_passed, late_passed)]

    order = [0]
    while len(order) < nrow:
        order = [2 * n for n in order] + [2 * n + 1 for n in order]
    kept, given, tags = call(
        functools.partial(gram_kernel, nrow, ncol, rows, teach_groups, order),
        [sds((nrow * rows // 2, batch), F32 if small else BF16), sds((nrow * rows // 2 + TAIL, batch), BF16), sds((TAIL, batch), BF16)],
        teach_refs,
        scratch=[pltpu.VMEM((batch, part), BF16), pltpu.VMEM((nrow * rows, part), BF16)],
    )
    came, k = other_core(given), 1
    while k < nrow:
        count = kept.shape[0] // 2
        kept, give, tags = call(
            functools.partial(fold_kernel, k == 1),
            [sds((count, batch), kept.dtype), sds((count + TAIL, batch), BF16), sds((TAIL, batch), BF16)],
            [kept, came, tags],
        )
        came = along_row(give, k)
        folded = tags if k == 1 else folded
        k *= 2

    message, *all_raw = call(
        functools.partial(raw_gram_kernel, nrow, ncol, rows, raw_groups),
        [sds((rows + 8, batch), F32)] + ([sds((batch, half), BF16)] if small else []),
        raw_refs,
        after=[folded],
        scratch=[] if small else [pltpu.VMEM((batch, half), BF16)],
    )
    gram, norms, squares, *all_units = call(
        functools.partial(unit_gram_kernel, ncol),
        [sds((rows, batch), F32), sds((rows, 128), F32), sds((8, batch), F32)] + ([sds((batch, half), BF16)] if small else []),
        [message, other_core(message)] + all_raw,
    )
    error_b = call(
        functools.partial(error_kernel, batch),
        sds((rows // 2, batch), BF16),
        [kept, came, tags, gram, scale],
    )
    return call(
        functools.partial(final_kernel, nrow, ncol, None if small else raw_groups),
        sds((rows, half), F32),
        [error_b, other_core(error_b), gram, norms, squares, student] + (all_units if small else raw_refs),
        scratch=[pltpu.VMEM((rows, batch), BF16)] + ([] if small else [pltpu.VMEM((batch, half), BF16)]),
    )


def solution(mesh):
    spec = P(("groups", "row", "col"), "sub")
    return jax.shard_map(
        shards,
        mesh=mesh,
        in_specs=(spec, spec, P(("groups", "row", "col"))),
        out_specs=spec,
        check_vma=False,
    )
```

```python
import functools

import jax
import jax.numpy as jnp
from jax import lax
from jax.experimental import pallas as pl
from jax.experimental.pallas import tpu as pltpu
from jax.sharding import PartitionSpec as P

F32, BF16 = jnp.float32, jnp.bfloat16
INNER = (((1,), (1,)), ((), ()))
TAIL = 16


def call(body, out_shape, operands, space=pltpu.VMEM, scratch=(), after=()):
    outs = out_shape if isinstance(out_shape, (list, tuple)) else [out_shape]
    moved = sum(x.size * x.dtype.itemsize for x in list(operands) + list(outs))

    def run(*refs):
        body(*refs[: len(operands)], *refs[len(operands) + len(after) :])

    return pl.pallas_call(
        run,
        out_shape=out_shape,
        in_specs=[pl.BlockSpec(memory_space=space)] * len(operands) + [pl.BlockSpec(memory_space=pl.ANY)] * len(after),
        out_specs=jax.tree.map(lambda _: pl.BlockSpec(memory_space=pltpu.VMEM), out_shape),
        scratch_shapes=list(scratch),
        cost_estimate=pl.CostEstimate(flops=0, bytes_accessed=0, transcendentals=0),
        compiler_params=pltpu.CompilerParams(vmem_limit_bytes=min(56 << 20, (8 << 20) + 3 * moved)),
    )(*operands, *after)


def column(row, first=0, count=None):
    shape = (count or row.shape[1], row.shape[1])
    eye = lax.broadcasted_iota(jnp.int32, shape, 0) + first == lax.broadcasted_iota(jnp.int32, shape, 1)
    return jnp.sum(jnp.where(eye, row, 0.0), axis=1, keepdims=True)


def tags_of(scales, mass):
    shape = (TAIL, scales.shape[1])
    at = lax.broadcasted_iota(jnp.int32, shape, 0)
    high = mass.astype(BF16).astype(F32)
    return jnp.where(at < 8, scales, jnp.where(at < 12, high, mass - high)).astype(BF16)


def read_tags(tags):
    tags = tags.astype(F32)
    return tags[0:1, :], tags[8:9, 0:1] + tags[12:13, 0:1]


def cut_kernel(nrow, teach, *outs):
    part = teach.shape[1] // nrow
    z = lax.axis_index("row")
    for k in range(nrow):
        at = pl.multiple_of((z ^ k) * part, part)
        outs[k][...] = teach[:, pl.ds(at, part)]


def join_kernel(stud, scale, *refs):
    cuts, outs = refs[:-2], refs[-2:]
    rows, half = stud.shape
    squares = sum(jnp.sum(jnp.square(c[...].astype(F32)), axis=1, keepdims=True) for c in cuts)
    s = scale[...].astype(F32)
    mass = jnp.sum(jnp.square(column(s)) * squares, keepdims=True)
    tags = tags_of(jnp.concatenate([s, s], axis=1), mass)
    tags = jnp.concatenate([tags] * (half // (2 * rows)), axis=1)
    for out, cut in zip(outs, (cuts[0], cuts[len(cuts) // 2])):
        out[:rows, :] = stud[...]
        out[rows : rows + TAIL, :] = tags
        part = cut.shape[1]
        high = rows * part // half
        for n in range(half // part):
            out[rows + TAIL :, n * part : (n + 1) * part] = cut[n * high : (n + 1) * high, :]


def put(held, spot, rows, ref, at):
    width = held.shape[1]
    high = rows * width // ref.shape[1]
    for n in range(ref.shape[1] // width):
        held[pl.ds(spot + n * high, high), :] = ref[at : at + high, n * width : (n + 1) * width]


def late_kernel(rows, *refs):
    out = refs[-1]
    for k, ref in enumerate(refs[:-1]):
        put(out, k * rows, rows, ref, ref.shape[0] - rows * out.shape[1] // ref.shape[1])


def pack_kernel(spans, *refs):
    out, at = refs[-1], 0
    for r, (first, last) in zip(refs[:-1], spans):
        out[at : at + last - first, :] = r[first:last, :]
        at += last - first


def place(nrow, ncol, rows, k, c):
    return pl.multiple_of(((lax.axis_index("row") ^ k) * ncol + c) * rows, rows)


def gram_kernel(nrow, ncol, rows, *refs):
    outs, held = refs[2 * ncol : -1], refs[-1]
    for c in range(ncol):
        own, late = refs[2 * c : 2 * c + 2]
        put(held, place(nrow, ncol, rows, 0, c), rows, own, rows + TAIL)
        for k in range(1, nrow):
            put(held, place(nrow, ncol, rows, k, c), rows, late, (k - 1) * rows)
    for k in range(nrow):
        left = held[pl.ds(place(nrow, ncol, rows, k, 0), rows), :]
        outs[k][...] = lax.dot_general(left, held[...], INNER, preferred_element_type=F32).astype(outs[k].dtype)


def raw_blocks(ncol, step, keys, refs):
    blocks = []
    for c in range(ncol):
        own, rest = refs[2 * c : 2 * c + 2]
        blocks.append({0: (own, 0)} | {k: (rest, n * step) for n, k in enumerate(keys)})
    return blocks, refs[2 * ncol :]


def assemble(nrow, ncol, rows, blocks, held):
    for c in range(ncol):
        for k, (ref, at) in blocks[c].items():
            held[pl.ds(place(nrow, ncol, rows, k, c), rows), :] = ref[at : at + rows, :]


def raw_gram_kernel(nrow, ncol, rows, keys, *refs):
    step = rows + TAIL
    blocks, (out, vectors, raw) = raw_blocks(ncol, step, keys, refs)
    assemble(nrow, ncol, rows, blocks, raw)
    out[:rows, :] = lax.dot_general(blocks[0][0][0][:rows, :], raw[...], INNER, preferred_element_type=F32)
    batch, half = raw.shape
    chunk = min(batch, 512)
    for at in range(0, batch, chunk):
        squares = jnp.square(raw[at : at + chunk, :].astype(F32))
        out[rows:, at : at + chunk] = lax.dot_general(
            jnp.ones((8, half), F32), squares, INNER, precision=lax.Precision.HIGHEST, preferred_element_type=F32
        )
    lane = lax.broadcasted_iota(jnp.int32, (1, 2 * rows), 1)
    mass = jnp.zeros((1, 1), F32)
    for k in range(nrow):
        for c in range(0, ncol, 2):
            pair = []
            for d in (c, c + 1):
                ref, at = blocks[d][k]
                scales, part = read_tags(ref[at + rows : at + step, : 2 * rows])
                pair.append(scales)
                mass = mass + part
            spot = pl.multiple_of(place(nrow, ncol, rows, k, c), 2 * rows)
            vectors[0:8, pl.ds(spot, 2 * rows)] = jnp.broadcast_to(jnp.where(lane < rows, *pair), (8, 2 * rows))
    vectors[8:, :] = jnp.broadcast_to(mass, (8, batch))


def message_kernel(raw_gram, vectors, *refs):
    parts, out = refs[:-1], refs[-1]
    total = parts[0][...].astype(F32)
    for r in parts[1:]:
        total = total + r[...].astype(F32)
    rows = total.shape[0]
    out[:rows, :] = total
    out[rows : 2 * rows + 8, :] = raw_gram[...]
    out[2 * rows + 8 :, :] = vectors[8:, :]


def final_kernel(nrow, ncol, keys, mine, other, vectors, stud, scale, *refs):
    rows = stud.shape[0]
    if keys:
        blocks, (out, raw, units) = raw_blocks(ncol, rows + TAIL, keys, refs)
        assemble(nrow, ncol, rows, blocks, raw)
    else:
        raw, out, units = refs
    batch = mine.shape[1]
    squares = mine[2 * rows : 2 * rows + 8, :] + other[2 * rows : 2 * rows + 8, :]
    for at in range(0, batch, 128):
        norm = jnp.sqrt(column(squares[:1, at : at + 128]))
        units[at : at + 128, :] = (raw[at : at + 128, :].astype(F32) / norm).astype(BF16)
    own = squares_of_own(mine, other, ncol, rows)
    norm = jnp.sqrt(column(own))
    mass = (mine[2 * rows + 8 : 2 * rows + 9, :1] + other[2 * rows + 8 : 2 * rows + 9, :1]) / batch
    gram = (mine[rows : 2 * rows, :] + other[rows : 2 * rows, :]) / (norm * jnp.sqrt(squares[:1, :]))
    outer = column(scale[...].astype(F32)) * vectors[:1, :]
    error_b = (gram - outer * (mine[:rows, :] + other[:rows, :]) / mass).astype(BF16)
    grads = 4.0 * jnp.dot(error_b, units[...], preferred_element_type=F32)
    along = 4.0 * jnp.sum(error_b.astype(F32) * gram, axis=1, keepdims=True)
    unit = stud[...].astype(F32) / norm
    out[...] = (grads - along * unit) / norm


def squares_of_own(mine, other, ncol, rows):
    at = pl.ds(pl.multiple_of(lax.axis_index("row") * ncol * rows, 2 * rows), 2 * rows)
    return (mine[2 * rows : 2 * rows + 8, at] + other[2 * rows : 2 * rows + 8, at])[:1, :rows]


def shards(student, teacher, scale):
    rows, half = student.shape
    nrow, ncol = lax.axis_size("row"), lax.axis_size("col")
    batch = rows * nrow * ncol
    part = teacher.shape[1] // nrow
    small = batch <= 2048
    sds = jax.ShapeDtypeStruct
    scale = scale.reshape(1, rows)

    def along_row(x, k):
        return lax.ppermute(x, "row", [(i, i ^ k) for i in range(nrow)])

    def along_col(x, c):
        return lax.ppermute(x, "col", [(i, (i - c) % ncol) for i in range(ncol)])

    def other_core(x):
        return lax.ppermute(x, "sub", [(0, 1), (1, 0)])

    def pack(xs, spans, after=()):
        shape = (sum(last - first for first, last in spans), half)
        return call(functools.partial(pack_kernel, spans), sds(shape, BF16), xs, after=after)

    def with_columns(*xs):
        return [x if c == 0 else along_col(x, c) for c in range(ncol) for x in xs]

    step, middle = rows + TAIL, nrow // 2
    joined = sds((step + rows * part // half, half), BF16)
    cuts = call(functools.partial(cut_kernel, nrow), [sds((rows, part), BF16)] * nrow, [teacher])
    own, far = call(join_kernel, [joined, joined], [student, scale] + list(cuts))
    pieces = [along_row(far if k == middle else cuts[k], k) for k in range(1, nrow)]
    far = pieces[middle - 1]
    own = with_columns(own)
    late = call(functools.partial(late_kernel, rows), sds(((nrow - 1) * rows, part), BF16), pieces, after=own[1:2])
    late = with_columns(late)
    partial = call(
        functools.partial(gram_kernel, nrow, ncol, rows),
        [sds((rows, batch), F32)] + [sds((rows, batch), BF16)] * (nrow - 1),
        [r for pair in zip(own, late) for r in pair],
        scratch=[pltpu.VMEM((batch, part), BF16)],
    )
    returned = [partial[0]] + [along_row(partial[k], k) for k in range(1, nrow)]

    keys, received, spans = [0, middle], [far], [(0, step)]
    stack, k = pack([own[0], far], [(0, step)] * 2, after=late[:1]), middle // 2
    while k:
        received.append(along_row(stack, k))
        spans.append((0, stack.shape[0]))
        keys = keys + [n ^ k for n in keys]
        if k > 1:
            stack = pack([stack, received[-1]], [(0, stack.shape[0])] * 2)
        k //= 2
    keys = keys[1:]
    rest = with_columns(pack(received, spans))
    raw_refs = [r for pair in zip(own, rest) for r in pair]
    raw_gram, vectors, *all_raw = call(
        functools.partial(raw_gram_kernel, nrow, ncol, rows, keys),
        [sds((rows + 8, batch), F32), sds((16, batch), F32)] + ([sds((batch, half), BF16)] if small else []),
        raw_refs,
        scratch=[] if small else [pltpu.VMEM((batch, half), BF16)],
    )
    message = call(message_kernel, sds((2 * rows + 16, batch), F32), [raw_gram, vectors] + returned)
    return call(
        functools.partial(final_kernel, nrow, ncol, None if small else keys),
        sds((rows, half), F32),
        [message, other_core(message), vectors, student, scale] + (all_raw if small else raw_refs),
        scratch=([] if small else [pltpu.VMEM((batch, half), BF16)]) + [pltpu.VMEM((batch, half), BF16)],
    )


def solution(mesh):
    spec = P(("groups", "row", "col"), "sub")
    return jax.shard_map(
        shards,
        mesh=mesh,
        in_specs=(spec, spec, P(("groups", "row", "col"))),
        out_specs=spec,
        check_vma=False,
    )
```

```python
import functools

import jax
import jax.numpy as jnp
from jax import lax
from jax.experimental import pallas as pl
from jax.experimental.pallas import tpu as pltpu
from jax.sharding import PartitionSpec as P

F32, BF16 = jnp.float32, jnp.bfloat16
INNER = (((1,), (1,)), ((), ()))
TAIL = 16


def call(body, out_shape, operands, space=pltpu.VMEM, scratch=(), after=()):
    outs = out_shape if isinstance(out_shape, (list, tuple)) else [out_shape]
    moved = sum(x.size * x.dtype.itemsize for x in list(operands) + list(outs))

    def run(*refs):
        body(*refs[: len(operands)], *refs[len(operands) + len(after) :])

    return pl.pallas_call(
        run,
        out_shape=out_shape,
        in_specs=[pl.BlockSpec(memory_space=space)] * len(operands) + [pl.BlockSpec(memory_space=pl.ANY)] * len(after),
        out_specs=jax.tree.map(lambda _: pl.BlockSpec(memory_space=pltpu.VMEM), out_shape),
        scratch_shapes=list(scratch),
        cost_estimate=pl.CostEstimate(flops=0, bytes_accessed=0, transcendentals=0),
        compiler_params=pltpu.CompilerParams(vmem_limit_bytes=min(56 << 20, (8 << 20) + 3 * moved)),
    )(*operands, *after)


def column(row):
    shape = (row.shape[1], row.shape[1])
    eye = lax.broadcasted_iota(jnp.int32, shape, 0) == lax.broadcasted_iota(jnp.int32, shape, 1)
    return jnp.sum(jnp.where(eye, row, 0.0), axis=1, keepdims=True)


def tags_of(scales, mass):
    shape = (TAIL, scales.shape[1])
    at = lax.broadcasted_iota(jnp.int32, shape, 0)
    high = mass.astype(BF16).astype(F32)
    return jnp.where(at < 8, scales, jnp.where(at < 12, high, mass - high)).astype(BF16)


def read_tags(tags):
    tags = tags.astype(F32)
    return tags[0:1, :], tags[8:9, 0:1] + tags[12:13, 0:1]


def lane_row(col):
    shape = (col.shape[0], col.shape[0])
    eye = lax.broadcasted_iota(jnp.int32, shape, 0) == lax.broadcasted_iota(jnp.int32, shape, 1)
    return jnp.sum(jnp.where(eye, col, 0.0), axis=0, keepdims=True)


def wide(out, at, piece):
    rows, part = piece.shape
    width = out.shape[1]
    high = rows * part // width
    for n in range(width // part):
        out[at : at + high, n * part : (n + 1) * part] = piece[n * high : (n + 1) * high, :]


def put(held, spot, rows, ref, at):
    width = held.shape[1]
    high = rows * width // ref.shape[1]
    for n in range(ref.shape[1] // width):
        held[pl.ds(spot + n * high, high), :] = ref[at : at + high, n * width : (n + 1) * width]


def cut_kernel(nrow, teach, *outs):
    part = teach.shape[1] // nrow
    z = lax.axis_index("row")
    for k in range(nrow):
        at = pl.multiple_of((z ^ k) * part, part)
        outs[k][...] = teach[:, pl.ds(at, part)]


def ride_kernel(stud, *refs):
    rows, count = stud.shape[0], len(refs) // 2
    for piece, out in zip(refs[:count], refs[count:]):
        out[:rows, :] = stud[...]
        wide(out, rows, piece)


def own_kernel(teach, stud, scale, cut, out):
    rows, half = stud.shape
    ts = teach[...].astype(F32)
    s = scale[...].astype(F32)
    mass = jnp.sum(jnp.square(column(s)) * jnp.sum(ts * ts, axis=1, keepdims=True), keepdims=True)
    tags = tags_of(jnp.concatenate([s, s], axis=1), mass)
    out[:rows, :] = stud[...]
    out[rows : rows + TAIL, :] = jnp.concatenate([tags] * (half // (2 * rows)), axis=1)
    wide(out, rows + TAIL, cut[...])


def take_kernel(rows, ref, out):
    put(out, 0, rows, ref, rows)


def pack_kernel(spans, *refs):
    out, at = refs[-1], 0
    for r, (first, last) in zip(refs[:-1], spans):
        out[at : at + last - first, :] = r[first:last, :]
        at += last - first


def place(nrow, ncol, rows, k, c):
    return pl.multiple_of(((lax.axis_index("row") ^ k) * ncol + c) * rows, rows)


def group_spot(nrow, ncol, rows, k):
    return pl.multiple_of((lax.axis_index("row") ^ k) * ncol * rows, 2 * rows)


def gram_kernel(nrow, ncol, rows, order, *refs):
    count = nrow * ncol
    outs, held, left = refs[count : count + nrow], refs[-2], refs[-1]
    for c in range(ncol):
        own = refs[c * nrow]
        put(held, place(nrow, ncol, rows, 0, c), rows, own, rows + TAIL)
        for k in range(1, nrow):
            put(held, place(nrow, ncol, rows, k, c), rows, refs[c * nrow + k], 0)
    for n, k in enumerate(order):
        left[n * rows : (n + 1) * rows, :] = held[pl.ds(place(nrow, ncol, rows, k, 0), rows), :]
    sub = rows // 2
    at = lax.broadcasted_iota(jnp.int32, (sub, 2 * rows), 0)
    lane = lax.broadcasted_iota(jnp.int32, (sub, 2 * rows), 1)
    note, mass = jnp.zeros((sub, 2 * rows), F32), jnp.zeros((1, 1), F32)
    for c in range(ncol):
        scales, part = read_tags(refs[c * nrow][rows : rows + TAIL, : 2 * rows])
        turned = jnp.concatenate([scales[:, sub:], scales[:, :sub]], axis=1)
        note = jnp.where(at == 2 * c, scales, jnp.where(at == 2 * c + 1, turned, note))
        mass = mass + part
    high = mass.astype(BF16).astype(F32)
    note = jnp.where(at < sub // 2, note, jnp.where(at < sub * 3 // 4, high, mass - high))
    per = max(1, 2048 * rows * nrow // held.shape[0] // rows // 8)
    for first in range(0, nrow, per):
        last = min(first + per, nrow)
        gram = lax.dot_general(left[first * rows : last * rows, :], held[...], INNER, preferred_element_type=F32)
        for n in range(first, last):
            out = outs[order[n]]
            out[...] = gram[(n - first) * rows : (n - first + 1) * rows, :].astype(out.dtype)
            spot = pl.ds(group_spot(nrow, ncol, rows, order[n]), 2 * rows)
            seen = out[sub:, spot].astype(F32)
            out[sub:, spot] = jnp.where(lane < sub, note, seen).astype(out.dtype)


def assemble(nrow, ncol, rows, keys, refs, held):
    each = len(keys)
    for c in range(ncol):
        for stack, ref in zip(keys, refs[c * each : (c + 1) * each]):
            for n, k in enumerate(stack):
                held[pl.ds(place(nrow, ncol, rows, k, c), rows), :] = ref[n * rows : (n + 1) * rows, :]


def raw_gram_kernel(nrow, ncol, rows, keys, *refs):
    count = len(keys) * ncol
    out, raw = refs[count:]
    assemble(nrow, ncol, rows, keys, refs, raw)
    out[:rows, :] = lax.dot_general(refs[0][:rows, :], raw[...], INNER, preferred_element_type=F32)
    for at in range(0, raw.shape[0], 128):
        squares = jnp.sum(jnp.square(raw[at : at + 128, :].astype(F32)), axis=1, keepdims=True)
        out[rows:, at : at + 128] = jnp.broadcast_to(lane_row(squares), (8, 128))


def message_kernel(nrow, ncol, raw_gram, *refs):
    parts, (out, vectors) = refs[:-2], refs[-2:]
    rows = parts[0].shape[0]
    sub = rows // 2
    total = parts[0][...].astype(F32)
    for r in parts[1:]:
        total = total + r[...].astype(F32)
    out[:rows, :] = total
    own = pl.ds(group_spot(nrow, ncol, rows, 0), 2 * rows)
    mirror = jnp.transpose(out[:sub, own])[sub : 2 * sub, :]
    out[sub:rows, own] = jnp.concatenate([mirror, out[sub:rows, own][:, sub:]], axis=1)
    mass = jnp.zeros((1, 1), F32)
    for k, part in enumerate(parts):
        note = part[sub:, own].astype(F32)[:, :sub]
        mass = mass + note[sub // 2 : sub // 2 + 1, :1] + note[sub * 3 // 4 : sub * 3 // 4 + 1, :1]
        line = jnp.concatenate([note[n : n + 1, :] for n in range(2 * ncol)], axis=1)
        vectors[:, pl.ds(group_spot(nrow, ncol, rows, k), ncol * rows)] = jnp.broadcast_to(line, (8, ncol * rows))
    out[rows : 2 * rows + 8, :] = raw_gram[...]
    out[2 * rows + 8 :, :] = jnp.broadcast_to(mass, (8, out.shape[1]))


def final_kernel(nrow, ncol, keys, mine, other, vectors, stud, scale, *refs):
    rows = stud.shape[0]
    if keys:
        out, raw, units = refs[-3:]
        assemble(nrow, ncol, rows, keys, refs, raw)
    else:
        raw, out, units = refs
    batch = mine.shape[1]
    squares = mine[2 * rows : 2 * rows + 8, :] + other[2 * rows : 2 * rows + 8, :]
    for at in range(0, batch, 128):
        norm = jnp.sqrt(column(squares[:1, at : at + 128]))
        units[at : at + 128, :] = (raw[at : at + 128, :].astype(F32) / norm).astype(BF16)
    at = pl.ds(group_spot(nrow, ncol, rows, 0), 2 * rows)
    own = (mine[2 * rows : 2 * rows + 8, at] + other[2 * rows : 2 * rows + 8, at])[:1, :rows]
    norm = jnp.sqrt(column(own))
    mass = (mine[2 * rows + 8 : 2 * rows + 9, :1] + other[2 * rows + 8 : 2 * rows + 9, :1]) / batch
    gram = (mine[rows : 2 * rows, :] + other[rows : 2 * rows, :]) / (norm * jnp.sqrt(squares[:1, :]))
    outer = column(scale[...].astype(F32)) * vectors[:1, :]
    error_b = (gram - outer * (mine[:rows, :] + other[:rows, :]) / mass).astype(BF16)
    grads = 4.0 * jnp.dot(error_b, units[...], preferred_element_type=F32)
    along = 4.0 * jnp.sum(error_b.astype(F32) * gram, axis=1, keepdims=True)
    unit = stud[...].astype(F32) / norm
    out[...] = (grads - along * unit) / norm


def shards(student, teacher, scale):
    rows, half = student.shape
    nrow, ncol = lax.axis_size("row"), lax.axis_size("col")
    batch = rows * nrow * ncol
    part = teacher.shape[1] // nrow
    small = batch <= 2048
    sds = jax.ShapeDtypeStruct
    scale = scale.reshape(1, rows)

    def along_row(x, k):
        return lax.ppermute(x, "row", [(i, i ^ k) for i in range(nrow)])

    def along_col(x, c):
        return lax.ppermute(x, "col", [(i, (i - c) % ncol) for i in range(ncol)])

    def other_core(x):
        return lax.ppermute(x, "sub", [(0, 1), (1, 0)])

    def pack(xs, spans, after=()):
        shape = (sum(last - first for first, last in spans), half)
        return call(functools.partial(pack_kernel, spans), sds(shape, BF16), xs, after=after)

    def with_columns(x):
        return [x if c == 0 else along_col(x, c) for c in range(ncol)]

    middle, high = nrow // 2, rows * part // half
    order = list(range(middle, nrow)) + list(range(middle))
    riders = (1, middle)
    cuts = call(functools.partial(cut_kernel, nrow), [sds((rows, part), BF16)] * nrow, [teacher])
    ridden = call(ride_kernel, [sds((rows + high, half), BF16)] * 2, [student] + [cuts[k] for k in riders])
    leaving = dict(enumerate(cuts)) | dict(zip(riders, ridden))
    came = {k: along_row(leaving[k], k) for k in order if k}
    own = call(own_kernel, sds((rows + TAIL + high, half), BF16), [teacher, student, scale, cuts[0]])
    columns = {0: with_columns(own)}
    for k in range(1, nrow):
        piece = came[k]
        if k in riders:
            piece = call(functools.partial(take_kernel, rows), sds((rows, part), BF16), [piece])
        columns[k] = with_columns(piece)
    partial = call(
        functools.partial(gram_kernel, nrow, ncol, rows, order),
        [sds((rows, batch), BF16 if k else F32) for k in range(nrow)],
        [columns[k][c] for c in range(ncol) for k in range(nrow)],
        scratch=[pltpu.VMEM((batch, part), BF16), pltpu.VMEM((nrow * rows, part), BF16)],
    )
    returned = {k: along_row(partial[k], k) if k else partial[0] for k in order}

    near, far = came[1], came[middle]
    stack, keys, k, spans, got, got_keys = [student, far], [0, middle], middle // 2, [(0, rows)] * 2, [], []
    while k:
        first = 1 if k == 1 else 0
        sent = pack(stack[first:], spans[first:])
        got.append(along_row(sent, k))
        got_keys += [n ^ k for n in keys[first:]]
        stack, spans, keys = stack + got[-1:], spans + [(0, len(keys) * rows)], keys + [n ^ k for n in keys]
        k //= 2
    rest = pack([near, far] + got, [(0, rows)] * 2 + [(0, g.shape[0]) for g in got], after=[partial[0]])
    raw_keys = [[0], [1, middle] + got_keys]
    sources = [columns[0], with_columns(rest)]
    raw_refs = [x[c] for c in range(ncol) for x in sources]
    raw_gram, *all_raw = call(
        functools.partial(raw_gram_kernel, nrow, ncol, rows, raw_keys),
        [sds((rows + 8, batch), F32)] + ([sds((batch, half), BF16)] if small else []),
        raw_refs,
        scratch=[] if small else [pltpu.VMEM((batch, half), BF16)],
    )
    message, vectors = call(
        functools.partial(message_kernel, nrow, ncol),
        [sds((2 * rows + 16, batch), F32), sds((8, batch), F32)],
        [raw_gram] + [returned[k] for k in range(nrow)],
    )
    return call(
        functools.partial(final_kernel, nrow, ncol, None if small else raw_keys),
        sds((rows, half), F32),
        [message, other_core(message), vectors, student, scale] + (all_raw if small else raw_refs),
        scratch=([] if small else [pltpu.VMEM((batch, half), BF16)]) + [pltpu.VMEM((batch, half), BF16)],
    )


def solution(mesh):
    spec = P(("groups", "row", "col"), "sub")
    return jax.shard_map(
        shards,
        mesh=mesh,
        in_specs=(spec, spec, P(("groups", "row", "col"))),
        out_specs=spec,
        check_vma=False,
    )
```

```python
import functools

import jax
import jax.numpy as jnp
from jax import lax
from jax.experimental import pallas as pl
from jax.experimental.pallas import tpu as pltpu
from jax.sharding import PartitionSpec as P

F32, BF16 = jnp.float32, jnp.bfloat16
INNER = (((1,), (1,)), ((), ()))
TAIL = 16


def call(body, out_shape, operands, space=pltpu.VMEM, scratch=(), after=(), limit=None):
    outs = out_shape if isinstance(out_shape, (list, tuple)) else [out_shape]
    moved = sum(x.size * x.dtype.itemsize for x in list(operands) + list(outs))

    def run(*refs):
        body(*refs[: len(operands)], *refs[len(operands) + len(after) :])

    return pl.pallas_call(
        run,
        out_shape=out_shape,
        in_specs=[pl.BlockSpec(memory_space=space)] * len(operands) + [pl.BlockSpec(memory_space=pl.ANY)] * len(after),
        out_specs=jax.tree.map(lambda _: pl.BlockSpec(memory_space=space), out_shape),
        scratch_shapes=list(scratch),
        cost_estimate=pl.CostEstimate(flops=0, bytes_accessed=0, transcendentals=0),
        compiler_params=pltpu.CompilerParams(vmem_limit_bytes=limit or min(56 << 20, (8 << 20) + 3 * moved)),
    )(*operands, *after)


def column(row):
    shape = (row.shape[1], row.shape[1])
    eye = lax.broadcasted_iota(jnp.int32, shape, 0) == lax.broadcasted_iota(jnp.int32, shape, 1)
    return jnp.sum(jnp.where(eye, row, 0.0), axis=1, keepdims=True)


def tags_of(scales, mass):
    shape = (TAIL, scales.shape[1])
    at = lax.broadcasted_iota(jnp.int32, shape, 0)
    high = mass.astype(BF16).astype(F32)
    return jnp.where(at < 8, scales, jnp.where(at < 12, high, mass - high)).astype(BF16)


def read_tags(tags):
    tags = tags.astype(F32)
    return tags[0:1, :], tags[8:9, 0:1] + tags[12:13, 0:1]


def lane_row(col):
    shape = (col.shape[0], col.shape[0])
    eye = lax.broadcasted_iota(jnp.int32, shape, 0) == lax.broadcasted_iota(jnp.int32, shape, 1)
    return jnp.sum(jnp.where(eye, col, 0.0), axis=0, keepdims=True)


def wide(out, at, piece):
    rows, part = piece.shape
    width = out.shape[1]
    high = rows * part // width
    for n in range(width // part):
        out[at : at + high, n * part : (n + 1) * part] = piece[n * high : (n + 1) * high, :]


def put(held, spot, rows, ref, at):
    width = held.shape[1]
    high = rows * width // ref.shape[1]
    for n in range(ref.shape[1] // width):
        held[pl.ds(spot + n * high, high), :] = ref[at : at + high, n * width : (n + 1) * width]


def cut_kernel(nrow, riders, teach, stud, *refs):
    outs, sems = (None, *refs[: nrow - 1]), refs[nrow - 1]
    rows, half = stud.shape
    part = teach.shape[1] // nrow
    high = rows * part // half
    z = lax.axis_index("row")
    copies = []
    for k in range(1, nrow):
        at = pl.multiple_of((z ^ k) * part, part)
        if k in riders:
            copies.append((stud, outs[k].at[pl.ds(0, rows), :]))
            for n in range(half // part):
                target = outs[k].at[pl.ds(rows, high), pl.ds(n * part, part)]
                copies.append((teach.at[pl.ds(n * high, high), pl.ds(at, part)], target))
        else:
            copies.append((teach.at[:, pl.ds(at, part)], outs[k]))
    copies = [pltpu.make_async_copy(a, b, sems.at[n]) for n, (a, b) in enumerate(copies)]
    for c in copies:
        c.start()
    for c in copies:
        c.wait()


def own_kernel(nrow, teach, stud, scale, out):
    rows, half = stud.shape
    part = teach.shape[1] // nrow
    ts = teach[...].astype(F32)
    s = scale[...].astype(F32)
    mass = jnp.sum(jnp.square(column(s)) * jnp.sum(ts * ts, axis=1, keepdims=True), keepdims=True)
    tags = tags_of(jnp.concatenate([s, s], axis=1), mass)
    out[:rows, :] = stud[...]
    out[rows : rows + TAIL, :] = jnp.concatenate([tags] * (half // (2 * rows)), axis=1)
    wide(out, rows + TAIL, teach[:, pl.ds(pl.multiple_of(lax.axis_index("row") * part, part), part)])


def take_kernel(rows, ref, out):
    put(out, 0, rows, ref, rows)


def pack_kernel(spans, *refs):
    out, at = refs[-1], 0
    for r, (first, last) in zip(refs[:-1], spans):
        out[at : at + last - first, :] = r[first:last, :]
        at += last - first


def place(nrow, ncol, rows, k, c):
    return pl.multiple_of(((lax.axis_index("row") ^ k) * ncol + c) * rows, rows)


def group_spot(nrow, ncol, rows, k):
    return pl.multiple_of((lax.axis_index("row") ^ k) * ncol * rows, 2 * rows)


def gram_kernel(nrow, ncol, rows, order, *refs):
    count = nrow * ncol
    outs, held, left = refs[count : count + nrow], refs[-2], refs[-1]
    for c in range(ncol):
        own = refs[c * nrow]
        put(held, place(nrow, ncol, rows, 0, c), rows, own, rows + TAIL)
        for k in range(1, nrow):
            put(held, place(nrow, ncol, rows, k, c), rows, refs[c * nrow + k], 0)
    for n, k in enumerate(order):
        left[n * rows : (n + 1) * rows, :] = held[pl.ds(place(nrow, ncol, rows, k, 0), rows), :]
    sub = rows // 2
    at = lax.broadcasted_iota(jnp.int32, (sub, 2 * rows), 0)
    lane = lax.broadcasted_iota(jnp.int32, (sub, 2 * rows), 1)
    note, mass = jnp.zeros((sub, 2 * rows), F32), jnp.zeros((1, 1), F32)
    for c in range(ncol):
        scales, part = read_tags(refs[c * nrow][rows : rows + TAIL, : 2 * rows])
        turned = jnp.concatenate([scales[:, sub:], scales[:, :sub]], axis=1)
        note = jnp.where(at == 2 * c, scales, jnp.where(at == 2 * c + 1, turned, note))
        mass = mass + part
    high = mass.astype(BF16).astype(F32)
    note = jnp.where(at < sub // 2, note, jnp.where(at < sub * 3 // 4, high, mass - high))
    per = max(1, 2048 * rows * nrow // held.shape[0] // rows // 8)
    for first in range(0, nrow, per):
        last = min(first + per, nrow)
        gram = lax.dot_general(left[first * rows : last * rows, :], held[...], INNER, preferred_element_type=F32)
        for n in range(first, last):
            out = outs[order[n]]
            out[...] = gram[(n - first) * rows : (n - first + 1) * rows, :].astype(out.dtype)
            spot = pl.ds(group_spot(nrow, ncol, rows, order[n]), 2 * rows)
            seen = out[sub:, spot].astype(F32)
            out[sub:, spot] = jnp.where(lane < sub, note, seen).astype(out.dtype)


def assemble(nrow, ncol, rows, keys, refs, held):
    each = len(keys)
    for c in range(ncol):
        for stack, ref in zip(keys, refs[c * each : (c + 1) * each]):
            for n, k in enumerate(stack):
                held[pl.ds(place(nrow, ncol, rows, k, c), rows), :] = ref[n * rows : (n + 1) * rows, :]


def raw_gram_kernel(nrow, ncol, rows, keys, *refs):
    count = len(keys) * ncol
    out, raw = refs[count:]
    assemble(nrow, ncol, rows, keys, refs, raw)
    out[:rows, :] = lax.dot_general(refs[0][:rows, :], raw[...], INNER, preferred_element_type=F32)
    for at in range(0, raw.shape[0], 128):
        squares = jnp.sum(jnp.square(raw[at : at + 128, :].astype(F32)), axis=1, keepdims=True)
        out[rows:, at : at + 128] = jnp.broadcast_to(lane_row(squares), (8, 128))


def message_kernel(nrow, ncol, order, raw_gram, *refs):
    parts, (out, vectors) = [refs[order.index(k)] for k in range(nrow)], refs[-2:]
    rows = parts[0].shape[0]
    sub = rows // 2
    total = parts[0][...].astype(F32)
    for r in parts[1:]:
        total = total + r[...].astype(F32)
    out[:rows, :] = total
    own = pl.ds(group_spot(nrow, ncol, rows, 0), 2 * rows)
    mirror = jnp.transpose(out[:sub, own])[sub : 2 * sub, :]
    out[sub:rows, own] = jnp.concatenate([mirror, out[sub:rows, own][:, sub:]], axis=1)
    mass = jnp.zeros((1, 1), F32)
    for k, part in enumerate(parts):
        note = part[sub:, own].astype(F32)[:, :sub]
        mass = mass + note[sub // 2 : sub // 2 + 1, :1] + note[sub * 3 // 4 : sub * 3 // 4 + 1, :1]
        line = jnp.concatenate([note[n : n + 1, :] for n in range(2 * ncol)], axis=1)
        vectors[:, pl.ds(group_spot(nrow, ncol, rows, k), ncol * rows)] = jnp.broadcast_to(line, (8, ncol * rows))
    out[rows : 2 * rows + 8, :] = raw_gram[...]
    out[2 * rows + 8 :, :] = jnp.broadcast_to(mass, (8, out.shape[1]))


def final_kernel(nrow, ncol, keys, mine, other, vectors, stud, scale, *refs):
    rows = stud.shape[0]
    if keys:
        out, raw, units = refs[-3:]
        assemble(nrow, ncol, rows, keys, refs, raw)
    else:
        raw, out, units = refs
    batch = mine.shape[1]
    squares = mine[2 * rows : 2 * rows + 8, :] + other[2 * rows : 2 * rows + 8, :]
    for at in range(0, batch, 128):
        norm = jnp.sqrt(column(squares[:1, at : at + 128]))
        units[at : at + 128, :] = (raw[at : at + 128, :].astype(F32) / norm).astype(BF16)
    at = pl.ds(group_spot(nrow, ncol, rows, 0), 2 * rows)
    own = (mine[2 * rows : 2 * rows + 8, at] + other[2 * rows : 2 * rows + 8, at])[:1, :rows]
    norm = jnp.sqrt(column(own))
    mass = (mine[2 * rows + 8 : 2 * rows + 9, :1] + other[2 * rows + 8 : 2 * rows + 9, :1]) / batch
    gram = (mine[rows : 2 * rows, :] + other[rows : 2 * rows, :]) / (norm * jnp.sqrt(squares[:1, :]))
    outer = column(scale[...].astype(F32)) * vectors[:1, :]
    error_b = (gram - outer * (mine[:rows, :] + other[:rows, :]) / mass).astype(BF16)
    grads = 4.0 * jnp.dot(error_b, units[...], preferred_element_type=F32)
    along = 4.0 * jnp.sum(error_b.astype(F32) * gram, axis=1, keepdims=True)
    unit = stud[...].astype(F32) / norm
    out[...] = (grads - along * unit) / norm


def shards(student, teacher, scale):
    rows, half = student.shape
    nrow, ncol = lax.axis_size("row"), lax.axis_size("col")
    batch = rows * nrow * ncol
    part = teacher.shape[1] // nrow
    small = batch <= 2048
    sds = jax.ShapeDtypeStruct
    scale = scale.reshape(1, rows)

    def along_row(x, k):
        return lax.ppermute(x, "row", [(i, i ^ k) for i in range(nrow)])

    def along_col(x, c):
        return lax.ppermute(x, "col", [(i, (i - c) % ncol) for i in range(ncol)])

    def other_core(x):
        return lax.ppermute(x, "sub", [(0, 1), (1, 0)])

    def pack(xs, spans, after=()):
        shape = (sum(last - first for first, last in spans), half)
        return call(functools.partial(pack_kernel, spans), sds(shape, BF16), xs, after=after)

    def with_columns(x):
        return [x if c == 0 else along_col(x, c) for c in range(ncol)]

    middle, high = nrow // 2, rows * part // half
    order = list(range(middle, nrow)) + list(range(middle))
    riders = (1, middle)
    cuts = call(
        functools.partial(cut_kernel, nrow, riders),
        [sds((rows + high, half) if k in riders else (rows, part), BF16) for k in range(1, nrow)],
        [teacher, student],
        space=pl.ANY,
        scratch=[pltpu.SemaphoreType.DMA((nrow + 2 * (half // part),))],
        limit=60 << 20,
    )
    came = {k: along_row(cuts[k - 1], k) for k in order if k}
    own = call(
        functools.partial(own_kernel, nrow),
        sds((rows + TAIL + high, half), BF16),
        [teacher, student, scale],
        after=[came[nrow - 1]],
    )
    columns = {0: with_columns(own)}
    for k in range(1, nrow):
        piece = came[k]
        if k in riders:
            piece = call(functools.partial(take_kernel, rows), sds((rows, part), BF16), [piece])
        columns[k] = with_columns(piece)
    partial = call(
        functools.partial(gram_kernel, nrow, ncol, rows, order),
        [sds((rows, batch), BF16 if k else F32) for k in range(nrow)],
        [columns[k][c] for c in range(ncol) for k in range(nrow)],
        scratch=[pltpu.VMEM((batch, part), BF16), pltpu.VMEM((nrow * rows, part), BF16)],
    )
    returned = {k: along_row(partial[k], k) if k else partial[0] for k in order}

    near, far = came[1], came[middle]
    stack, keys, k, spans, got, got_keys = [student, far], [0, middle], middle // 2, [(0, rows)] * 2, [], []
    while k:
        first = 1 if k == 1 else 0
        sent = pack(stack[first:], spans[first:])
        got.append(along_row(sent, k))
        got_keys += [n ^ k for n in keys[first:]]
        stack, spans, keys = stack + got[-1:], spans + [(0, len(keys) * rows)], keys + [n ^ k for n in keys]
        k //= 2
    rest = pack([near, far] + got, [(0, rows)] * 2 + [(0, g.shape[0]) for g in got], after=[partial[0]])
    raw_keys = [[0], [1, middle] + got_keys]
    sources = [columns[0], with_columns(rest)]
    raw_refs = [x[c] for c in range(ncol) for x in sources]
    raw_gram, *all_raw = call(
        functools.partial(raw_gram_kernel, nrow, ncol, rows, raw_keys),
        [sds((rows + 8, batch), F32)] + ([sds((batch, half), BF16)] if small else []),
        raw_refs,
        scratch=[] if small else [pltpu.VMEM((batch, half), BF16)],
    )
    message, vectors = call(
        functools.partial(message_kernel, nrow, ncol, order),
        [sds((2 * rows + 16, batch), F32), sds((8, batch), F32)],
        [raw_gram] + [returned[k] for k in order],
    )
    return call(
        functools.partial(final_kernel, nrow, ncol, None if small else raw_keys),
        sds((rows, half), F32),
        [message, other_core(message), vectors, student, scale] + (all_raw if small else raw_refs),
        scratch=([] if small else [pltpu.VMEM((batch, half), BF16)]) + [pltpu.VMEM((batch, half), BF16)],
    )


def solution(mesh):
    spec = P(("groups", "row", "col"), "sub")
    return jax.shard_map(
        shards,
        mesh=mesh,
        in_specs=(spec, spec, P(("groups", "row", "col"))),
        out_specs=spec,
        check_vma=False,
    )
```

```python
import functools

import jax
import jax.numpy as jnp
from jax import lax
from jax.experimental import pallas as pl
from jax.experimental.pallas import tpu as pltpu
from jax.sharding import PartitionSpec as P

F32, BF16 = jnp.float32, jnp.bfloat16
INNER = (((1,), (1,)), ((), ()))
TAIL = 16


def call(body, out_shape, operands, scratch=(), after=()):
    outs = out_shape if isinstance(out_shape, (list, tuple)) else [out_shape]
    moved = sum(x.size * x.dtype.itemsize for x in list(operands) + list(outs))

    def run(*refs):
        body(*refs[: len(operands)], *refs[len(operands) + len(after) :])

    return pl.pallas_call(
        run,
        out_shape=out_shape,
        in_specs=[pl.BlockSpec(memory_space=pltpu.VMEM)] * len(operands) + [pl.BlockSpec(memory_space=pl.ANY)] * len(after),
        out_specs=jax.tree.map(lambda _: pl.BlockSpec(memory_space=pltpu.VMEM), out_shape),
        scratch_shapes=list(scratch),
        cost_estimate=pl.CostEstimate(flops=0, bytes_accessed=0, transcendentals=0),
        compiler_params=pltpu.CompilerParams(vmem_limit_bytes=min(56 << 20, (8 << 20) + 3 * moved)),
    )(*operands, *after)


def column(row):
    shape = (row.shape[1], row.shape[1])
    eye = lax.broadcasted_iota(jnp.int32, shape, 0) == lax.broadcasted_iota(jnp.int32, shape, 1)
    return jnp.sum(jnp.where(eye, row, 0.0), axis=1, keepdims=True)


def tags_of(scales, mass):
    shape = (TAIL, scales.shape[1])
    at = lax.broadcasted_iota(jnp.int32, shape, 0)
    high = mass.astype(BF16).astype(F32)
    return jnp.where(at < 8, scales, jnp.where(at < 12, high, mass - high)).astype(BF16)


def read_tags(tags):
    tags = tags.astype(F32)
    return tags[0:1, :], tags[8:9, 0:1] + tags[12:13, 0:1]


def lane_row(col):
    shape = (col.shape[0], col.shape[0])
    eye = lax.broadcasted_iota(jnp.int32, shape, 0) == lax.broadcasted_iota(jnp.int32, shape, 1)
    return jnp.sum(jnp.where(eye, col, 0.0), axis=0, keepdims=True)


def wide(out, at, piece):
    rows, part = piece.shape
    width = out.shape[1]
    high = rows * part // width
    for n in range(width // part):
        out[at : at + high, n * part : (n + 1) * part] = piece[n * high : (n + 1) * high, :]


def put(held, spot, rows, ref, at):
    width = held.shape[1]
    high = rows * width // ref.shape[1]
    for n in range(ref.shape[1] // width):
        held[pl.ds(spot + n * high, high), :] = ref[at : at + high, n * width : (n + 1) * width]


def cut_kernel(nrow, teach, *outs):
    part = teach.shape[1] // nrow
    z = lax.axis_index("row")
    for k in range(1, nrow):
        at = pl.multiple_of((z ^ k) * part, part)
        outs[k - 1][...] = teach[:, pl.ds(at, part)]


def ride_kernel(stud, *refs):
    rows, count = stud.shape[0], len(refs) // 2
    for piece, out in zip(refs[:count], refs[count:]):
        out[:rows, :] = stud[...]
        wide(out, rows, piece)


def own_kernel(nrow, teach, stud, scale, out):
    rows, half = stud.shape
    part = teach.shape[1] // nrow
    ts = teach[...].astype(F32)
    s = scale[...].astype(F32)
    mass = jnp.sum(jnp.square(column(s)) * jnp.sum(ts * ts, axis=1, keepdims=True), keepdims=True)
    tags = tags_of(jnp.concatenate([s, s], axis=1), mass)
    out[:rows, :] = stud[...]
    out[rows : rows + TAIL, :] = jnp.concatenate([tags] * (half // (2 * rows)), axis=1)
    wide(out, rows + TAIL, teach[:, pl.ds(pl.multiple_of(lax.axis_index("row") * part, part), part)])


def take_kernel(rows, ref, out):
    put(out, 0, rows, ref, rows)


def pack_kernel(spans, *refs):
    out, at = refs[-1], 0
    for r, (first, last) in zip(refs[:-1], spans):
        out[at : at + last - first, :] = r[first:last, :]
        at += last - first


def place(nrow, ncol, rows, k, c):
    return pl.multiple_of(((lax.axis_index("row") ^ k) * ncol + c) * rows, rows)


def group_spot(nrow, ncol, rows, k):
    return pl.multiple_of((lax.axis_index("row") ^ k) * ncol * rows, 2 * rows)


def gram_kernel(nrow, ncol, rows, order, *refs):
    count = nrow * ncol
    outs, held, left = refs[count : count + nrow], refs[-2], refs[-1]
    own = order.index(0) * ncol
    for n, k in enumerate(order):
        for c in range(ncol):
            put(held, place(nrow, ncol, rows, k, c), rows, refs[n * ncol + c], 0 if k else rows + TAIL)
    for n, k in enumerate(order):
        left[n * rows : (n + 1) * rows, :] = held[pl.ds(place(nrow, ncol, rows, k, 0), rows), :]
    sub = rows // 2
    at = lax.broadcasted_iota(jnp.int32, (sub, 2 * rows), 0)
    lane = lax.broadcasted_iota(jnp.int32, (sub, 2 * rows), 1)
    note, mass = jnp.zeros((sub, 2 * rows), F32), jnp.zeros((1, 1), F32)
    for c in range(ncol):
        scales, part = read_tags(refs[own + c][rows : rows + TAIL, : 2 * rows])
        turned = jnp.concatenate([scales[:, sub:], scales[:, :sub]], axis=1)
        note = jnp.where(at == 2 * c, scales, jnp.where(at == 2 * c + 1, turned, note))
        mass = mass + part
    high = mass.astype(BF16).astype(F32)
    note = jnp.where(at < sub // 2, note, jnp.where(at < sub * 3 // 4, high, mass - high))
    per = max(1, 2048 * rows * nrow // held.shape[0] // rows // 8)
    for first in range(0, nrow, per):
        last = min(first + per, nrow)
        gram = lax.dot_general(left[first * rows : last * rows, :], held[...], INNER, preferred_element_type=F32)
        for n in range(first, last):
            out = outs[order[n]]
            out[...] = gram[(n - first) * rows : (n - first + 1) * rows, :].astype(out.dtype)
            spot = pl.ds(group_spot(nrow, ncol, rows, order[n]), 2 * rows)
            seen = out[sub:, spot].astype(F32)
            out[sub:, spot] = jnp.where(lane < sub, note, seen).astype(out.dtype)


def assemble(nrow, ncol, rows, keys, refs, held):
    each = len(keys)
    for c in range(ncol):
        for stack, ref in zip(keys, refs[c * each : (c + 1) * each]):
            for n, k in enumerate(stack):
                held[pl.ds(place(nrow, ncol, rows, k, c), rows), :] = ref[n * rows : (n + 1) * rows, :]


def raw_gram_kernel(nrow, ncol, rows, keys, *refs):
    count = len(keys) * ncol
    out, raw = refs[count:]
    assemble(nrow, ncol, rows, keys, refs, raw)
    out[:rows, :] = lax.dot_general(refs[0][:rows, :], raw[...], INNER, preferred_element_type=F32)
    for at in range(0, raw.shape[0], 128):
        squares = jnp.sum(jnp.square(raw[at : at + 128, :].astype(F32)), axis=1, keepdims=True)
        out[rows:, at : at + 128] = jnp.broadcast_to(lane_row(squares), (8, 128))


def message_kernel(nrow, ncol, order, raw_gram, *refs):
    parts, (out, vectors) = [refs[order.index(k)] for k in range(nrow)], refs[-2:]
    rows = parts[0].shape[0]
    sub = rows // 2
    total = parts[0][...].astype(F32)
    for r in parts[1:]:
        total = total + r[...].astype(F32)
    out[:rows, :] = total
    own = pl.ds(group_spot(nrow, ncol, rows, 0), 2 * rows)
    mirror = jnp.transpose(out[:sub, own])[sub : 2 * sub, :]
    out[sub:rows, own] = jnp.concatenate([mirror, out[sub:rows, own][:, sub:]], axis=1)
    mass = jnp.zeros((1, 1), F32)
    for k, part in enumerate(parts):
        note = part[sub:, own].astype(F32)[:, :sub]
        mass = mass + note[sub // 2 : sub // 2 + 1, :1] + note[sub * 3 // 4 : sub * 3 // 4 + 1, :1]
        line = jnp.concatenate([note[n : n + 1, :] for n in range(2 * ncol)], axis=1)
        vectors[:, pl.ds(group_spot(nrow, ncol, rows, k), ncol * rows)] = jnp.broadcast_to(line, (8, ncol * rows))
    out[rows : 2 * rows + 8, :] = raw_gram[...]
    out[2 * rows + 8 :, :] = jnp.broadcast_to(mass, (8, out.shape[1]))


def final_kernel(nrow, ncol, keys, mine, other, vectors, stud, scale, *refs):
    rows = stud.shape[0]
    if keys:
        out, raw, units = refs[-3:]
        assemble(nrow, ncol, rows, keys, refs, raw)
    else:
        raw, out, units = refs
    batch = mine.shape[1]
    squares = mine[2 * rows : 2 * rows + 8, :] + other[2 * rows : 2 * rows + 8, :]
    for at in range(0, batch, 128):
        norm = jnp.sqrt(column(squares[:1, at : at + 128]))
        units[at : at + 128, :] = (raw[at : at + 128, :].astype(F32) / norm).astype(BF16)
    at = pl.ds(group_spot(nrow, ncol, rows, 0), 2 * rows)
    own = (mine[2 * rows : 2 * rows + 8, at] + other[2 * rows : 2 * rows + 8, at])[:1, :rows]
    norm = jnp.sqrt(column(own))
    mass = (mine[2 * rows + 8 : 2 * rows + 9, :1] + other[2 * rows + 8 : 2 * rows + 9, :1]) / batch
    gram = (mine[rows : 2 * rows, :] + other[rows : 2 * rows, :]) / (norm * jnp.sqrt(squares[:1, :]))
    outer = column(scale[...].astype(F32)) * vectors[:1, :]
    error_b = (gram - outer * (mine[:rows, :] + other[:rows, :]) / mass).astype(BF16)
    grads = 4.0 * jnp.dot(error_b, units[...], preferred_element_type=F32)
    along = 4.0 * jnp.sum(error_b.astype(F32) * gram, axis=1, keepdims=True)
    unit = stud[...].astype(F32) / norm
    out[...] = (grads - along * unit) / norm


def shards(student, teacher, scale):
    rows, half = student.shape
    nrow, ncol = lax.axis_size("row"), lax.axis_size("col")
    batch = rows * nrow * ncol
    part = teacher.shape[1] // nrow
    small = batch <= 2048
    sds = jax.ShapeDtypeStruct
    scale = scale.reshape(1, rows)

    def along_row(x, k):
        return lax.ppermute(x, "row", [(i, i ^ k) for i in range(nrow)])

    def along_col(x, c):
        return lax.ppermute(x, "col", [(i, (i - c) % ncol) for i in range(ncol)])

    def other_core(x):
        return lax.ppermute(x, "sub", [(0, 1), (1, 0)])

    def pack(xs, spans, after=()):
        shape = (sum(last - first for first, last in spans), half)
        return call(functools.partial(pack_kernel, spans), sds(shape, BF16), xs, after=after)

    def with_columns(x):
        return [x if c == 0 else along_col(x, c) for c in range(ncol)]

    middle, high = nrow // 2, rows * part // half
    order = list(range(middle, nrow)) + list(range(middle))
    riders = (1, middle)
    cuts = call(functools.partial(cut_kernel, nrow), [sds((rows, part), BF16)] * (nrow - 1), [teacher])
    ridden = call(ride_kernel, [sds((rows + high, half), BF16)] * 2, [student] + [cuts[k - 1] for k in riders])
    leaving = dict(enumerate(cuts, 1)) | dict(zip(riders, ridden))
    came = {k: along_row(leaving[k], k) for k in order if k}
    own = call(
        functools.partial(own_kernel, nrow),
        sds((rows + TAIL + high, half), BF16),
        [teacher, student, scale],
        after=[came[nrow - 1]],
    )
    columns = {0: with_columns(own)}
    for k in range(1, nrow):
        piece = came[k]
        if k in riders:
            piece = call(functools.partial(take_kernel, rows), sds((rows, part), BF16), [piece])
        columns[k] = with_columns(piece)
    partial = call(
        functools.partial(gram_kernel, nrow, ncol, rows, order),
        [sds((rows, batch), BF16 if k else F32) for k in range(nrow)],
        [columns[k][c] for k in order for c in range(ncol)],
        scratch=[pltpu.VMEM((batch, part), BF16), pltpu.VMEM((nrow * rows, part), BF16)],
    )
    returned = {k: along_row(partial[k], k) if k else partial[0] for k in order}

    near, far = came[1], came[middle]
    stack, keys, k, spans, got, got_keys = [student, far], [0, middle], middle // 2, [(0, rows)] * 2, [], []
    while k:
        first = 1 if k == 1 else 0
        sent = pack(stack[first:], spans[first:])
        got.append(along_row(sent, k))
        got_keys += [n ^ k for n in keys[first:]]
        stack, spans, keys = stack + got[-1:], spans + [(0, len(keys) * rows)], keys + [n ^ k for n in keys]
        k //= 2
    rest = pack([near, far] + got, [(0, rows)] * 2 + [(0, g.shape[0]) for g in got], after=[partial[0]])
    raw_keys = [[0], [1, middle] + got_keys]
    sources = [columns[0], with_columns(rest)]
    raw_refs = [x[c] for c in range(ncol) for x in sources]
    raw_gram, *all_raw = call(
        functools.partial(raw_gram_kernel, nrow, ncol, rows, raw_keys),
        [sds((rows + 8, batch), F32)] + ([sds((batch, half), BF16)] if small else []),
        raw_refs,
        scratch=[] if small else [pltpu.VMEM((batch, half), BF16)],
    )
    message, vectors = call(
        functools.partial(message_kernel, nrow, ncol, order),
        [sds((2 * rows + 16, batch), F32), sds((8, batch), F32)],
        [raw_gram] + [returned[k] for k in order],
    )
    return call(
        functools.partial(final_kernel, nrow, ncol, None if small else raw_keys),
        sds((rows, half), F32),
        [message, other_core(message), vectors, student, scale] + (all_raw if small else raw_refs),
        scratch=([] if small else [pltpu.VMEM((batch, half), BF16)]) + [pltpu.VMEM((batch, half), BF16)],
    )


def solution(mesh):
    spec = P(("groups", "row", "col"), "sub")
    return jax.shard_map(
        shards,
        mesh=mesh,
        in_specs=(spec, spec, P(("groups", "row", "col"))),
        out_specs=spec,
        check_vma=False,
    )
```

```python
import functools

import jax
import jax.numpy as jnp
from jax import lax
from jax.experimental import pallas as pl
from jax.experimental.pallas import tpu as pltpu
from jax.sharding import PartitionSpec as P

F32, BF16 = jnp.float32, jnp.bfloat16
INNER = (((1,), (1,)), ((), ()))
TAIL = 16


def call(body, out_shape, operands, scratch=(), after=()):
    outs = out_shape if isinstance(out_shape, (list, tuple)) else [out_shape]
    moved = sum(x.size * x.dtype.itemsize for x in list(operands) + list(outs))

    def run(*refs):
        body(*refs[: len(operands)], *refs[len(operands) + len(after) :])

    return pl.pallas_call(
        run,
        out_shape=out_shape,
        in_specs=[pl.BlockSpec(memory_space=pltpu.VMEM)] * len(operands) + [pl.BlockSpec(memory_space=pl.ANY)] * len(after),
        out_specs=jax.tree.map(lambda _: pl.BlockSpec(memory_space=pltpu.VMEM), out_shape),
        scratch_shapes=list(scratch),
        cost_estimate=pl.CostEstimate(flops=0, bytes_accessed=0, transcendentals=0),
        compiler_params=pltpu.CompilerParams(vmem_limit_bytes=min(56 << 20, (8 << 20) + 3 * moved)),
    )(*operands, *after)


def column(row):
    shape = (row.shape[1], row.shape[1])
    eye = lax.broadcasted_iota(jnp.int32, shape, 0) == lax.broadcasted_iota(jnp.int32, shape, 1)
    return jnp.sum(jnp.where(eye, row, 0.0), axis=1, keepdims=True)


def tags_of(scales, mass):
    shape = (TAIL, scales.shape[1])
    at = lax.broadcasted_iota(jnp.int32, shape, 0)
    high = mass.astype(BF16).astype(F32)
    return jnp.where(at < 8, scales, jnp.where(at < 12, high, mass - high)).astype(BF16)


def read_tags(tags):
    tags = tags.astype(F32)
    return tags[0:1, :], tags[8:9, 0:1] + tags[12:13, 0:1]


def lane_row(col):
    shape = (col.shape[0], col.shape[0])
    eye = lax.broadcasted_iota(jnp.int32, shape, 0) == lax.broadcasted_iota(jnp.int32, shape, 1)
    return jnp.sum(jnp.where(eye, col, 0.0), axis=0, keepdims=True)


def wide(out, at, piece):
    rows, part = piece.shape
    width = out.shape[1]
    high = rows * part // width
    for n in range(width // part):
        out[at : at + high, n * part : (n + 1) * part] = piece[n * high : (n + 1) * high, :]


def put(held, spot, rows, ref, at):
    width = held.shape[1]
    high = rows * width // ref.shape[1]
    for n in range(ref.shape[1] // width):
        held[pl.ds(spot + n * high, high), :] = ref[at : at + high, n * width : (n + 1) * width]


def cut_kernel(nrow, teach, *outs):
    part = teach.shape[1] // nrow
    z = lax.axis_index("row")
    for k in range(1, nrow):
        at = pl.multiple_of((z ^ k) * part, part)
        outs[k - 1][...] = teach[:, pl.ds(at, part)]


def ride_kernel(stud, piece, out):
    rows = stud.shape[0]
    out[:rows, :] = stud[...]
    wide(out, rows, piece[...])


def own_kernel(nrow, teach, stud, scale, out):
    rows, half = stud.shape
    part = teach.shape[1] // nrow
    ts = teach[...].astype(F32)
    s = scale[...].astype(F32)
    mass = jnp.sum(jnp.square(column(s)) * jnp.sum(ts * ts, axis=1, keepdims=True), keepdims=True)
    tags = tags_of(jnp.concatenate([s, s], axis=1), mass)
    out[:rows, :] = stud[...]
    out[rows : rows + TAIL, :] = jnp.concatenate([tags] * (half // (2 * rows)), axis=1)
    wide(out, rows + TAIL, teach[:, pl.ds(pl.multiple_of(lax.axis_index("row") * part, part), part)])


def take_kernel(rows, ref, out):
    put(out, 0, rows, ref, rows)


def pack_kernel(spans, *refs):
    out, at = refs[-1], 0
    for r, (first, last) in zip(refs[:-1], spans):
        out[at : at + last - first, :] = r[first:last, :]
        at += last - first


def place(nrow, ncol, rows, k, c):
    return pl.multiple_of(((lax.axis_index("row") ^ k) * ncol + c) * rows, rows)


def group_spot(nrow, ncol, rows, k):
    return pl.multiple_of((lax.axis_index("row") ^ k) * ncol * rows, 2 * rows)


def gram_kernel(nrow, ncol, rows, order, *refs):
    count = nrow * ncol
    outs, held, left = refs[count : count + nrow], refs[-2], refs[-1]
    own = order.index(0) * ncol
    for n, k in enumerate(order):
        for c in range(ncol):
            put(held, place(nrow, ncol, rows, k, c), rows, refs[n * ncol + c], 0 if k else rows + TAIL)
    for n, k in enumerate(order):
        left[n * rows : (n + 1) * rows, :] = held[pl.ds(place(nrow, ncol, rows, k, 0), rows), :]
    sub = rows // 2
    at = lax.broadcasted_iota(jnp.int32, (sub, 2 * rows), 0)
    lane = lax.broadcasted_iota(jnp.int32, (sub, 2 * rows), 1)
    note, mass = jnp.zeros((sub, 2 * rows), F32), jnp.zeros((1, 1), F32)
    for c in range(ncol):
        scales, part = read_tags(refs[own + c][rows : rows + TAIL, : 2 * rows])
        turned = jnp.concatenate([scales[:, sub:], scales[:, :sub]], axis=1)
        note = jnp.where(at == 2 * c, scales, jnp.where(at == 2 * c + 1, turned, note))
        mass = mass + part
    high = mass.astype(BF16).astype(F32)
    note = jnp.where(at < sub // 2, note, jnp.where(at < sub * 3 // 4, high, mass - high))
    per = max(1, 2048 * rows * nrow // held.shape[0] // rows // 8)
    for first in range(0, nrow, per):
        last = min(first + per, nrow)
        gram = lax.dot_general(left[first * rows : last * rows, :], held[...], INNER, preferred_element_type=F32)
        for n in range(first, last):
            out = outs[order[n]]
            out[...] = gram[(n - first) * rows : (n - first + 1) * rows, :].astype(out.dtype)
            spot = pl.ds(group_spot(nrow, ncol, rows, order[n]), 2 * rows)
            seen = out[sub:, spot].astype(F32)
            out[sub:, spot] = jnp.where(lane < sub, note, seen).astype(out.dtype)


def assemble(nrow, ncol, rows, keys, refs, held):
    each = len(keys)
    for c in range(ncol):
        for stack, ref in zip(keys, refs[c * each : (c + 1) * each]):
            for n, k in enumerate(stack):
                held[pl.ds(place(nrow, ncol, rows, k, c), rows), :] = ref[n * rows : (n + 1) * rows, :]


def raw_gram_kernel(nrow, ncol, rows, keys, *refs):
    count = len(keys) * ncol
    out, raw = refs[count:]
    assemble(nrow, ncol, rows, keys, refs, raw)
    out[:rows, :] = lax.dot_general(refs[0][:rows, :], raw[...], INNER, preferred_element_type=F32)
    for at in range(0, raw.shape[0], 128):
        squares = jnp.sum(jnp.square(raw[at : at + 128, :].astype(F32)), axis=1, keepdims=True)
        out[rows:, at : at + 128] = jnp.broadcast_to(lane_row(squares), (8, 128))


def message_kernel(nrow, ncol, order, raw_gram, *refs):
    parts, (out, vectors) = [refs[order.index(k)] for k in range(nrow)], refs[-2:]
    rows = parts[0].shape[0]
    sub = rows // 2
    total = parts[0][...].astype(F32)
    for r in parts[1:]:
        total = total + r[...].astype(F32)
    out[:rows, :] = total
    own = pl.ds(group_spot(nrow, ncol, rows, 0), 2 * rows)
    mirror = jnp.transpose(out[:sub, own])[sub : 2 * sub, :]
    out[sub:rows, own] = jnp.concatenate([mirror, out[sub:rows, own][:, sub:]], axis=1)
    mass = jnp.zeros((1, 1), F32)
    for k, part in enumerate(parts):
        note = part[sub:, own].astype(F32)[:, :sub]
        mass = mass + note[sub // 2 : sub // 2 + 1, :1] + note[sub * 3 // 4 : sub * 3 // 4 + 1, :1]
        line = jnp.concatenate([note[n : n + 1, :] for n in range(2 * ncol)], axis=1)
        vectors[:, pl.ds(group_spot(nrow, ncol, rows, k), ncol * rows)] = jnp.broadcast_to(line, (8, ncol * rows))
    out[rows : 2 * rows + 8, :] = raw_gram[...]
    out[2 * rows + 8 :, :] = jnp.broadcast_to(mass, (8, out.shape[1]))


def final_kernel(nrow, ncol, keys, mine, other, vectors, stud, scale, *refs):
    rows = stud.shape[0]
    if keys:
        out, raw, units = refs[-3:]
        assemble(nrow, ncol, rows, keys, refs, raw)
    else:
        raw, out, units = refs
    batch = mine.shape[1]
    squares = mine[2 * rows : 2 * rows + 8, :] + other[2 * rows : 2 * rows + 8, :]
    for at in range(0, batch, 128):
        inverse = 1.0 / jnp.sqrt(column(squares[:1, at : at + 128]))
        units[at : at + 128, :] = (raw[at : at + 128, :].astype(F32) * inverse).astype(BF16)
    at = pl.ds(group_spot(nrow, ncol, rows, 0), 2 * rows)
    own = (mine[2 * rows : 2 * rows + 8, at] + other[2 * rows : 2 * rows + 8, at])[:1, :rows]
    inverse = 1.0 / jnp.sqrt(column(own))
    mass = (mine[2 * rows + 8 : 2 * rows + 9, :1] + other[2 * rows + 8 : 2 * rows + 9, :1]) / batch
    gram = (mine[rows : 2 * rows, :] + other[rows : 2 * rows, :]) * (inverse * (1.0 / jnp.sqrt(squares[:1, :])))
    outer = (column(scale[...].astype(F32)) / mass) * vectors[:1, :]
    error_b = (gram - outer * (mine[:rows, :] + other[:rows, :])).astype(BF16)
    grads = 4.0 * jnp.dot(error_b, units[...], preferred_element_type=F32)
    along = 4.0 * jnp.sum(error_b.astype(F32) * gram, axis=1, keepdims=True)
    unit = stud[...].astype(F32) * inverse
    out[...] = (grads - along * unit) * inverse


def shards(student, teacher, scale):
    rows, half = student.shape
    nrow, ncol = lax.axis_size("row"), lax.axis_size("col")
    batch = rows * nrow * ncol
    part = teacher.shape[1] // nrow
    small = batch <= 2048
    sds = jax.ShapeDtypeStruct
    scale = scale.reshape(1, rows)

    def along_row(x, k):
        return lax.ppermute(x, "row", [(i, i ^ k) for i in range(nrow)])

    def along_col(x, c):
        return lax.ppermute(x, "col", [(i, (i - c) % ncol) for i in range(ncol)])

    def other_core(x):
        return lax.ppermute(x, "sub", [(0, 1), (1, 0)])

    def pack(xs, spans, after=()):
        shape = (sum(last - first for first, last in spans), half)
        return call(functools.partial(pack_kernel, spans), sds(shape, BF16), xs, after=after)

    def with_columns(x):
        return [x if c == 0 else along_col(x, c) for c in range(ncol)]

    middle, high = nrow // 2, rows * part // half
    order = list(range(middle, nrow)) + list(range(middle))
    riders = (1, middle)
    cuts = call(functools.partial(cut_kernel, nrow), [sds((rows, part), BF16)] * (nrow - 1), [teacher])
    last = nrow - 1
    came, landed = {last: along_row(cuts[last - 1], last)}, ()
    for k in [k for k in order if k not in (0, 1, last)] + [1]:
        leaving = cuts[k - 1]
        if k in riders:
            leaving = call(ride_kernel, sds((rows + high, half), BF16), [student, leaving], after=landed)
            landed = (came[last],)
        came[k] = along_row(leaving, k)
    own = call(
        functools.partial(own_kernel, nrow),
        sds((rows + TAIL + high, half), BF16),
        [teacher, student, scale],
        after=[came[nrow - 1]],
    )
    columns = {0: with_columns(own)}
    for k in range(1, nrow):
        piece = came[k]
        if k in riders:
            piece = call(functools.partial(take_kernel, rows), sds((rows, part), BF16), [piece])
        columns[k] = with_columns(piece)
    partial = call(
        functools.partial(gram_kernel, nrow, ncol, rows, order),
        [sds((rows, batch), BF16 if k else F32) for k in range(nrow)],
        [columns[k][c] for k in order for c in range(ncol)],
        scratch=[pltpu.VMEM((batch, part), BF16), pltpu.VMEM((nrow * rows, part), BF16)],
    )
    returned = {k: along_row(partial[k], k) if k else partial[0] for k in order}

    near, far = came[1], came[middle]
    stack, keys, k, spans, got, got_keys = [student, far], [0, middle], middle // 2, [(0, rows)] * 2, [], []
    while k:
        first = 1 if k == 1 else 0
        sent = pack(stack[first:], spans[first:])
        got.append(along_row(sent, k))
        got_keys += [n ^ k for n in keys[first:]]
        stack, spans, keys = stack + got[-1:], spans + [(0, len(keys) * rows)], keys + [n ^ k for n in keys]
        k //= 2
    rest = pack([near, far] + got, [(0, rows)] * 2 + [(0, g.shape[0]) for g in got], after=[partial[0]])
    raw_keys = [[0], [1, middle] + got_keys]
    sources = [columns[0], with_columns(rest)]
    raw_refs = [x[c] for c in range(ncol) for x in sources]
    raw_gram, *all_raw = call(
        functools.partial(raw_gram_kernel, nrow, ncol, rows, raw_keys),
        [sds((rows + 8, batch), F32)] + ([sds((batch, half), BF16)] if small else []),
        raw_refs,
        scratch=[] if small else [pltpu.VMEM((batch, half), BF16)],
    )
    message, vectors = call(
        functools.partial(message_kernel, nrow, ncol, order),
        [sds((2 * rows + 16, batch), F32), sds((8, batch), F32)],
        [raw_gram] + [returned[k] for k in order],
    )
    return call(
        functools.partial(final_kernel, nrow, ncol, None if small else raw_keys),
        sds((rows, half), F32),
        [message, other_core(message), vectors, student, scale] + (all_raw if small else raw_refs),
        scratch=([] if small else [pltpu.VMEM((batch, half), BF16)]) + [pltpu.VMEM((batch, half), BF16)],
    )


def solution(mesh):
    spec = P(("groups", "row", "col"), "sub")
    return jax.shard_map(
        shards,
        mesh=mesh,
        in_specs=(spec, spec, P(("groups", "row", "col"))),
        out_specs=spec,
        check_vma=False,
    )
```

```python
import functools

import jax
import jax.numpy as jnp
from jax import lax
from jax.experimental import pallas as pl
from jax.experimental.pallas import tpu as pltpu
from jax.sharding import PartitionSpec as P

F32, BF16 = jnp.float32, jnp.bfloat16
INNER = (((1,), (1,)), ((), ()))
TAIL = 16


def call(body, out_shape, operands, scratch=(), after=()):
    outs = out_shape if isinstance(out_shape, (list, tuple)) else [out_shape]
    moved = sum(x.size * x.dtype.itemsize for x in list(operands) + list(outs))

    def run(*refs):
        body(*refs[: len(operands)], *refs[len(operands) + len(after) :])

    return pl.pallas_call(
        run,
        out_shape=out_shape,
        in_specs=[pl.BlockSpec(memory_space=pltpu.VMEM)] * len(operands) + [pl.BlockSpec(memory_space=pl.ANY)] * len(after),
        out_specs=jax.tree.map(lambda _: pl.BlockSpec(memory_space=pltpu.VMEM), out_shape),
        scratch_shapes=list(scratch),
        cost_estimate=pl.CostEstimate(flops=0, bytes_accessed=0, transcendentals=0),
        compiler_params=pltpu.CompilerParams(vmem_limit_bytes=min(56 << 20, (8 << 20) + 3 * moved)),
    )(*operands, *after)


def column(row):
    shape = (row.shape[1], row.shape[1])
    eye = lax.broadcasted_iota(jnp.int32, shape, 0) == lax.broadcasted_iota(jnp.int32, shape, 1)
    return jnp.sum(jnp.where(eye, row, 0.0), axis=1, keepdims=True)


def tags_of(scales, mass):
    shape = (TAIL, scales.shape[1])
    at = lax.broadcasted_iota(jnp.int32, shape, 0)
    high = mass.astype(BF16).astype(F32)
    return jnp.where(at < 8, scales, jnp.where(at < 12, high, mass - high)).astype(BF16)


def read_tags(tags):
    tags = tags.astype(F32)
    return tags[0:1, :], tags[8:9, 0:1] + tags[12:13, 0:1]


def lane_row(col):
    shape = (col.shape[0], col.shape[0])
    eye = lax.broadcasted_iota(jnp.int32, shape, 0) == lax.broadcasted_iota(jnp.int32, shape, 1)
    return jnp.sum(jnp.where(eye, col, 0.0), axis=0, keepdims=True)


def wide(out, at, piece):
    rows, part = piece.shape
    width = out.shape[1]
    high = rows * part // width
    for n in range(width // part):
        out[at : at + high, n * part : (n + 1) * part] = piece[n * high : (n + 1) * high, :]


def put(held, spot, rows, ref, at):
    width = held.shape[1]
    high = rows * width // ref.shape[1]
    for n in range(ref.shape[1] // width):
        held[pl.ds(spot + n * high, high), :] = ref[at : at + high, n * width : (n + 1) * width]


def cut_kernel(nrow, teach, *outs):
    part = teach.shape[1] // nrow
    z = lax.axis_index("row")
    for k in range(1, nrow):
        at = pl.multiple_of((z ^ k) * part, part)
        outs[k - 1][...] = teach[:, pl.ds(at, part)]


def ride_kernel(stud, piece, out):
    rows = stud.shape[0]
    out[:rows, :] = stud[...]
    wide(out, rows, piece[...])


def own_kernel(nrow, teach, stud, scale, out):
    rows, half = stud.shape
    part = teach.shape[1] // nrow
    ts = teach[...].astype(F32)
    s = scale[...].astype(F32)
    mass = jnp.sum(jnp.square(column(s)) * jnp.sum(ts * ts, axis=1, keepdims=True), keepdims=True)
    tags = tags_of(jnp.concatenate([s, s], axis=1), mass)
    out[:rows, :] = stud[...]
    out[rows : rows + TAIL, :] = jnp.concatenate([tags] * (half // (2 * rows)), axis=1)
    wide(out, rows + TAIL, teach[:, pl.ds(pl.multiple_of(lax.axis_index("row") * part, part), part)])


def take_kernel(rows, ref, out):
    put(out, 0, rows, ref, rows)


def pack_kernel(spans, *refs):
    out, at = refs[-1], 0
    for r, (first, last) in zip(refs[:-1], spans):
        out[at : at + last - first, :] = r[first:last, :]
        at += last - first


def place(nrow, ncol, rows, k, c):
    return pl.multiple_of(((lax.axis_index("row") ^ k) * ncol + c) * rows, rows)


def group_spot(nrow, ncol, rows, k):
    return pl.multiple_of((lax.axis_index("row") ^ k) * ncol * rows, 2 * rows)


def gram_kernel(nrow, ncol, rows, order, *refs):
    count = nrow * ncol
    outs, held, left = refs[count : count + nrow], refs[-2], refs[-1]
    own = order.index(0) * ncol
    for n, k in enumerate(order):
        for c in range(ncol):
            put(held, place(nrow, ncol, rows, k, c), rows, refs[n * ncol + c], 0 if k else rows + TAIL)
    for n, k in enumerate(order):
        left[n * rows : (n + 1) * rows, :] = held[pl.ds(place(nrow, ncol, rows, k, 0), rows), :]
    sub = rows // 2
    at = lax.broadcasted_iota(jnp.int32, (sub, 2 * rows), 0)
    lane = lax.broadcasted_iota(jnp.int32, (sub, 2 * rows), 1)
    note, mass = jnp.zeros((sub, 2 * rows), F32), jnp.zeros((1, 1), F32)
    for c in range(ncol):
        scales, part = read_tags(refs[own + c][rows : rows + TAIL, : 2 * rows])
        turned = jnp.concatenate([scales[:, sub:], scales[:, :sub]], axis=1)
        note = jnp.where(at == 2 * c, scales, jnp.where(at == 2 * c + 1, turned, note))
        mass = mass + part
    high = mass.astype(BF16).astype(F32)
    note = jnp.where(at < sub // 2, note, jnp.where(at < sub * 3 // 4, high, mass - high))
    per = max(1, 2048 * rows * nrow // held.shape[0] // rows // 8)
    for first in range(0, nrow, per):
        last = min(first + per, nrow)
        gram = lax.dot_general(left[first * rows : last * rows, :], held[...], INNER, preferred_element_type=F32)
        for n in range(first, last):
            out = outs[order[n]]
            out[...] = gram[(n - first) * rows : (n - first + 1) * rows, :].astype(out.dtype)
            spot = pl.ds(group_spot(nrow, ncol, rows, order[n]), 2 * rows)
            seen = out[sub:, spot].astype(F32)
            out[sub:, spot] = jnp.where(lane < sub, note, seen).astype(out.dtype)


def assemble(nrow, ncol, rows, keys, refs, held):
    each = len(keys)
    for c in range(ncol):
        for stack, ref in zip(keys, refs[c * each : (c + 1) * each]):
            for n, k in enumerate(stack):
                held[pl.ds(place(nrow, ncol, rows, k, c), rows), :] = ref[n * rows : (n + 1) * rows, :]


def raw_gram_kernel(nrow, ncol, rows, keys, *refs):
    count = len(keys) * ncol
    out, raw = refs[count:]
    assemble(nrow, ncol, rows, keys, refs, raw)
    out[:rows, :] = lax.dot_general(refs[0][:rows, :], raw[...], INNER, preferred_element_type=F32)
    for at in range(0, raw.shape[0], 128):
        squares = jnp.sum(jnp.square(raw[at : at + 128, :].astype(F32)), axis=1, keepdims=True)
        out[rows:, at : at + 128] = jnp.broadcast_to(lane_row(squares), (8, 128))


def message_kernel(nrow, ncol, order, raw_gram, *refs):
    parts, (out, vectors) = [refs[order.index(k)] for k in range(nrow)], refs[-2:]
    rows = parts[0].shape[0]
    sub = rows // 2
    total = parts[0][...].astype(F32)
    for r in parts[1:]:
        total = total + r[...].astype(F32)
    out[:rows, :] = total
    own = pl.ds(group_spot(nrow, ncol, rows, 0), 2 * rows)
    mirror = jnp.transpose(out[:sub, own])[sub : 2 * sub, :]
    out[sub:rows, own] = jnp.concatenate([mirror, out[sub:rows, own][:, sub:]], axis=1)
    mass = jnp.zeros((1, 1), F32)
    for k, part in enumerate(parts):
        note = part[sub:, own].astype(F32)[:, :sub]
        mass = mass + note[sub // 2 : sub // 2 + 1, :1] + note[sub * 3 // 4 : sub * 3 // 4 + 1, :1]
        line = jnp.concatenate([note[n : n + 1, :] for n in range(2 * ncol)], axis=1)
        vectors[:, pl.ds(group_spot(nrow, ncol, rows, k), ncol * rows)] = jnp.broadcast_to(line, (8, ncol * rows))
    out[rows : 2 * rows + 8, :] = raw_gram[...]
    out[2 * rows + 8 :, :] = jnp.broadcast_to(mass, (8, out.shape[1]))


def final_kernel(nrow, ncol, keys, mine, other, vectors, stud, scale, *refs):
    rows = stud.shape[0]
    if keys:
        out, raw, units = refs[-3:]
        assemble(nrow, ncol, rows, keys, refs, raw)
    else:
        raw, out, units = refs
    batch = mine.shape[1]
    squares = mine[2 * rows : 2 * rows + 8, :] + other[2 * rows : 2 * rows + 8, :]
    for at in range(0, batch, 128):
        inverse = 1.0 / jnp.sqrt(column(squares[:1, at : at + 128]))
        units[at : at + 128, :] = (raw[at : at + 128, :].astype(F32) * inverse).astype(BF16)
    at = pl.ds(group_spot(nrow, ncol, rows, 0), 2 * rows)
    own = (mine[2 * rows : 2 * rows + 8, at] + other[2 * rows : 2 * rows + 8, at])[:1, :rows]
    inverse = 1.0 / jnp.sqrt(column(own))
    mass = (mine[2 * rows + 8 : 2 * rows + 9, :1] + other[2 * rows + 8 : 2 * rows + 9, :1]) / batch
    gram = (mine[rows : 2 * rows, :] + other[rows : 2 * rows, :]) * (inverse * (1.0 / jnp.sqrt(squares[:1, :])))
    outer = (column(scale[...].astype(F32)) / mass) * vectors[:1, :]
    error_b = (gram - outer * (mine[:rows, :] + other[:rows, :])).astype(BF16)
    grads = 4.0 * jnp.dot(error_b, units[...], preferred_element_type=F32)
    along = 4.0 * jnp.sum(error_b.astype(F32) * gram, axis=1, keepdims=True)
    unit = stud[...].astype(F32) * inverse
    out[...] = (grads - along * unit) * inverse


def shards(student, teacher, scale):
    rows, half = student.shape
    nrow, ncol = lax.axis_size("row"), lax.axis_size("col")
    batch = rows * nrow * ncol
    part = teacher.shape[1] // nrow
    small = batch <= 2048
    sds = jax.ShapeDtypeStruct
    scale = scale.reshape(1, rows)

    def along_row(x, k):
        return lax.ppermute(x, "row", [(i, i ^ k) for i in range(nrow)])

    def along_col(x, c):
        return lax.ppermute(x, "col", [(i, (i - c) % ncol) for i in range(ncol)])

    def other_core(x):
        return lax.ppermute(x, "sub", [(0, 1), (1, 0)])

    def pack(xs, spans, after=()):
        shape = (sum(last - first for first, last in spans), half)
        return call(functools.partial(pack_kernel, spans), sds(shape, BF16), xs, after=after)

    def with_columns(x):
        return [x if c == 0 else along_col(x, c) for c in range(ncol)]

    middle, high = nrow // 2, rows * part // half
    order = list(range(middle, nrow)) + list(range(middle))
    riders = (1, middle)
    cuts = call(functools.partial(cut_kernel, nrow), [sds((rows, part), BF16)] * (nrow - 1), [teacher])
    came = {}
    for k in order:
        if k:
            leaving = cuts[k - 1]
            if k in riders:
                leaving = call(ride_kernel, sds((rows + high, half), BF16), [student, leaving])
            came[k] = along_row(leaving, k)
    own = call(
        functools.partial(own_kernel, nrow),
        sds((rows + TAIL + high, half), BF16),
        [teacher, student, scale],
        after=[came[nrow - 1]],
    )
    columns, taken = {0: with_columns(own)}, ()
    for k in order:
        piece = came.get(k)
        if k in riders:
            piece = call(functools.partial(take_kernel, rows), sds((rows, part), BF16), [piece], after=taken)
            taken = (piece,)
        if k:
            columns[k] = with_columns(piece)
    partial = call(
        functools.partial(gram_kernel, nrow, ncol, rows, order),
        [sds((rows, batch), BF16 if k else F32) for k in range(nrow)],
        [columns[k][c] for k in order for c in range(ncol)],
        scratch=[pltpu.VMEM((batch, part), BF16), pltpu.VMEM((nrow * rows, part), BF16)],
    )
    returned = {k: along_row(partial[k], k) if k else partial[0] for k in order}

    near, far = came[1], came[middle]
    stack, keys, k, spans, got, got_keys = [student, far], [0, middle], middle // 2, [(0, rows)] * 2, [], []
    while k:
        first = 1 if k == 1 else 0
        sent = pack(stack[first:], spans[first:])
        got.append(along_row(sent, k))
        got_keys += [n ^ k for n in keys[first:]]
        stack, spans, keys = stack + got[-1:], spans + [(0, len(keys) * rows)], keys + [n ^ k for n in keys]
        k //= 2
    rest = pack([far, near] + got, [(0, rows)] * 2 + [(0, g.shape[0]) for g in got], after=[partial[0]])
    raw_keys = [[0], [middle, 1] + got_keys]
    sources = [columns[0], with_columns(rest)]
    raw_refs = [x[c] for c in range(ncol) for x in sources]
    raw_gram, *all_raw = call(
        functools.partial(raw_gram_kernel, nrow, ncol, rows, raw_keys),
        [sds((rows + 8, batch), F32)] + ([sds((batch, half), BF16)] if small else []),
        raw_refs,
        scratch=[] if small else [pltpu.VMEM((batch, half), BF16)],
    )
    message, vectors = call(
        functools.partial(message_kernel, nrow, ncol, order),
        [sds((2 * rows + 16, batch), F32), sds((8, batch), F32)],
        [raw_gram] + [returned[k] for k in order],
    )
    return call(
        functools.partial(final_kernel, nrow, ncol, None if small else raw_keys),
        sds((rows, half), F32),
        [message, other_core(message), vectors, student, scale] + (all_raw if small else raw_refs),
        scratch=([] if small else [pltpu.VMEM((batch, half), BF16)]) + [pltpu.VMEM((batch, half), BF16)],
    )


def solution(mesh):
    spec = P(("groups", "row", "col"), "sub")
    return jax.shard_map(
        shards,
        mesh=mesh,
        in_specs=(spec, spec, P(("groups", "row", "col"))),
        out_specs=spec,
        check_vma=False,
    )
```

```python
import functools

import jax
import jax.numpy as jnp
from jax import lax
from jax.experimental import pallas as pl
from jax.experimental.pallas import tpu as pltpu
from jax.sharding import PartitionSpec as P

F32, BF16 = jnp.float32, jnp.bfloat16
INNER = (((1,), (1,)), ((), ()))
TAIL = 16


def call(body, out_shape, operands, scratch=(), after=()):
    outs = out_shape if isinstance(out_shape, (list, tuple)) else [out_shape]
    moved = sum(x.size * x.dtype.itemsize for x in list(operands) + list(outs))

    def run(*refs):
        body(*refs[: len(operands)], *refs[len(operands) + len(after) :])

    return pl.pallas_call(
        run,
        out_shape=out_shape,
        in_specs=[pl.BlockSpec(memory_space=pltpu.VMEM)] * len(operands) + [pl.BlockSpec(memory_space=pl.ANY)] * len(after),
        out_specs=jax.tree.map(lambda _: pl.BlockSpec(memory_space=pltpu.VMEM), out_shape),
        scratch_shapes=list(scratch),
        cost_estimate=pl.CostEstimate(flops=0, bytes_accessed=0, transcendentals=0),
        compiler_params=pltpu.CompilerParams(vmem_limit_bytes=min(56 << 20, (8 << 20) + 3 * moved)),
    )(*operands, *after)


def column(row):
    shape = (row.shape[1], row.shape[1])
    eye = lax.broadcasted_iota(jnp.int32, shape, 0) == lax.broadcasted_iota(jnp.int32, shape, 1)
    return jnp.sum(jnp.where(eye, row, 0.0), axis=1, keepdims=True)


def tags_of(scales, mass):
    shape = (TAIL, scales.shape[1])
    at = lax.broadcasted_iota(jnp.int32, shape, 0)
    high = mass.astype(BF16).astype(F32)
    return jnp.where(at < 8, scales, jnp.where(at < 12, high, mass - high)).astype(BF16)


def read_tags(tags):
    tags = tags.astype(F32)
    return tags[0:1, :], tags[8:9, 0:1] + tags[12:13, 0:1]


def lane_row(col):
    shape = (col.shape[0], col.shape[0])
    eye = lax.broadcasted_iota(jnp.int32, shape, 0) == lax.broadcasted_iota(jnp.int32, shape, 1)
    return jnp.sum(jnp.where(eye, col, 0.0), axis=0, keepdims=True)


def wide(out, at, piece):
    rows, part = piece.shape
    width = out.shape[1]
    high = rows * part // width
    for n in range(width // part):
        out[at : at + high, n * part : (n + 1) * part] = piece[n * high : (n + 1) * high, :]


def put(held, spot, rows, ref, at):
    width = held.shape[1]
    high = rows * width // ref.shape[1]
    for n in range(ref.shape[1] // width):
        held[pl.ds(spot + n * high, high), :] = ref[at : at + high, n * width : (n + 1) * width]


def cut_kernel(nrow, teach, *outs):
    part = teach.shape[1] // nrow
    z = lax.axis_index("row")
    for k in range(1, nrow):
        at = pl.multiple_of((z ^ k) * part, part)
        outs[k - 1][...] = teach[:, pl.ds(at, part)]


def ride_kernel(stud, piece, out):
    rows = stud.shape[0]
    out[:rows, :] = stud[...]
    wide(out, rows, piece[...])


def own_kernel(nrow, teach, stud, scale, out):
    rows, half = stud.shape
    part = teach.shape[1] // nrow
    ts = teach[...].astype(F32)
    s = scale[...].astype(F32)
    mass = jnp.sum(jnp.square(column(s)) * jnp.sum(ts * ts, axis=1, keepdims=True), keepdims=True)
    tags = tags_of(jnp.concatenate([s, s], axis=1), mass)
    out[:rows, :] = stud[...]
    out[rows : rows + TAIL, :] = jnp.concatenate([tags] * (half // (2 * rows)), axis=1)
    wide(out, rows + TAIL, teach[:, pl.ds(pl.multiple_of(lax.axis_index("row") * part, part), part)])


def take_kernel(rows, ref, out):
    put(out, 0, rows, ref, rows)


def pack_kernel(spans, *refs):
    out, at = refs[-1], 0
    for r, (first, last) in zip(refs[:-1], spans):
        out[at : at + last - first, :] = r[first:last, :]
        at += last - first


def place(nrow, ncol, rows, k, c):
    return pl.multiple_of(((lax.axis_index("row") ^ k) * ncol + c) * rows, rows)


def group_spot(nrow, ncol, rows, k):
    return pl.multiple_of((lax.axis_index("row") ^ k) * ncol * rows, 2 * rows)


def gram_kernel(nrow, ncol, rows, order, *refs):
    count = nrow * ncol
    outs, held, left = refs[count : count + nrow], refs[-2], refs[-1]
    own = order.index(0) * ncol
    for n, k in enumerate(order):
        for c in range(ncol):
            put(held, place(nrow, ncol, rows, k, c), rows, refs[n * ncol + c], 0 if k else rows + TAIL)
    for n, k in enumerate(order):
        left[n * rows : (n + 1) * rows, :] = held[pl.ds(place(nrow, ncol, rows, k, 0), rows), :]
    sub = rows // 2
    at = lax.broadcasted_iota(jnp.int32, (sub, 2 * rows), 0)
    lane = lax.broadcasted_iota(jnp.int32, (sub, 2 * rows), 1)
    note, mass = jnp.zeros((sub, 2 * rows), F32), jnp.zeros((1, 1), F32)
    for c in range(ncol):
        scales, part = read_tags(refs[own + c][rows : rows + TAIL, : 2 * rows])
        turned = jnp.concatenate([scales[:, sub:], scales[:, :sub]], axis=1)
        note = jnp.where(at == 2 * c, scales, jnp.where(at == 2 * c + 1, turned, note))
        mass = mass + part
    high = mass.astype(BF16).astype(F32)
    note = jnp.where(at < sub // 2, note, jnp.where(at < sub * 3 // 4, high, mass - high))
    per = max(1, 2048 * rows * nrow // held.shape[0] // rows // 8)
    for first in range(0, nrow, per):
        last = min(first + per, nrow)
        gram = lax.dot_general(left[first * rows : last * rows, :], held[...], INNER, preferred_element_type=F32)
        for n in range(first, last):
            out = outs[order[n]]
            out[...] = gram[(n - first) * rows : (n - first + 1) * rows, :].astype(out.dtype)
            spot = pl.ds(group_spot(nrow, ncol, rows, order[n]), 2 * rows)
            seen = out[sub:, spot].astype(F32)
            out[sub:, spot] = jnp.where(lane < sub, note, seen).astype(out.dtype)


def assemble(nrow, ncol, rows, keys, refs, held):
    each = len(keys)
    for c in range(ncol):
        for stack, ref in zip(keys, refs[c * each : (c + 1) * each]):
            for n, k in enumerate(stack):
                held[pl.ds(place(nrow, ncol, rows, k, c), rows), :] = ref[n * rows : (n + 1) * rows, :]


def raw_gram_kernel(nrow, ncol, rows, keys, *refs):
    count = len(keys) * ncol
    out, raw = refs[count:]
    assemble(nrow, ncol, rows, keys, refs, raw)
    out[:rows, :] = lax.dot_general(refs[0][:rows, :], raw[...], INNER, preferred_element_type=F32)
    for at in range(0, raw.shape[0], 128):
        squares = jnp.sum(jnp.square(raw[at : at + 128, :].astype(F32)), axis=1, keepdims=True)
        out[rows:, at : at + 128] = jnp.broadcast_to(lane_row(squares), (8, 128))


def message_kernel(nrow, ncol, order, raw_gram, *refs):
    parts, (out, vectors) = [refs[order.index(k)] for k in range(nrow)], refs[-2:]
    rows = parts[0].shape[0]
    sub = rows // 2
    total = parts[0][...].astype(F32)
    for r in parts[1:]:
        total = total + r[...].astype(F32)
    out[:rows, :] = total
    own = pl.ds(group_spot(nrow, ncol, rows, 0), 2 * rows)
    mirror = jnp.transpose(out[:sub, own])[sub : 2 * sub, :]
    out[sub:rows, own] = jnp.concatenate([mirror, out[sub:rows, own][:, sub:]], axis=1)
    mass = jnp.zeros((1, 1), F32)
    for k, part in enumerate(parts):
        note = part[sub:, own].astype(F32)[:, :sub]
        mass = mass + note[sub // 2 : sub // 2 + 1, :1] + note[sub * 3 // 4 : sub * 3 // 4 + 1, :1]
        line = jnp.concatenate([note[n : n + 1, :] for n in range(2 * ncol)], axis=1)
        vectors[:, pl.ds(group_spot(nrow, ncol, rows, k), ncol * rows)] = jnp.broadcast_to(line, (8, ncol * rows))
    out[rows : 2 * rows + 8, :] = raw_gram[...]
    out[2 * rows + 8 :, :] = jnp.broadcast_to(mass, (8, out.shape[1]))


def final_kernel(nrow, ncol, keys, mine, other, vectors, stud, scale, *refs):
    rows = stud.shape[0]
    if keys:
        out, raw, units = refs[-3:]
        assemble(nrow, ncol, rows, keys, refs, raw)
    else:
        raw, out, units = refs
    batch = mine.shape[1]
    squares = mine[2 * rows : 2 * rows + 8, :] + other[2 * rows : 2 * rows + 8, :]
    for at in range(0, batch, 128):
        inverse = 1.0 / jnp.sqrt(column(squares[:1, at : at + 128]))
        units[at : at + 128, :] = (raw[at : at + 128, :].astype(F32) * inverse).astype(BF16)
    at = pl.ds(group_spot(nrow, ncol, rows, 0), 2 * rows)
    own = (mine[2 * rows : 2 * rows + 8, at] + other[2 * rows : 2 * rows + 8, at])[:1, :rows]
    inverse = 1.0 / jnp.sqrt(column(own))
    mass = (mine[2 * rows + 8 : 2 * rows + 9, :1] + other[2 * rows + 8 : 2 * rows + 9, :1]) / batch
    gram = (mine[rows : 2 * rows, :] + other[rows : 2 * rows, :]) * (inverse * (1.0 / jnp.sqrt(squares[:1, :])))
    outer = (column(scale[...].astype(F32)) / mass) * vectors[:1, :]
    error_b = (gram - outer * (mine[:rows, :] + other[:rows, :])).astype(BF16)
    grads = 4.0 * jnp.dot(error_b, units[...], preferred_element_type=F32)
    along = 4.0 * jnp.sum(error_b.astype(F32) * gram, axis=1, keepdims=True)
    unit = stud[...].astype(F32) * inverse
    out[...] = (grads - along * unit) * inverse


def shards(student, teacher, scale):
    rows, half = student.shape
    nrow, ncol = lax.axis_size("row"), lax.axis_size("col")
    batch = rows * nrow * ncol
    part = teacher.shape[1] // nrow
    small = batch <= 2048
    sds = jax.ShapeDtypeStruct
    scale = scale.reshape(1, rows)

    def along_row(x, k):
        return lax.ppermute(x, "row", [(i, i ^ k) for i in range(nrow)])

    def along_col(x, c):
        return lax.ppermute(x, "col", [(i, (i - c) % ncol) for i in range(ncol)])

    def other_core(x):
        return lax.ppermute(x, "sub", [(0, 1), (1, 0)])

    def pack(xs, spans, after=()):
        shape = (sum(last - first for first, last in spans), half)
        return call(functools.partial(pack_kernel, spans), sds(shape, BF16), xs, after=after)

    def with_columns(x):
        return [x if c == 0 else along_col(x, c) for c in range(ncol)]

    middle, high = nrow // 2, rows * part // half
    order = list(range(middle, nrow)) + list(range(middle))
    riders = (1,)
    cuts = call(functools.partial(cut_kernel, nrow), [sds((rows, part), BF16)] * (nrow - 1), [teacher])
    came = {}
    for k in order:
        if k:
            leaving = cuts[k - 1]
            if k in riders:
                leaving = call(ride_kernel, sds((rows + high, half), BF16), [student, leaving])
            came[k] = along_row(leaving, k)
    own = call(
        functools.partial(own_kernel, nrow),
        sds((rows + TAIL + high, half), BF16),
        [teacher, student, scale],
        after=[came[n] for n in (nrow - 1,)],
    )
    columns, taken = {0: with_columns(own)}, ()
    for k in order:
        piece = came.get(k)
        if k in riders:
            piece = call(functools.partial(take_kernel, rows), sds((rows, part), BF16), [piece], after=taken)
            taken = (piece,)
        if k:
            columns[k] = with_columns(piece)
    partial = call(
        functools.partial(gram_kernel, nrow, ncol, rows, order),
        [sds((rows, batch), BF16 if k else F32) for k in range(nrow)],
        [columns[k][c] for k in order for c in range(ncol)],
        scratch=[pltpu.VMEM((batch, part), BF16), pltpu.VMEM((nrow * rows, part), BF16)],
    )
    returned = {k: along_row(partial[k], k) if k else partial[0] for k in order}

    stack, spans, keys, k = [student, came[1]], [(0, rows)] * 2, [0, 1], 2
    while k < nrow:
        sent = pack(stack, spans, after=[came[n] for n in (middle, nrow - 1)] if k == 2 else ())
        stack, spans = stack + [along_row(sent, k)], spans + [(0, len(keys) * rows)]
        keys, k = keys + [n ^ k for n in keys], 2 * k
    rest = pack(stack[1:], spans[1:], after=[partial[0]])
    raw_keys = [[0], keys[1:]]
    sources = [columns[0], with_columns(rest)]
    raw_refs = [x[c] for c in range(ncol) for x in sources]
    raw_gram, *all_raw = call(
        functools.partial(raw_gram_kernel, nrow, ncol, rows, raw_keys),
        [sds((rows + 8, batch), F32)] + ([sds((batch, half), BF16)] if small else []),
        raw_refs,
        scratch=[] if small else [pltpu.VMEM((batch, half), BF16)],
    )
    message, vectors = call(
        functools.partial(message_kernel, nrow, ncol, order),
        [sds((2 * rows + 16, batch), F32), sds((8, batch), F32)],
        [raw_gram] + [returned[k] for k in order],
    )
    return call(
        functools.partial(final_kernel, nrow, ncol, None if small else raw_keys),
        sds((rows, half), F32),
        [message, other_core(message), vectors, student, scale] + (all_raw if small else raw_refs),
        scratch=([] if small else [pltpu.VMEM((batch, half), BF16)]) + [pltpu.VMEM((batch, half), BF16)],
    )


def solution(mesh):
    spec = P(("groups", "row", "col"), "sub")
    return jax.shard_map(
        shards,
        mesh=mesh,
        in_specs=(spec, spec, P(("groups", "row", "col"))),
        out_specs=spec,
        check_vma=False,
    )
```

```python
import functools

import jax
import jax.numpy as jnp
from jax import lax
from jax.experimental import pallas as pl
from jax.experimental.pallas import tpu as pltpu
from jax.sharding import PartitionSpec as P

F32, BF16 = jnp.float32, jnp.bfloat16
INNER = (((1,), (1,)), ((), ()))
TAIL = 16


def call(body, out_shape, operands, scratch=(), after=()):
    outs = out_shape if isinstance(out_shape, (list, tuple)) else [out_shape]
    moved = sum(x.size * x.dtype.itemsize for x in list(operands) + list(outs))

    def run(*refs):
        body(*refs[: len(operands)], *refs[len(operands) + len(after) :])

    return pl.pallas_call(
        run,
        out_shape=out_shape,
        in_specs=[pl.BlockSpec(memory_space=pltpu.VMEM)] * len(operands) + [pl.BlockSpec(memory_space=pl.ANY)] * len(after),
        out_specs=jax.tree.map(lambda _: pl.BlockSpec(memory_space=pltpu.VMEM), out_shape),
        scratch_shapes=list(scratch),
        cost_estimate=pl.CostEstimate(flops=0, bytes_accessed=0, transcendentals=0),
        compiler_params=pltpu.CompilerParams(vmem_limit_bytes=min(56 << 20, (8 << 20) + 3 * moved)),
    )(*operands, *after)


def column(row):
    shape = (row.shape[1], row.shape[1])
    eye = lax.broadcasted_iota(jnp.int32, shape, 0) == lax.broadcasted_iota(jnp.int32, shape, 1)
    return jnp.sum(jnp.where(eye, row, 0.0), axis=1, keepdims=True)


def tags_of(scales, mass):
    shape = (TAIL, scales.shape[1])
    at = lax.broadcasted_iota(jnp.int32, shape, 0)
    high = mass.astype(BF16).astype(F32)
    return jnp.where(at < 8, scales, jnp.where(at < 12, high, mass - high)).astype(BF16)


def read_tags(tags):
    tags = tags.astype(F32)
    return tags[0:1, :], tags[8:9, 0:1] + tags[12:13, 0:1]


def lane_row(col):
    shape = (col.shape[0], col.shape[0])
    eye = lax.broadcasted_iota(jnp.int32, shape, 0) == lax.broadcasted_iota(jnp.int32, shape, 1)
    return jnp.sum(jnp.where(eye, col, 0.0), axis=0, keepdims=True)


def wide(out, at, piece):
    rows, part = piece.shape
    width = out.shape[1]
    high = rows * part // width
    for n in range(width // part):
        out[at : at + high, n * part : (n + 1) * part] = piece[n * high : (n + 1) * high, :]


def put(held, spot, rows, ref, at):
    width = held.shape[1]
    high = rows * width // ref.shape[1]
    for n in range(ref.shape[1] // width):
        held[pl.ds(spot + n * high, high), :] = ref[at : at + high, n * width : (n + 1) * width]


def cut_kernel(nrow, teach, *outs):
    part = teach.shape[1] // nrow
    z = lax.axis_index("row")
    for k in range(nrow):
        at = pl.multiple_of((z ^ k) * part, part)
        outs[k][...] = teach[:, pl.ds(at, part)]


def ride_kernel(stud, piece, out):
    rows = stud.shape[0]
    out[:rows, :] = stud[...]
    wide(out, rows, piece[...])


def tag_kernel(teach, scale, out):
    rows, width = teach.shape[0], out.shape[1]
    ts = teach[...].astype(F32)
    s = scale[...].astype(F32)
    mass = jnp.sum(jnp.square(column(s)) * jnp.sum(ts * ts, axis=1, keepdims=True), keepdims=True)
    tags = tags_of(jnp.concatenate([s, s], axis=1), mass)
    out[...] = jnp.concatenate([tags] * (width // (2 * rows)), axis=1)


def late_kernel(order, rows, tags, *refs):
    out = refs[-1]
    for n, (k, ref) in enumerate(zip(order, refs[:-1])):
        put(out, n * rows, rows, ref, rows if k == 1 else 0)
    out[len(order) * rows :, :] = tags[...]


def pack_kernel(spans, *refs):
    out, at = refs[-1], 0
    for r, (first, last) in zip(refs[:-1], spans):
        out[at : at + last - first, :] = r[first:last, :]
        at += last - first


def place(nrow, ncol, rows, k, c):
    return pl.multiple_of(((lax.axis_index("row") ^ k) * ncol + c) * rows, rows)


def group_spot(nrow, ncol, rows, k):
    return pl.multiple_of((lax.axis_index("row") ^ k) * ncol * rows, 2 * rows)


def gram_kernel(nrow, ncol, rows, order, *refs):
    outs, held, left = refs[2 * ncol : 2 * ncol + nrow], refs[-2], refs[-1]
    for c in range(ncol):
        put(held, place(nrow, ncol, rows, 0, c), rows, refs[2 * c], 0)
        for n, k in enumerate([k for k in order if k]):
            put(held, place(nrow, ncol, rows, k, c), rows, refs[2 * c + 1], n * rows)
    for n, k in enumerate(order):
        left[n * rows : (n + 1) * rows, :] = held[pl.ds(place(nrow, ncol, rows, k, 0), rows), :]
    sub = rows // 2
    at = lax.broadcasted_iota(jnp.int32, (sub, 2 * rows), 0)
    lane = lax.broadcasted_iota(jnp.int32, (sub, 2 * rows), 1)
    note, mass = jnp.zeros((sub, 2 * rows), F32), jnp.zeros((1, 1), F32)
    for c in range(ncol):
        scales, part = read_tags(refs[2 * c + 1][(nrow - 1) * rows :, : 2 * rows])
        turned = jnp.concatenate([scales[:, sub:], scales[:, :sub]], axis=1)
        note = jnp.where(at == 2 * c, scales, jnp.where(at == 2 * c + 1, turned, note))
        mass = mass + part
    high = mass.astype(BF16).astype(F32)
    note = jnp.where(at < sub // 2, note, jnp.where(at < sub * 3 // 4, high, mass - high))
    per = max(1, 2048 * rows * nrow // held.shape[0] // rows // 8)
    for first in range(0, nrow, per):
        last = min(first + per, nrow)
        gram = lax.dot_general(left[first * rows : last * rows, :], held[...], INNER, preferred_element_type=F32)
        for n in range(first, last):
            out = outs[order[n]]
            out[...] = gram[(n - first) * rows : (n - first + 1) * rows, :].astype(out.dtype)
            spot = pl.ds(group_spot(nrow, ncol, rows, order[n]), 2 * rows)
            seen = out[sub:, spot].astype(F32)
            out[sub:, spot] = jnp.where(lane < sub, note, seen).astype(out.dtype)


def assemble(nrow, ncol, rows, keys, refs, held):
    each = len(keys)
    for c in range(ncol):
        for stack, ref in zip(keys, refs[c * each : (c + 1) * each]):
            for n, k in enumerate(stack):
                held[pl.ds(place(nrow, ncol, rows, k, c), rows), :] = ref[n * rows : (n + 1) * rows, :]


def sum_kernel(nrow, ncol, order, *refs):
    parts, (out, vectors) = [refs[order.index(k)] for k in range(nrow)], refs[-2:]
    rows = parts[0].shape[0]
    sub = rows // 2
    total = parts[0][...].astype(F32)
    for r in parts[1:]:
        total = total + r[...].astype(F32)
    out[...] = total
    own = pl.ds(group_spot(nrow, ncol, rows, 0), 2 * rows)
    mirror = jnp.transpose(out[:sub, own])[sub : 2 * sub, :]
    out[sub:rows, own] = jnp.concatenate([mirror, out[sub:rows, own][:, sub:]], axis=1)
    mass = jnp.zeros((1, 1), F32)
    for k, part in enumerate(parts):
        note = part[sub:, own].astype(F32)[:, :sub]
        mass = mass + note[sub // 2 : sub // 2 + 1, :1] + note[sub * 3 // 4 : sub * 3 // 4 + 1, :1]
        line = jnp.concatenate([note[n : n + 1, :] for n in range(2 * ncol)], axis=1)
        vectors[:8, pl.ds(group_spot(nrow, ncol, rows, k), ncol * rows)] = jnp.broadcast_to(line, (8, ncol * rows))
    vectors[8:, :] = jnp.broadcast_to(mass, (8, out.shape[1]))


def message_kernel(nrow, ncol, keys, total, vectors, *refs):
    out, raw = refs[-2:]
    rows = total.shape[0]
    assemble(nrow, ncol, rows, keys, refs, raw)
    out[:rows, :] = total[...]
    out[rows : 2 * rows, :] = lax.dot_general(refs[0][:rows, :], raw[...], INNER, preferred_element_type=F32)
    for at in range(0, raw.shape[0], 128):
        squares = jnp.sum(jnp.square(raw[at : at + 128, :].astype(F32)), axis=1, keepdims=True)
        out[2 * rows : 2 * rows + 8, at : at + 128] = jnp.broadcast_to(lane_row(squares), (8, 128))
    out[2 * rows + 8 :, :] = vectors[8:, :]


def final_kernel(nrow, ncol, keys, mine, other, vectors, stud, scale, *refs):
    rows = stud.shape[0]
    if keys:
        out, raw, units = refs[-3:]
        assemble(nrow, ncol, rows, keys, refs, raw)
    else:
        raw, out, units = refs
    batch = mine.shape[1]
    squares = mine[2 * rows : 2 * rows + 8, :] + other[2 * rows : 2 * rows + 8, :]
    for at in range(0, batch, 128):
        inverse = 1.0 / jnp.sqrt(column(squares[:1, at : at + 128]))
        units[at : at + 128, :] = (raw[at : at + 128, :].astype(F32) * inverse).astype(BF16)
    at = pl.ds(group_spot(nrow, ncol, rows, 0), 2 * rows)
    own = (mine[2 * rows : 2 * rows + 8, at] + other[2 * rows : 2 * rows + 8, at])[:1, :rows]
    inverse = 1.0 / jnp.sqrt(column(own))
    mass = (mine[2 * rows + 8 : 2 * rows + 9, :1] + other[2 * rows + 8 : 2 * rows + 9, :1]) / batch
    gram = (mine[rows : 2 * rows, :] + other[rows : 2 * rows, :]) * (inverse * (1.0 / jnp.sqrt(squares[:1, :])))
    outer = (column(scale[...].astype(F32)) / mass) * vectors[:1, :]
    error_b = (gram - outer * (mine[:rows, :] + other[:rows, :])).astype(BF16)
    grads = 4.0 * jnp.dot(error_b, units[...], preferred_element_type=F32)
    along = 4.0 * jnp.sum(error_b.astype(F32) * gram, axis=1, keepdims=True)
    unit = stud[...].astype(F32) * inverse
    out[...] = (grads - along * unit) * inverse


def shards(student, teacher, scale):
    rows, half = student.shape
    nrow, ncol = lax.axis_size("row"), lax.axis_size("col")
    batch = rows * nrow * ncol
    part = teacher.shape[1] // nrow
    small = batch <= 2048
    sds = jax.ShapeDtypeStruct
    scale = scale.reshape(1, rows)

    def along_row(x, k):
        return lax.ppermute(x, "row", [(i, i ^ k) for i in range(nrow)])

    def along_col(x, c):
        return lax.ppermute(x, "col", [(i, (i - c) % ncol) for i in range(ncol)])

    def other_core(x):
        return lax.ppermute(x, "sub", [(0, 1), (1, 0)])

    def pack(xs, spans, after=()):
        shape = (sum(last - first for first, last in spans), half)
        return call(functools.partial(pack_kernel, spans), sds(shape, BF16), xs, after=after)

    def with_columns(x):
        return [x if c == 0 else along_col(x, c) for c in range(ncol)]

    middle, high = nrow // 2, rows * part // half
    order = list(range(middle, nrow)) + list(range(middle))
    riders = (1,)
    cuts = call(functools.partial(cut_kernel, nrow), [sds((rows, part), BF16)] * nrow, [teacher])
    came = {}
    for k in order:
        if k:
            leaving = cuts[k]
            if k in riders:
                leaving = call(ride_kernel, sds((rows + high, half), BF16), [student, leaving])
            came[k] = along_row(leaving, k)
    tags = call(tag_kernel, sds((TAIL, part), BF16), [teacher, scale], after=[came[n] for n in ()])
    own = with_columns(cuts[0])
    mine = with_columns(student)
    others = [k for k in order if k]
    late = call(
        functools.partial(late_kernel, others, rows),
        sds(((nrow - 1) * rows + TAIL, part), BF16),
        [tags] + [came[k] for k in others],
        after=own[1:2] + mine[1:2],
    )
    late = with_columns(late)
    partial = call(
        functools.partial(gram_kernel, nrow, ncol, rows, order),
        [sds((rows, batch), BF16 if k else F32) for k in range(nrow)],
        [r for pair in zip(own, late) for r in pair],
        scratch=[pltpu.VMEM((batch, part), BF16), pltpu.VMEM((nrow * rows, part), BF16)],
    )
    returned = {k: along_row(partial[k], k) if k else partial[0] for k in order}

    stack, spans, keys, k = [student, came[1]], [(0, rows)] * 2, [0, 1], 2
    while k < nrow:
        stack.append(along_row(pack(stack, spans), k))
        spans.append((0, len(keys) * rows))
        keys, k = keys + [n ^ k for n in keys], 2 * k
    cut = (len(keys) - 2) // 2 * rows
    near = with_columns(pack(stack[1:2], spans[1:2], after=[partial[0]]))
    rest = pack(stack[2:], spans[2:], after=[partial[0]]) if len(stack) > 3 else stack[2]
    rest = [with_columns(pack([rest], [span], after=[partial[0]])) for span in ((0, cut), (cut, 2 * cut))]
    raw_keys = [[0], [1], keys[2 : 2 + cut // rows], keys[2 + cut // rows :]]
    raw_refs = [x[c] for c in range(ncol) for x in (mine, near, *rest)]
    total, vectors = call(
        functools.partial(sum_kernel, nrow, ncol, order),
        [sds((rows, batch), F32), sds((16, batch), F32)],
        [returned[k] for k in order],
    )
    message, *all_raw = call(
        functools.partial(message_kernel, nrow, ncol, raw_keys),
        [sds((2 * rows + 16, batch), F32)] + ([sds((batch, half), BF16)] if small else []),
        [total, vectors] + raw_refs,
        scratch=[] if small else [pltpu.VMEM((batch, half), BF16)],
    )
    return call(
        functools.partial(final_kernel, nrow, ncol, None if small else raw_keys),
        sds((rows, half), F32),
        [message, other_core(message), vectors, student, scale] + (all_raw if small else raw_refs),
        scratch=([] if small else [pltpu.VMEM((batch, half), BF16)]) + [pltpu.VMEM((batch, half), BF16)],
    )


def solution(mesh):
    spec = P(("groups", "row", "col"), "sub")
    return jax.shard_map(
        shards,
        mesh=mesh,
        in_specs=(spec, spec, P(("groups", "row", "col"))),
        out_specs=spec,
        check_vma=False,
    )
```

```python
import functools

import jax
import jax.numpy as jnp
from jax import lax
from jax.experimental import pallas as pl
from jax.experimental.pallas import tpu as pltpu
from jax.sharding import PartitionSpec as P

F32, BF16 = jnp.float32, jnp.bfloat16
INNER = (((1,), (1,)), ((), ()))


def call(body, out_shape, operands, scratch=(), after=()):
    outs = out_shape if isinstance(out_shape, (list, tuple)) else [out_shape]
    moved = sum(x.size * x.dtype.itemsize for x in list(operands) + list(outs))

    def run(*refs):
        body(*refs[: len(operands)], *refs[len(operands) + len(after) :])

    return pl.pallas_call(
        run,
        out_shape=out_shape,
        in_specs=[pl.BlockSpec(memory_space=pltpu.VMEM)] * len(operands) + [pl.BlockSpec(memory_space=pl.ANY)] * len(after),
        out_specs=jax.tree.map(lambda _: pl.BlockSpec(memory_space=pltpu.VMEM), out_shape),
        scratch_shapes=list(scratch),
        cost_estimate=pl.CostEstimate(flops=0, bytes_accessed=0, transcendentals=0),
        compiler_params=pltpu.CompilerParams(vmem_limit_bytes=min(56 << 20, (8 << 20) + 3 * moved)),
    )(*operands, *after)


def column(row):
    shape = (row.shape[1], row.shape[1])
    eye = lax.broadcasted_iota(jnp.int32, shape, 0) == lax.broadcasted_iota(jnp.int32, shape, 1)
    return jnp.sum(jnp.where(eye, row, 0.0), axis=1, keepdims=True)


def lane_row(col):
    shape = (col.shape[0], col.shape[0])
    eye = lax.broadcasted_iota(jnp.int32, shape, 0) == lax.broadcasted_iota(jnp.int32, shape, 1)
    return jnp.sum(jnp.where(eye, col, 0.0), axis=0, keepdims=True)


def place(nrow, ncol, rows, k, c):
    return pl.multiple_of(((lax.axis_index("row") ^ k) * ncol + c) * rows, rows)


def group(ncol, rows, k):
    at = (lax.axis_index("row") ^ k) * ncol * rows
    return pl.ds(pl.multiple_of(at, 2 * rows), ncol * rows)


def side(k):
    top = k.bit_length() - 1
    return lax.rem(lax.shift_right_logical(lax.axis_index("row"), top), 2)


def cut_kernel(nrow, teach, *outs):
    part = teach.shape[1] // 2
    for k in range(1, nrow):
        at = pl.multiple_of((1 - side(k)) * part, part)
        outs[k - 1][...] = teach[:, pl.ds(at, part)]


def tag_kernel(teach, scale, out):
    ts = teach[...].astype(F32)
    s = scale[...].astype(F32)
    mass = jnp.sum(jnp.square(column(s)) * jnp.sum(ts * ts, axis=1, keepdims=True), keepdims=True)
    at = lax.broadcasted_iota(jnp.int32, out.shape, 0)
    out[...] = jnp.where(at < 4, jnp.concatenate([s, s], axis=1), mass)


def gram_kernel(nrow, ncol, rows, *refs):
    own, tags, pieces = refs[:ncol], refs[ncol : 2 * ncol], refs[2 * ncol : 2 * ncol + nrow - 1]
    local, note, *outs = refs[2 * ncol + nrow - 1 : -1]
    held = refs[-1]
    away, beside = outs[: nrow - 1], outs[nrow - 1 :]
    part = held.shape[1] // 2
    for c in range(ncol):
        held[c * rows : (c + 1) * rows, :] = own[c][...]
    lane = lax.broadcasted_iota(jnp.int32, (8, 2 * rows), 1)
    at = lax.broadcasted_iota(jnp.int32, (8, 2 * rows), 0)
    mass = sum(t[4:5, :1] for t in tags)
    for c in range(0, ncol, 2):
        pair = jnp.where(lane < rows, tags[c][0:1, :], tags[c + 1][0:1, :])
        note[:, c * rows : (c + 2) * rows] = jnp.where(at < 4, pair, mass)
    for k in range(1, nrow):
        piece = pieces[k - 1][...]
        mine = held[:, pl.ds(pl.multiple_of(side(k) * part, part), part)]
        away[k - 1][:rows, :] = lax.dot_general(piece, mine, INNER, preferred_element_type=F32)
        away[k - 1][rows:, :] = note[...]
        here = lax.dot_general(mine, piece, INNER, preferred_element_type=F32)
        for c in range(1, ncol):
            beside[c - 1][:, (k - 1) * rows : k * rows] = here[c * rows : (c + 1) * rows, :]
        local[:, group(ncol, rows, k)] = jnp.concatenate([here[:rows, :], jnp.zeros((rows, (ncol - 1) * rows), F32)], axis=1)
    local[:, group(ncol, rows, 0)] = lax.dot_general(held[:rows, :], held[...], INNER, preferred_element_type=F32)


def sum_kernel(nrow, ncol, rows, local, note, *refs):
    away, beside, (out, vectors) = refs[: nrow - 1], refs[nrow - 1 : -2], refs[-2:]
    mass = note[4:5, :1]
    vectors[:, group(ncol, rows, 0)] = note[...]
    out[:rows, group(ncol, rows, 0)] = local[:, group(ncol, rows, 0)]
    for k in range(1, nrow):
        at = group(ncol, rows, k)
        block = local[:, at] + away[k - 1][:rows, :]
        more = [beside[ncol - c - 1][:, (k - 1) * rows : k * rows] for c in range(1, ncol)]
        out[:rows, at] = block + jnp.concatenate([jnp.zeros((rows, rows), F32)] + more, axis=1)
        vectors[:, at] = away[k - 1][rows:, :]
        mass = mass + away[k - 1][rows + 4 : rows + 5, :1]
    out[rows:, :] = jnp.broadcast_to(mass, (8, out.shape[1]))


def pack_kernel(*refs):
    out, at = refs[-1], 0
    for r in refs[:-1]:
        out[at : at + r.shape[0], :] = r[...]
        at += r.shape[0]


def assemble(nrow, ncol, rows, keys, refs, held):
    for c in range(ncol):
        for n, k in enumerate(keys):
            held[pl.ds(place(nrow, ncol, rows, k, c), rows), :] = refs[c][n * rows : (n + 1) * rows, :]


def raw_gram_kernel(nrow, ncol, rows, keys, *refs):
    out, raw = refs[ncol:]
    assemble(nrow, ncol, rows, keys, refs, raw)
    out[:rows, :] = lax.dot_general(refs[0][:rows, :], raw[...], INNER, preferred_element_type=F32)
    for at in range(0, raw.shape[0], 128):
        squares = jnp.sum(jnp.square(raw[at : at + 128, :].astype(F32)), axis=1, keepdims=True)
        out[rows:, at : at + 128] = jnp.broadcast_to(lane_row(squares), (8, 128))


def normalize(raw, squares, units):
    for at in range(0, raw.shape[0], 128):
        inverse = 1.0 / jnp.sqrt(column(squares[:1, at : at + 128]))
        units[at : at + 128, :] = (raw[at : at + 128, :].astype(F32) * inverse).astype(BF16)


def unit_gram_kernel(ncol, mine, other, *refs):
    rows = mine.shape[0] - 8
    gram, inverses, squares = refs[1:4] if len(refs) > 3 else refs
    squares[...] = mine[rows:, :] + other[rows:, :]
    at = pl.multiple_of(lax.axis_index("row") * ncol * rows, 2 * rows)
    inverse = 1.0 / jnp.sqrt(column(squares[:1, pl.ds(at, 2 * rows)][:, :rows]))
    inverses[...] = jnp.broadcast_to(inverse, inverses.shape)
    gram[...] = (mine[:rows, :] + other[:rows, :]) * (inverse * (1.0 / jnp.sqrt(squares[:1, :])))
    if len(refs) > 3:
        normalize(refs[0], squares, refs[4])


def final_kernel(nrow, ncol, keys, mine, other, vectors, gram, inverses, squares, stud, scale, *refs):
    rows = stud.shape[0]
    if keys:
        out, units = refs[-2:]
        assemble(nrow, ncol, rows, keys, refs, units)
        normalize(units, squares, units)
    else:
        units, out = refs
    inverse = inverses[:, :1]
    mass = (mine[rows : rows + 1, :1] + other[rows : rows + 1, :1]) / mine.shape[1]
    outer = (column(scale[...].astype(F32)) / mass) * vectors[:1, :]
    error_b = (gram[...] - outer * (mine[:rows, :] + other[:rows, :])).astype(BF16)
    grads = 4.0 * jnp.dot(error_b, units[...], preferred_element_type=F32)
    along = 4.0 * jnp.sum(error_b.astype(F32) * gram[...], axis=1, keepdims=True)
    unit = stud[...].astype(F32) * inverse
    out[...] = (grads - along * unit) * inverse


def shards(student, teacher, scale):
    rows, half = student.shape
    nrow, ncol = lax.axis_size("row"), lax.axis_size("col")
    batch, width = rows * nrow * ncol, teacher.shape[1]
    small = batch <= 2048
    sds = jax.ShapeDtypeStruct
    scale = scale.reshape(1, rows)

    def along_row(x, k):
        return lax.ppermute(x, "row", [(i, i ^ k) for i in range(nrow)])

    def along_col(x, c):
        return lax.ppermute(x, "col", [(i, (i - c) % ncol) for i in range(ncol)])

    def other_core(x):
        return lax.ppermute(x, "sub", [(0, 1), (1, 0)])

    def with_columns(x):
        return [x if c == 0 else along_col(x, c) for c in range(ncol)]

    def pack(xs, after=()):
        if len(xs) == 1:
            return xs[0]
        return call(pack_kernel, sds((sum(x.shape[0] for x in xs), half), BF16), xs, after=after)

    cuts = call(functools.partial(cut_kernel, nrow), [sds((rows, width // 2), BF16)] * (nrow - 1), [teacher])
    others = list(range(nrow // 2, nrow)) + list(range(1, nrow // 2))
    came = {k: along_row(cuts[k - 1], k) for k in others}
    own = with_columns(teacher)
    tags = with_columns(call(tag_kernel, sds((8, 2 * rows), F32), [teacher, scale]))

    stack, keys, k = [student], [0], nrow // 2
    while k:
        stack.append(along_row(pack(stack, after=own[1:]), k))
        keys, k = keys + [n ^ k for n in keys], k // 2
    raw_refs = with_columns(pack(stack, after=list(came.values()) + tags[1:] + own[1:]))
    raw_gram, *raw = call(
        functools.partial(raw_gram_kernel, nrow, ncol, rows, keys),
        [sds((rows + 8, batch), F32)] + ([sds((batch, half), BF16)] if small else []),
        raw_refs,
        scratch=[] if small else [pltpu.VMEM((batch, half), BF16)],
    )
    gram, inverses, squares, *units = call(
        functools.partial(unit_gram_kernel, ncol),
        [sds((rows, batch), F32), sds((rows, 128), F32), sds((8, batch), F32)] + ([sds((batch, half), BF16)] if small else []),
        [raw_gram, other_core(raw_gram)] + raw,
    )

    local, note, *outs = call(
        functools.partial(gram_kernel, nrow, ncol, rows),
        [sds((rows, batch), F32), sds((8, ncol * rows), F32)]
        + [sds((rows + 8, ncol * rows), F32)] * (nrow - 1)
        + [sds((rows, (nrow - 1) * rows), F32)] * (ncol - 1),
        own + tags + [came[k] for k in range(1, nrow)],
        scratch=[pltpu.VMEM((ncol * rows, width), BF16)],
    )
    away = {k: along_row(outs[k - 1], k) for k in others}
    beside = [along_col(outs[nrow - 2 + c], -c) for c in range(1, ncol)]
    message, vectors = call(
        functools.partial(sum_kernel, nrow, ncol, rows),
        [sds((rows + 8, batch), F32), sds((8, batch), F32)],
        [local, note] + [away[k] for k in range(1, nrow)] + beside,
    )
    return call(
        functools.partial(final_kernel, nrow, ncol, None if small else keys),
        sds((rows, half), F32),
        [message, other_core(message), vectors, gram, inverses, squares, student, scale] + (units if small else raw_refs),
        scratch=[] if small else [pltpu.VMEM((batch, half), BF16)],
    )


def solution(mesh):
    spec = P(("groups", "row", "col"), "sub")
    return jax.shard_map(
        shards,
        mesh=mesh,
        in_specs=(spec, spec, P(("groups", "row", "col"))),
        out_specs=spec,
        check_vma=False,
    )
```

```python
import functools

import jax
import jax.numpy as jnp
from jax import lax
from jax.experimental import pallas as pl
from jax.experimental.pallas import tpu as pltpu
from jax.sharding import PartitionSpec as P

F32, BF16 = jnp.float32, jnp.bfloat16
INNER = (((1,), (1,)), ((), ()))


def call(body, out_shape, operands, scratch=(), after=()):
    outs = out_shape if isinstance(out_shape, (list, tuple)) else [out_shape]
    moved = sum(x.size * x.dtype.itemsize for x in list(operands) + list(outs))

    def run(*refs):
        body(*refs[: len(operands)], *refs[len(operands) + len(after) :])

    return pl.pallas_call(
        run,
        out_shape=out_shape,
        in_specs=[pl.BlockSpec(memory_space=pltpu.VMEM)] * len(operands) + [pl.BlockSpec(memory_space=pl.ANY)] * len(after),
        out_specs=jax.tree.map(lambda _: pl.BlockSpec(memory_space=pltpu.VMEM), out_shape),
        scratch_shapes=list(scratch),
        cost_estimate=pl.CostEstimate(flops=0, bytes_accessed=0, transcendentals=0),
        compiler_params=pltpu.CompilerParams(vmem_limit_bytes=min(56 << 20, (8 << 20) + 3 * moved)),
    )(*operands, *after)


def column(row):
    shape = (row.shape[1], row.shape[1])
    eye = lax.broadcasted_iota(jnp.int32, shape, 0) == lax.broadcasted_iota(jnp.int32, shape, 1)
    return jnp.sum(jnp.where(eye, row, 0.0), axis=1, keepdims=True)


def lane_row(col):
    shape = (col.shape[0], col.shape[0])
    eye = lax.broadcasted_iota(jnp.int32, shape, 0) == lax.broadcasted_iota(jnp.int32, shape, 1)
    return jnp.sum(jnp.where(eye, col, 0.0), axis=0, keepdims=True)


def place(nrow, ncol, rows, k, c):
    return pl.multiple_of(((lax.axis_index("row") ^ k) * ncol + c) * rows, rows)


def group(ncol, rows, k):
    at = (lax.axis_index("row") ^ k) * ncol * rows
    return pl.ds(pl.multiple_of(at, 2 * rows), ncol * rows)


def side(k):
    top = k.bit_length() - 1
    return lax.rem(lax.shift_right_logical(lax.axis_index("row"), top), 2)


def cut_kernel(nrow, teach, *outs):
    part = teach.shape[1] // 2
    for k in range(1, nrow):
        at = pl.multiple_of((1 - side(k)) * part, part)
        outs[k - 1][...] = teach[:, pl.ds(at, part)]


def tag_kernel(teach, scale, out):
    ts = teach[...].astype(F32)
    s = scale[...].astype(F32)
    mass = jnp.sum(jnp.square(column(s)) * jnp.sum(ts * ts, axis=1, keepdims=True), keepdims=True)
    at = lax.broadcasted_iota(jnp.int32, out.shape, 0)
    out[...] = jnp.where(at < 4, jnp.concatenate([s, s], axis=1), mass)


def gram_kernel(nrow, ncol, rows, *refs):
    own, tags, pieces = refs[:ncol], refs[ncol : 2 * ncol], refs[2 * ncol : 2 * ncol + nrow - 1]
    local, note, *outs = refs[2 * ncol + nrow - 1 : -1]
    held = refs[-1]
    away, beside = outs[: nrow - 1], outs[nrow - 1 :]
    part = held.shape[1] // 2
    for c in range(ncol):
        held[c * rows : (c + 1) * rows, :] = own[c][...]
    lane = lax.broadcasted_iota(jnp.int32, (8, 2 * rows), 1)
    at = lax.broadcasted_iota(jnp.int32, (8, 2 * rows), 0)
    mass = sum(t[4:5, :1] for t in tags)
    for c in range(0, ncol, 2):
        pair = jnp.where(lane < rows, tags[c][0:1, :], tags[c + 1][0:1, :])
        note[:, c * rows : (c + 2) * rows] = jnp.where(at < 4, pair, mass)
    for k in range(1, nrow):
        piece = pieces[k - 1][...]
        mine = held[:, pl.ds(pl.multiple_of(side(k) * part, part), part)]
        away[k - 1][:rows, :] = lax.dot_general(piece, mine, INNER, preferred_element_type=F32)
        away[k - 1][rows:, :] = note[...]
        here = lax.dot_general(mine, piece, INNER, preferred_element_type=F32)
        for c in range(1, ncol):
            beside[c - 1][:, (k - 1) * rows : k * rows] = here[c * rows : (c + 1) * rows, :]
        local[:, group(ncol, rows, k)] = jnp.concatenate([here[:rows, :], jnp.zeros((rows, (ncol - 1) * rows), F32)], axis=1)
    local[:, group(ncol, rows, 0)] = lax.dot_general(held[:rows, :], held[...], INNER, preferred_element_type=F32)


def sum_kernel(nrow, ncol, rows, local, note, *refs):
    away, beside, (out, vectors) = refs[: nrow - 1], refs[nrow - 1 : -2], refs[-2:]
    mass = note[4:5, :1]
    vectors[:, group(ncol, rows, 0)] = note[...]
    out[:rows, group(ncol, rows, 0)] = local[:, group(ncol, rows, 0)]
    for k in range(1, nrow):
        at = group(ncol, rows, k)
        block = local[:, at] + away[k - 1][:rows, :]
        more = [beside[ncol - c - 1][:, (k - 1) * rows : k * rows] for c in range(1, ncol)]
        out[:rows, at] = block + jnp.concatenate([jnp.zeros((rows, rows), F32)] + more, axis=1)
        vectors[:, at] = away[k - 1][rows:, :]
        mass = mass + away[k - 1][rows + 4 : rows + 5, :1]
    out[rows:, :] = jnp.broadcast_to(mass, (8, out.shape[1]))


def pack_kernel(*refs):
    out, at = refs[-1], 0
    for r in refs[:-1]:
        out[at : at + r.shape[0], :] = r[...]
        at += r.shape[0]


def assemble(nrow, ncol, rows, keys, refs, held):
    half = nrow // 2
    for c in range(ncol):
        for n, k in enumerate(keys):
            ref, at = refs[2 * c + n // half], n % half * rows
            held[pl.ds(place(nrow, ncol, rows, k, c), rows), :] = ref[at : at + rows, :]


def raw_gram_kernel(nrow, ncol, rows, keys, *refs):
    out, raw = refs[2 * ncol :]
    assemble(nrow, ncol, rows, keys, refs, raw)
    out[:rows, :] = lax.dot_general(refs[0][:rows, :], raw[...], INNER, preferred_element_type=F32)
    for at in range(0, raw.shape[0], 128):
        squares = jnp.sum(jnp.square(raw[at : at + 128, :].astype(F32)), axis=1, keepdims=True)
        out[rows:, at : at + 128] = jnp.broadcast_to(lane_row(squares), (8, 128))


def normalize(raw, squares, units):
    for at in range(0, raw.shape[0], 128):
        inverse = 1.0 / jnp.sqrt(column(squares[:1, at : at + 128]))
        units[at : at + 128, :] = (raw[at : at + 128, :].astype(F32) * inverse).astype(BF16)


def unit_gram_kernel(ncol, mine, other, *refs):
    rows = mine.shape[0] - 8
    gram, inverses, squares = refs[1:4] if len(refs) > 3 else refs
    squares[...] = mine[rows:, :] + other[rows:, :]
    at = pl.multiple_of(lax.axis_index("row") * ncol * rows, 2 * rows)
    inverse = 1.0 / jnp.sqrt(column(squares[:1, pl.ds(at, 2 * rows)][:, :rows]))
    inverses[...] = jnp.broadcast_to(inverse, inverses.shape)
    gram[...] = (mine[:rows, :] + other[:rows, :]) * (inverse * (1.0 / jnp.sqrt(squares[:1, :])))
    if len(refs) > 3:
        normalize(refs[0], squares, refs[4])


def final_kernel(nrow, ncol, keys, mine, other, vectors, gram, inverses, squares, stud, scale, *refs):
    rows = stud.shape[0]
    if keys:
        out, units = refs[-2:]
        assemble(nrow, ncol, rows, keys, refs, units)
        normalize(units, squares, units)
    else:
        units, out = refs
    inverse = inverses[:, :1]
    mass = (mine[rows : rows + 1, :1] + other[rows : rows + 1, :1]) / mine.shape[1]
    outer = (column(scale[...].astype(F32)) / mass) * vectors[:1, :]
    error_b = (gram[...] - outer * (mine[:rows, :] + other[:rows, :])).astype(BF16)
    grads = 4.0 * jnp.dot(error_b, units[...], preferred_element_type=F32)
    along = 4.0 * jnp.sum(error_b.astype(F32) * gram[...], axis=1, keepdims=True)
    unit = stud[...].astype(F32) * inverse
    out[...] = (grads - along * unit) * inverse


def shards(student, teacher, scale):
    rows, half = student.shape
    nrow, ncol = lax.axis_size("row"), lax.axis_size("col")
    batch, width = rows * nrow * ncol, teacher.shape[1]
    small = batch <= 2048
    sds = jax.ShapeDtypeStruct
    scale = scale.reshape(1, rows)

    def along_row(x, k):
        return lax.ppermute(x, "row", [(i, i ^ k) for i in range(nrow)])

    def along_col(x, c):
        return lax.ppermute(x, "col", [(i, (i - c) % ncol) for i in range(ncol)])

    def other_core(x):
        return lax.ppermute(x, "sub", [(0, 1), (1, 0)])

    def with_columns(x):
        return [x if c == 0 else along_col(x, c) for c in range(ncol)]

    def pack(xs, after=()):
        if len(xs) == 1:
            return xs[0]
        return call(pack_kernel, sds((sum(x.shape[0] for x in xs), half), BF16), xs, after=after)

    cuts = call(functools.partial(cut_kernel, nrow), [sds((rows, width // 2), BF16)] * (nrow - 1), [teacher])
    others = list(range(nrow // 2, nrow)) + list(range(1, nrow // 2))
    came = {k: along_row(cuts[k - 1], k) for k in others}
    own = with_columns(teacher)
    tags = with_columns(call(tag_kernel, sds((8, 2 * rows), F32), [teacher, scale]))

    stack, keys, k = [student], [0], nrow // 2
    while k:
        joined = pack(stack, after=())
        sent = joined
        if k == 1:
            first = with_columns(joined)
            sent = call(pack_kernel, sds(joined.shape, BF16), [joined], after=first[1:] + [came[nrow - 1]])
        stack.append(along_row(sent, k))
        keys, k = keys + [n ^ k for n in keys], k // 2
    second = with_columns(call(pack_kernel, sds(joined.shape, BF16), stack[-1:], after=list(came.values()) + tags[1:]))
    raw_refs = [r for pair in zip(first, second) for r in pair]
    raw_gram, *raw = call(
        functools.partial(raw_gram_kernel, nrow, ncol, rows, keys),
        [sds((rows + 8, batch), F32)] + ([sds((batch, half), BF16)] if small else []),
        raw_refs,
        scratch=[] if small else [pltpu.VMEM((batch, half), BF16)],
    )
    gram, inverses, squares, *units = call(
        functools.partial(unit_gram_kernel, ncol),
        [sds((rows, batch), F32), sds((rows, 128), F32), sds((8, batch), F32)] + ([sds((batch, half), BF16)] if small else []),
        [raw_gram, other_core(raw_gram)] + raw,
    )

    local, note, *outs = call(
        functools.partial(gram_kernel, nrow, ncol, rows),
        [sds((rows, batch), F32), sds((8, ncol * rows), F32)]
        + [sds((rows + 8, ncol * rows), F32)] * (nrow - 1)
        + [sds((rows, (nrow - 1) * rows), F32)] * (ncol - 1),
        own + tags + [came[k] for k in range(1, nrow)],
        scratch=[pltpu.VMEM((ncol * rows, width), BF16)],
    )
    away = {k: along_row(outs[k - 1], k) for k in others}
    beside = [along_col(outs[nrow - 2 + c], -c) for c in range(1, ncol)]
    message, vectors = call(
        functools.partial(sum_kernel, nrow, ncol, rows),
        [sds((rows + 8, batch), F32), sds((8, batch), F32)],
        [local, note] + [away[k] for k in range(1, nrow)] + beside,
    )
    return call(
        functools.partial(final_kernel, nrow, ncol, None if small else keys),
        sds((rows, half), F32),
        [message, other_core(message), vectors, gram, inverses, squares, student, scale] + (units if small else raw_refs),
        scratch=[] if small else [pltpu.VMEM((batch, half), BF16)],
    )


def solution(mesh):
    spec = P(("groups", "row", "col"), "sub")
    return jax.shard_map(
        shards,
        mesh=mesh,
        in_specs=(spec, spec, P(("groups", "row", "col"))),
        out_specs=spec,
        check_vma=False,
    )
```

```python
import functools

import jax
import jax.numpy as jnp
from jax import lax
from jax.experimental import pallas as pl
from jax.experimental.pallas import tpu as pltpu
from jax.sharding import PartitionSpec as P

F32, BF16 = jnp.float32, jnp.bfloat16
INNER = (((1,), (1,)), ((), ()))
TAIL = 16


def call(body, out_shape, operands, scratch=(), after=()):
    outs = out_shape if isinstance(out_shape, (list, tuple)) else [out_shape]
    moved = sum(x.size * x.dtype.itemsize for x in list(operands) + list(outs))

    def run(*refs):
        body(*refs[: len(operands)], *refs[len(operands) + len(after) :])

    return pl.pallas_call(
        run,
        out_shape=out_shape,
        in_specs=[pl.BlockSpec(memory_space=pltpu.VMEM)] * len(operands) + [pl.BlockSpec(memory_space=pl.ANY)] * len(after),
        out_specs=jax.tree.map(lambda _: pl.BlockSpec(memory_space=pltpu.VMEM), out_shape),
        scratch_shapes=list(scratch),
        cost_estimate=pl.CostEstimate(flops=0, bytes_accessed=0, transcendentals=0),
        compiler_params=pltpu.CompilerParams(vmem_limit_bytes=min(56 << 20, (8 << 20) + 3 * moved)),
    )(*operands, *after)


def column(row):
    shape = (row.shape[1], row.shape[1])
    eye = lax.broadcasted_iota(jnp.int32, shape, 0) == lax.broadcasted_iota(jnp.int32, shape, 1)
    return jnp.sum(jnp.where(eye, row, 0.0), axis=1, keepdims=True)


def tags_of(scales, mass):
    shape = (TAIL, scales.shape[1])
    at = lax.broadcasted_iota(jnp.int32, shape, 0)
    high = mass.astype(BF16).astype(F32)
    return jnp.where(at < 8, scales, jnp.where(at < 12, high, mass - high)).astype(BF16)


def read_tags(tags):
    tags = tags.astype(F32)
    return tags[0:1, :], tags[8:9, 0:1] + tags[12:13, 0:1]


def lane_row(col):
    shape = (col.shape[0], col.shape[0])
    eye = lax.broadcasted_iota(jnp.int32, shape, 0) == lax.broadcasted_iota(jnp.int32, shape, 1)
    return jnp.sum(jnp.where(eye, col, 0.0), axis=0, keepdims=True)


def put(held, spot, rows, ref, at):
    width = held.shape[1]
    high = rows * width // ref.shape[1]
    for n in range(ref.shape[1] // width):
        held[pl.ds(spot + n * high, high), :] = ref[at : at + high, n * width : (n + 1) * width]


def cut_kernel(nrow, teach, *outs):
    part = teach.shape[1] // nrow
    z = lax.axis_index("row")
    for k in range(nrow):
        at = pl.multiple_of((z ^ k) * part, part)
        outs[k][...] = teach[:, pl.ds(at, part)]


def tag_kernel(teach, scale, out):
    rows, width = teach.shape[0], out.shape[1]
    ts = teach[...].astype(F32)
    s = scale[...].astype(F32)
    mass = jnp.sum(jnp.square(column(s)) * jnp.sum(ts * ts, axis=1, keepdims=True), keepdims=True)
    tags = tags_of(jnp.concatenate([s, s], axis=1), mass)
    out[...] = jnp.concatenate([tags] * (width // (2 * rows)), axis=1)


def late_kernel(rows, tags, *refs):
    out = refs[-1]
    for n, ref in enumerate(refs[:-1]):
        put(out, n * rows, rows, ref, 0)
    out[(len(refs) - 1) * rows :, :] = tags[...]


def pack_kernel(*refs):
    out, at = refs[-1], 0
    for r in refs[:-1]:
        out[at : at + r.shape[0], :] = r[...]
        at += r.shape[0]


def place(nrow, ncol, rows, k, c):
    return pl.multiple_of(((lax.axis_index("row") ^ k) * ncol + c) * rows, rows)


def group(ncol, rows, k):
    at = (lax.axis_index("row") ^ k) * ncol * rows
    return pl.ds(pl.multiple_of(at, 2 * rows), ncol * rows)


def gram_kernel(nrow, ncol, rows, order, *refs):
    outs, held, left = refs[2 * ncol : 2 * ncol + nrow], refs[-2], refs[-1]
    for c in range(ncol):
        put(held, place(nrow, ncol, rows, 0, c), rows, refs[2 * c], 0)
        for n, k in enumerate([k for k in order if k]):
            put(held, place(nrow, ncol, rows, k, c), rows, refs[2 * c + 1], n * rows)
    for n, k in enumerate(order):
        left[n * rows : (n + 1) * rows, :] = held[pl.ds(place(nrow, ncol, rows, k, 0), rows), :]
    sub = rows // 2
    at = lax.broadcasted_iota(jnp.int32, (sub, 2 * rows), 0)
    lane = lax.broadcasted_iota(jnp.int32, (sub, 2 * rows), 1)
    note, mass = jnp.zeros((sub, 2 * rows), F32), jnp.zeros((1, 1), F32)
    for c in range(ncol):
        scales, part = read_tags(refs[2 * c + 1][(nrow - 1) * rows :, : 2 * rows])
        turned = jnp.concatenate([scales[:, sub:], scales[:, :sub]], axis=1)
        note = jnp.where(at == 2 * c, scales, jnp.where(at == 2 * c + 1, turned, note))
        mass = mass + part
    high = mass.astype(BF16).astype(F32)
    note = jnp.where(at < sub // 2, note, jnp.where(at < sub * 3 // 4, high, mass - high))
    per = max(1, 2048 * rows * nrow // held.shape[0] // rows // 8)
    for first in range(0, nrow, per):
        last = min(first + per, nrow)
        gram = lax.dot_general(left[first * rows : last * rows, :], held[...], INNER, preferred_element_type=F32)
        for n in range(first, last):
            out = outs[order[n]]
            out[...] = gram[(n - first) * rows : (n - first + 1) * rows, :].astype(out.dtype)
            spot = pl.ds(pl.multiple_of(place(nrow, ncol, rows, order[n], 0), 2 * rows), 2 * rows)
            seen = out[sub:, spot].astype(F32)
            out[sub:, spot] = jnp.where(lane < sub, note, seen).astype(out.dtype)


def sum_kernel(nrow, ncol, order, *refs):
    parts, (out, vectors) = [refs[order.index(k)] for k in range(nrow)], refs[-2:]
    rows = parts[0].shape[0]
    sub = rows // 2
    total = parts[0][...].astype(F32)
    for r in parts[1:]:
        total = total + r[...].astype(F32)
    out[:rows, :] = total
    own = group(ncol, rows, 0)
    mirror = jnp.transpose(out[:sub, own])[sub : 2 * sub, :]
    out[sub:rows, own] = jnp.concatenate([mirror, out[sub:rows, own][:, sub:]], axis=1)
    mass = jnp.zeros((1, 1), F32)
    for k, part in enumerate(parts):
        note = part[sub:, own].astype(F32)[:, :sub]
        mass = mass + note[sub // 2 : sub // 2 + 1, :1] + note[sub * 3 // 4 : sub * 3 // 4 + 1, :1]
        line = jnp.concatenate([note[n : n + 1, :] for n in range(2 * ncol)], axis=1)
        vectors[:, group(ncol, rows, k)] = jnp.broadcast_to(line, (8, ncol * rows))
    out[rows:, :] = jnp.broadcast_to(mass, (8, out.shape[1]))


def assemble(nrow, ncol, rows, keys, refs, held):
    for c in range(ncol):
        for n, k in enumerate(keys):
            held[pl.ds(place(nrow, ncol, rows, k, c), rows), :] = refs[c][n * rows : (n + 1) * rows, :]


def raw_gram_kernel(nrow, ncol, rows, keys, *refs):
    out, raw = refs[ncol:]
    assemble(nrow, ncol, rows, keys, refs, raw)
    out[:rows, :] = lax.dot_general(refs[0][:rows, :], raw[...], INNER, preferred_element_type=F32)
    for at in range(0, raw.shape[0], 128):
        squares = jnp.sum(jnp.square(raw[at : at + 128, :].astype(F32)), axis=1, keepdims=True)
        out[rows:, at : at + 128] = jnp.broadcast_to(lane_row(squares), (8, 128))


def normalize(raw, squares, units):
    for at in range(0, raw.shape[0], 128):
        inverse = 1.0 / jnp.sqrt(column(squares[:1, at : at + 128]))
        units[at : at + 128, :] = (raw[at : at + 128, :].astype(F32) * inverse).astype(BF16)


def unit_gram_kernel(ncol, mine, other, *refs):
    rows = mine.shape[0] - 8
    gram, inverses, squares = refs[1:4] if len(refs) > 3 else refs
    squares[...] = mine[rows:, :] + other[rows:, :]
    at = pl.multiple_of(lax.axis_index("row") * ncol * rows, 2 * rows)
    inverse = 1.0 / jnp.sqrt(column(squares[:1, pl.ds(at, 2 * rows)][:, :rows]))
    inverses[...] = jnp.broadcast_to(inverse, inverses.shape)
    gram[...] = (mine[:rows, :] + other[:rows, :]) * (inverse * (1.0 / jnp.sqrt(squares[:1, :])))
    if len(refs) > 3:
        normalize(refs[0], squares, refs[4])


def final_kernel(nrow, ncol, keys, mine, other, vectors, gram, inverses, squares, stud, scale, *refs):
    rows = stud.shape[0]
    if keys:
        out, units = refs[-2:]
        assemble(nrow, ncol, rows, keys, refs, units)
        normalize(units, squares, units)
    else:
        units, out = refs
    inverse = inverses[:, :1]
    mass = (mine[rows : rows + 1, :1] + other[rows : rows + 1, :1]) / mine.shape[1]
    outer = (column(scale[...].astype(F32)) / mass) * vectors[:1, :]
    error_b = (gram[...] - outer * (mine[:rows, :] + other[:rows, :])).astype(BF16)
    grads = 4.0 * jnp.dot(error_b, units[...], preferred_element_type=F32)
    along = 4.0 * jnp.sum(error_b.astype(F32) * gram[...], axis=1, keepdims=True)
    unit = stud[...].astype(F32) * inverse
    out[...] = (grads - along * unit) * inverse


def shards(student, teacher, scale):
    rows, half = student.shape
    nrow, ncol = lax.axis_size("row"), lax.axis_size("col")
    batch = rows * nrow * ncol
    part = teacher.shape[1] // nrow
    small = batch <= 2048
    sds = jax.ShapeDtypeStruct
    scale = scale.reshape(1, rows)

    def along_row(x, k):
        return lax.ppermute(x, "row", [(i, i ^ k) for i in range(nrow)])

    def along_col(x, c):
        return lax.ppermute(x, "col", [(i, (i - c) % ncol) for i in range(ncol)])

    def other_core(x):
        return lax.ppermute(x, "sub", [(0, 1), (1, 0)])

    def pack(xs, after=()):
        shape = (sum(x.shape[0] for x in xs), half)
        return call(pack_kernel, sds(shape, BF16), xs, after=after)

    def with_columns(x):
        return [x if c == 0 else along_col(x, c) for c in range(ncol)]

    middle = nrow // 2
    order = list(range(middle, nrow)) + list(range(middle))
    cuts = call(functools.partial(cut_kernel, nrow), [sds((rows, part), BF16)] * nrow, [teacher])
    came = {k: along_row(cuts[k], k) for k in order if k}
    swapped = along_row(student, middle)
    tags = call(tag_kernel, sds((TAIL, part), BF16), [teacher, scale], after=[came[n] for n in ()])
    own = with_columns(cuts[0])
    others = [k for k in order if k]
    late = call(
        functools.partial(late_kernel, rows),
        sds(((nrow - 1) * rows + TAIL, part), BF16),
        [tags] + [came[k] for k in others],
        after=own[1:2] + [swapped],
    )
    late = with_columns(late)
    partial = call(
        functools.partial(gram_kernel, nrow, ncol, rows, order),
        [sds((rows, batch), BF16 if k else F32) for k in range(nrow)],
        [r for pair in zip(own, late) for r in pair],
        scratch=[pltpu.VMEM((batch, part), BF16), pltpu.VMEM((nrow * rows, part), BF16)],
    )
    returned = {k: along_row(partial[k], k) if k else partial[0] for k in order}

    stack, keys, k = [student], [0], middle
    while k:
        joined = pack(stack, after=late[:1] if k == 1 else ()) if k < middle else student
        stack.append(swapped if k == middle else along_row(joined, k))
        keys, k = keys + [n ^ k for n in keys], k // 2
    raw_refs = with_columns(pack(stack, after=[partial[0]]))
    raw_gram, *raw = call(
        functools.partial(raw_gram_kernel, nrow, ncol, rows, keys),
        [sds((rows + 8, batch), F32)] + ([sds((batch, half), BF16)] if small else []),
        raw_refs,
        scratch=[] if small else [pltpu.VMEM((batch, half), BF16)],
    )
    gram, inverses, squares, *units = call(
        functools.partial(unit_gram_kernel, ncol),
        [sds((rows, batch), F32), sds((rows, 128), F32), sds((8, batch), F32)] + ([sds((batch, half), BF16)] if small else []),
        [raw_gram, other_core(raw_gram)] + raw,
    )
    message, vectors = call(
        functools.partial(sum_kernel, nrow, ncol, order),
        [sds((rows + 8, batch), F32), sds((8, batch), F32)],
        [returned[k] for k in order],
    )
    return call(
        functools.partial(final_kernel, nrow, ncol, None if small else keys),
        sds((rows, half), F32),
        [message, other_core(message), vectors, gram, inverses, squares, student, scale] + (units if small else raw_refs),
        scratch=[] if small else [pltpu.VMEM((batch, half), BF16)],
    )


def solution(mesh):
    spec = P(("groups", "row", "col"), "sub")
    return jax.shard_map(
        shards,
        mesh=mesh,
        in_specs=(spec, spec, P(("groups", "row", "col"))),
        out_specs=spec,
        check_vma=False,
    )
```

```python
import functools

import jax
import jax.numpy as jnp
from jax import lax
from jax.experimental import pallas as pl
from jax.experimental.pallas import tpu as pltpu
from jax.sharding import PartitionSpec as P

F32, BF16 = jnp.float32, jnp.bfloat16
INNER = (((1,), (1,)), ((), ()))
TAIL = 16


def call(body, out_shape, operands, scratch=(), after=()):
    outs = out_shape if isinstance(out_shape, (list, tuple)) else [out_shape]
    moved = sum(x.size * x.dtype.itemsize for x in list(operands) + list(outs))

    def run(*refs):
        body(*refs[: len(operands)], *refs[len(operands) + len(after) :])

    return pl.pallas_call(
        run,
        out_shape=out_shape,
        in_specs=[pl.BlockSpec(memory_space=pltpu.VMEM)] * len(operands) + [pl.BlockSpec(memory_space=pl.ANY)] * len(after),
        out_specs=jax.tree.map(lambda _: pl.BlockSpec(memory_space=pltpu.VMEM), out_shape),
        scratch_shapes=list(scratch),
        cost_estimate=pl.CostEstimate(flops=0, bytes_accessed=0, transcendentals=0),
        compiler_params=pltpu.CompilerParams(vmem_limit_bytes=min(56 << 20, (8 << 20) + 3 * moved)),
    )(*operands, *after)


def column(row):
    shape = (row.shape[1], row.shape[1])
    eye = lax.broadcasted_iota(jnp.int32, shape, 0) == lax.broadcasted_iota(jnp.int32, shape, 1)
    return jnp.sum(jnp.where(eye, row, 0.0), axis=1, keepdims=True)


def tags_of(scales, mass):
    shape = (TAIL, scales.shape[1])
    at = lax.broadcasted_iota(jnp.int32, shape, 0)
    high = mass.astype(BF16).astype(F32)
    return jnp.where(at < 8, scales, jnp.where(at < 12, high, mass - high)).astype(BF16)


def read_tags(tags):
    tags = tags.astype(F32)
    return tags[0:1, :], tags[8:9, 0:1] + tags[12:13, 0:1]


def lane_row(col):
    shape = (col.shape[0], col.shape[0])
    eye = lax.broadcasted_iota(jnp.int32, shape, 0) == lax.broadcasted_iota(jnp.int32, shape, 1)
    return jnp.sum(jnp.where(eye, col, 0.0), axis=0, keepdims=True)


def put(held, spot, rows, ref, at):
    width = held.shape[1]
    high = rows * width // ref.shape[1]
    for n in range(ref.shape[1] // width):
        held[pl.ds(spot + n * high, high), :] = ref[at : at + high, n * width : (n + 1) * width]


def cut_kernel(nrow, teach, *outs):
    part = teach.shape[1] // nrow
    z = lax.axis_index("row")
    for k in range(nrow):
        at = pl.multiple_of((z ^ k) * part, part)
        outs[k][...] = teach[:, pl.ds(at, part)]


def tag_kernel(teach, scale, cut, out, own):
    own[...] = cut[...]
    rows, width = teach.shape[0], out.shape[1]
    ts = teach[...].astype(F32)
    s = scale[...].astype(F32)
    mass = jnp.sum(jnp.square(column(s)) * jnp.sum(ts * ts, axis=1, keepdims=True), keepdims=True)
    tags = tags_of(jnp.concatenate([s, s], axis=1), mass)
    out[...] = jnp.concatenate([tags] * (width // (2 * rows)), axis=1)


def pack_kernel(*refs):
    out, at = refs[-1], 0
    for r in refs[:-1]:
        out[at : at + r.shape[0], :] = r[...]
        at += r.shape[0]


def place(nrow, ncol, rows, k, c):
    return pl.multiple_of(((lax.axis_index("row") ^ k) * ncol + c) * rows, rows)


def group(ncol, rows, k):
    at = (lax.axis_index("row") ^ k) * ncol * rows
    return pl.ds(pl.multiple_of(at, 2 * rows), ncol * rows)


def gram_kernel(nrow, ncol, rows, order, *refs):
    count = nrow * ncol
    outs, held, left = refs[count : count + nrow], refs[-2], refs[-1]
    for n, k in enumerate(order):
        for c in range(ncol):
            put(held, place(nrow, ncol, rows, k, c), rows, refs[n * ncol + c], 0)
    for n, k in enumerate(order):
        left[n * rows : (n + 1) * rows, :] = held[pl.ds(place(nrow, ncol, rows, k, 0), rows), :]
    sub = rows // 2
    at = lax.broadcasted_iota(jnp.int32, (sub, 2 * rows), 0)
    lane = lax.broadcasted_iota(jnp.int32, (sub, 2 * rows), 1)
    note, mass = jnp.zeros((sub, 2 * rows), F32), jnp.zeros((1, 1), F32)
    for c in range(ncol):
        scales, part = read_tags(refs[order.index(1) * ncol + c][rows:, : 2 * rows])
        turned = jnp.concatenate([scales[:, sub:], scales[:, :sub]], axis=1)
        note = jnp.where(at == 2 * c, scales, jnp.where(at == 2 * c + 1, turned, note))
        mass = mass + part
    high = mass.astype(BF16).astype(F32)
    note = jnp.where(at < sub // 2, note, jnp.where(at < sub * 3 // 4, high, mass - high))
    per = max(1, 2048 * rows * nrow // held.shape[0] // rows // 8)
    for first in range(0, nrow, per):
        last = min(first + per, nrow)
        gram = lax.dot_general(left[first * rows : last * rows, :], held[...], INNER, preferred_element_type=F32)
        for n in range(first, last):
            out = outs[order[n]]
            out[...] = gram[(n - first) * rows : (n - first + 1) * rows, :].astype(out.dtype)
            spot = pl.ds(pl.multiple_of(place(nrow, ncol, rows, order[n], 0), 2 * rows), 2 * rows)
            seen = out[sub:, spot].astype(F32)
            out[sub:, spot] = jnp.where(lane < sub, note, seen).astype(out.dtype)


def sum_kernel(nrow, ncol, order, *refs):
    parts, (out, vectors) = [refs[order.index(k)] for k in range(nrow)], refs[-2:]
    rows = parts[0].shape[0]
    sub = rows // 2
    total = parts[0][...].astype(F32)
    for r in parts[1:]:
        total = total + r[...].astype(F32)
    out[:rows, :] = total
    own = group(ncol, rows, 0)
    mirror = jnp.transpose(out[:sub, own])[sub : 2 * sub, :]
    out[sub:rows, own] = jnp.concatenate([mirror, out[sub:rows, own][:, sub:]], axis=1)
    mass = jnp.zeros((1, 1), F32)
    for k, part in enumerate(parts):
        note = part[sub:, own].astype(F32)[:, :sub]
        mass = mass + note[sub // 2 : sub // 2 + 1, :1] + note[sub * 3 // 4 : sub * 3 // 4 + 1, :1]
        line = jnp.concatenate([note[n : n + 1, :] for n in range(2 * ncol)], axis=1)
        vectors[:, group(ncol, rows, k)] = jnp.broadcast_to(line, (8, ncol * rows))
    out[rows:, :] = jnp.broadcast_to(mass, (8, out.shape[1]))


def assemble(nrow, ncol, rows, keys, refs, held):
    for c in range(ncol):
        for n, k in enumerate(keys):
            held[pl.ds(place(nrow, ncol, rows, k, c), rows), :] = refs[c][n * rows : (n + 1) * rows, :]


def raw_gram_kernel(nrow, ncol, rows, keys, *refs):
    out, raw = refs[ncol:]
    assemble(nrow, ncol, rows, keys, refs, raw)
    out[:rows, :] = lax.dot_general(refs[0][:rows, :], raw[...], INNER, preferred_element_type=F32)
    for at in range(0, raw.shape[0], 128):
        squares = jnp.sum(jnp.square(raw[at : at + 128, :].astype(F32)), axis=1, keepdims=True)
        out[rows:, at : at + 128] = jnp.broadcast_to(lane_row(squares), (8, 128))


def normalize(raw, squares, units):
    for at in range(0, raw.shape[0], 128):
        inverse = 1.0 / jnp.sqrt(column(squares[:1, at : at + 128]))
        units[at : at + 128, :] = (raw[at : at + 128, :].astype(F32) * inverse).astype(BF16)


def unit_gram_kernel(ncol, mine, other, *refs):
    rows = mine.shape[0] - 8
    gram, inverses, squares = refs[1:4] if len(refs) > 3 else refs
    squares[...] = mine[rows:, :] + other[rows:, :]
    at = pl.multiple_of(lax.axis_index("row") * ncol * rows, 2 * rows)
    inverse = 1.0 / jnp.sqrt(column(squares[:1, pl.ds(at, 2 * rows)][:, :rows]))
    inverses[...] = jnp.broadcast_to(inverse, inverses.shape)
    gram[...] = (mine[:rows, :] + other[:rows, :]) * (inverse * (1.0 / jnp.sqrt(squares[:1, :])))
    if len(refs) > 3:
        normalize(refs[0], squares, refs[4])


def final_kernel(nrow, ncol, keys, mine, other, vectors, gram, inverses, squares, stud, scale, *refs):
    rows = stud.shape[0]
    if keys:
        out, units = refs[-2:]
        assemble(nrow, ncol, rows, keys, refs, units)
        normalize(units, squares, units)
    else:
        units, out = refs
    inverse = inverses[:, :1]
    mass = (mine[rows : rows + 1, :1] + other[rows : rows + 1, :1]) / mine.shape[1]
    outer = (column(scale[...].astype(F32)) / mass) * vectors[:1, :]
    error_b = (gram[...] - outer * (mine[:rows, :] + other[:rows, :])).astype(BF16)
    grads = 4.0 * jnp.dot(error_b, units[...], preferred_element_type=F32)
    along = 4.0 * jnp.sum(error_b.astype(F32) * gram[...], axis=1, keepdims=True)
    unit = stud[...].astype(F32) * inverse
    out[...] = (grads - along * unit) * inverse


def shards(student, teacher, scale):
    rows, half = student.shape
    nrow, ncol = lax.axis_size("row"), lax.axis_size("col")
    batch = rows * nrow * ncol
    part = teacher.shape[1] // nrow
    small = batch <= 2048
    sds = jax.ShapeDtypeStruct
    scale = scale.reshape(1, rows)

    def along_row(x, k):
        return lax.ppermute(x, "row", [(i, i ^ k) for i in range(nrow)])

    def along_col(x, c):
        return lax.ppermute(x, "col", [(i, (i - c) % ncol) for i in range(ncol)])

    def other_core(x):
        return lax.ppermute(x, "sub", [(0, 1), (1, 0)])

    def pack(xs, after=()):
        shape = (sum(x.shape[0] for x in xs), half)
        return call(pack_kernel, sds(shape, BF16), xs, after=after)

    def with_columns(x):
        return [x if c == 0 else along_col(x, c) for c in range(ncol)]

    middle = nrow // 2
    order = list(range(middle, nrow)) + list(range(middle))
    cuts = call(functools.partial(cut_kernel, nrow), [sds((rows, part), BF16)] * nrow, [teacher])
    came = {k: along_row(cuts[k], k) for k in order if k}
    swapped = along_row(student, middle)
    tags, own = call(tag_kernel, [sds((TAIL, part), BF16), sds((rows, part), BF16)], [teacher, scale, cuts[0]])
    columns = {}
    for k in order:
        piece = came[k] if k else own
        if k == 1:
            piece = call(pack_kernel, sds((rows + TAIL, part), BF16), [piece, tags])
        columns[k] = with_columns(piece)
    partial = call(
        functools.partial(gram_kernel, nrow, ncol, rows, order),
        [sds((rows, batch), BF16 if k else F32) for k in range(nrow)],
        [columns[k][c] for k in order for c in range(ncol)],
        scratch=[pltpu.VMEM((batch, part), BF16), pltpu.VMEM((nrow * rows, part), BF16)],
    )
    returned = {k: along_row(partial[k], k) if k else partial[0] for k in order}

    stack, keys, k = [student], [0], middle
    while k:
        joined = pack(stack, after=columns[middle][1:2] + columns[0][1:2] + list(came.values()) if k == 1 else ()) if k < middle else student
        stack.append(swapped if k == middle else along_row(joined, k))
        keys, k = keys + [n ^ k for n in keys], k // 2
    raw_refs = with_columns(pack(stack, after=[partial[0]]))
    raw_gram, *raw = call(
        functools.partial(raw_gram_kernel, nrow, ncol, rows, keys),
        [sds((rows + 8, batch), F32)] + ([sds((batch, half), BF16)] if small else []),
        raw_refs,
        scratch=[] if small else [pltpu.VMEM((batch, half), BF16)],
    )
    gram, inverses, squares, *units = call(
        functools.partial(unit_gram_kernel, ncol),
        [sds((rows, batch), F32), sds((rows, 128), F32), sds((8, batch), F32)] + ([sds((batch, half), BF16)] if small else []),
        [raw_gram, other_core(raw_gram)] + raw,
    )
    message, vectors = call(
        functools.partial(sum_kernel, nrow, ncol, order),
        [sds((rows + 8, batch), F32), sds((8, batch), F32)],
        [returned[k] for k in order],
    )
    return call(
        functools.partial(final_kernel, nrow, ncol, None if small else keys),
        sds((rows, half), F32),
        [message, other_core(message), vectors, gram, inverses, squares, student, scale] + (units if small else raw_refs),
        scratch=[] if small else [pltpu.VMEM((batch, half), BF16)],
    )


def solution(mesh):
    spec = P(("groups", "row", "col"), "sub")
    return jax.shard_map(
        shards,
        mesh=mesh,
        in_specs=(spec, spec, P(("groups", "row", "col"))),
        out_specs=spec,
        check_vma=False,
    )
```

```python
import functools

import jax
import jax.numpy as jnp
from jax import lax
from jax.experimental import pallas as pl
from jax.experimental.pallas import tpu as pltpu
from jax.sharding import PartitionSpec as P

F32, BF16 = jnp.float32, jnp.bfloat16
INNER = (((1,), (1,)), ((), ()))
TAIL = 16


def call(body, out_shape, operands, scratch=(), after=()):
    outs = out_shape if isinstance(out_shape, (list, tuple)) else [out_shape]
    moved = sum(x.size * x.dtype.itemsize for x in list(operands) + list(outs))

    def run(*refs):
        body(*refs[: len(operands)], *refs[len(operands) + len(after) :])

    return pl.pallas_call(
        run,
        out_shape=out_shape,
        in_specs=[pl.BlockSpec(memory_space=pltpu.VMEM)] * len(operands) + [pl.BlockSpec(memory_space=pl.ANY)] * len(after),
        out_specs=jax.tree.map(lambda _: pl.BlockSpec(memory_space=pltpu.VMEM), out_shape),
        scratch_shapes=list(scratch),
        cost_estimate=pl.CostEstimate(flops=0, bytes_accessed=0, transcendentals=0),
        compiler_params=pltpu.CompilerParams(vmem_limit_bytes=min(56 << 20, (8 << 20) + 3 * moved)),
    )(*operands, *after)


def column(row):
    shape = (row.shape[1], row.shape[1])
    eye = lax.broadcasted_iota(jnp.int32, shape, 0) == lax.broadcasted_iota(jnp.int32, shape, 1)
    return jnp.sum(jnp.where(eye, row, 0.0), axis=1, keepdims=True)


def tags_of(scales, mass):
    shape = (TAIL, scales.shape[1])
    at = lax.broadcasted_iota(jnp.int32, shape, 0)
    high = mass.astype(BF16).astype(F32)
    return jnp.where(at < 8, scales, jnp.where(at < 12, high, mass - high)).astype(BF16)


def read_tags(tags):
    tags = tags.astype(F32)
    return tags[0:1, :], tags[8:9, 0:1] + tags[12:13, 0:1]


def lane_row(col):
    shape = (col.shape[0], col.shape[0])
    eye = lax.broadcasted_iota(jnp.int32, shape, 0) == lax.broadcasted_iota(jnp.int32, shape, 1)
    return jnp.sum(jnp.where(eye, col, 0.0), axis=0, keepdims=True)


def wide(out, at, piece):
    rows, part = piece.shape
    width = out.shape[1]
    high = rows * part // width
    for n in range(width // part):
        out[at : at + high, n * part : (n + 1) * part] = piece[n * high : (n + 1) * high, :]


def put(held, spot, rows, ref, at):
    width = held.shape[1]
    high = rows * width // ref.shape[1]
    for n in range(ref.shape[1] // width):
        held[pl.ds(spot + n * high, high), :] = ref[at : at + high, n * width : (n + 1) * width]


def cut_kernel(nrow, teach, *outs):
    part = teach.shape[1] // nrow
    z = lax.axis_index("row")
    for k in range(1, nrow):
        at = pl.multiple_of((z ^ k) * part, part)
        outs[k - 1][...] = teach[:, pl.ds(at, part)]


def ride_kernel(stud, *refs):
    rows, count = stud.shape[0], len(refs) // 2
    for piece, out in zip(refs[:count], refs[count:]):
        out[:rows, :] = stud[...]
        wide(out, rows, piece)


def own_kernel(nrow, teach, stud, scale, out):
    rows, half = stud.shape
    part = teach.shape[1] // nrow
    ts = teach[...].astype(F32)
    s = scale[...].astype(F32)
    mass = jnp.sum(jnp.square(column(s)) * jnp.sum(ts * ts, axis=1, keepdims=True), keepdims=True)
    tags = tags_of(jnp.concatenate([s, s], axis=1), mass)
    out[:rows, :] = stud[...]
    out[rows : rows + TAIL, :] = jnp.concatenate([tags] * (half // (2 * rows)), axis=1)
    wide(out, rows + TAIL, teach[:, pl.ds(pl.multiple_of(lax.axis_index("row") * part, part), part)])


def take_kernel(rows, ref, out):
    put(out, 0, rows, ref, rows)


def pack_kernel(spans, *refs):
    out, at = refs[-1], 0
    for r, (first, last) in zip(refs[:-1], spans):
        out[at : at + last - first, :] = r[first:last, :]
        at += last - first


def place(nrow, ncol, rows, k, c):
    return pl.multiple_of(((lax.axis_index("row") ^ k) * ncol + c) * rows, rows)


def group(ncol, rows, k):
    at = (lax.axis_index("row") ^ k) * ncol * rows
    return pl.ds(pl.multiple_of(at, 2 * rows), ncol * rows)


def gram_kernel(nrow, ncol, rows, order, *refs):
    count = nrow * ncol
    outs, held, left = refs[count : count + nrow], refs[-2], refs[-1]
    own = order.index(0) * ncol
    for n, k in enumerate(order):
        for c in range(ncol):
            put(held, place(nrow, ncol, rows, k, c), rows, refs[n * ncol + c], 0 if k else rows + TAIL)
    for n, k in enumerate(order):
        left[n * rows : (n + 1) * rows, :] = held[pl.ds(place(nrow, ncol, rows, k, 0), rows), :]
    sub = rows // 2
    at = lax.broadcasted_iota(jnp.int32, (sub, 2 * rows), 0)
    lane = lax.broadcasted_iota(jnp.int32, (sub, 2 * rows), 1)
    note, mass = jnp.zeros((sub, 2 * rows), F32), jnp.zeros((1, 1), F32)
    for c in range(ncol):
        scales, part = read_tags(refs[own + c][rows : rows + TAIL, : 2 * rows])
        turned = jnp.concatenate([scales[:, sub:], scales[:, :sub]], axis=1)
        note = jnp.where(at == 2 * c, scales, jnp.where(at == 2 * c + 1, turned, note))
        mass = mass + part
    high = mass.astype(BF16).astype(F32)
    note = jnp.where(at < sub // 2, note, jnp.where(at < sub * 3 // 4, high, mass - high))
    per = max(1, 2048 * rows * nrow // held.shape[0] // rows // 8)
    for first in range(0, nrow, per):
        last = min(first + per, nrow)
        gram = lax.dot_general(left[first * rows : last * rows, :], held[...], INNER, preferred_element_type=F32)
        for n in range(first, last):
            out = outs[order[n]]
            out[...] = gram[(n - first) * rows : (n - first + 1) * rows, :].astype(out.dtype)
            spot = pl.ds(pl.multiple_of(place(nrow, ncol, rows, order[n], 0), 2 * rows), 2 * rows)
            seen = out[sub:, spot].astype(F32)
            out[sub:, spot] = jnp.where(lane < sub, note, seen).astype(out.dtype)


def assemble(nrow, ncol, rows, keys, refs, held):
    each = len(keys)
    for c in range(ncol):
        for stack, ref in zip(keys, refs[c * each : (c + 1) * each]):
            for n, k in enumerate(stack):
                held[pl.ds(place(nrow, ncol, rows, k, c), rows), :] = ref[n * rows : (n + 1) * rows, :]


def raw_gram_kernel(nrow, ncol, rows, keys, *refs):
    count = len(keys) * ncol
    out, raw = refs[count:]
    assemble(nrow, ncol, rows, keys, refs, raw)
    out[:rows, :] = lax.dot_general(refs[0][:rows, :], raw[...], INNER, preferred_element_type=F32)
    for at in range(0, raw.shape[0], 128):
        squares = jnp.sum(jnp.square(raw[at : at + 128, :].astype(F32)), axis=1, keepdims=True)
        out[rows:, at : at + 128] = jnp.broadcast_to(lane_row(squares), (8, 128))


def sum_kernel(nrow, ncol, order, *refs):
    parts, (out, vectors) = [refs[order.index(k)] for k in range(nrow)], refs[-2:]
    rows = parts[0].shape[0]
    sub = rows // 2
    total = parts[0][...].astype(F32)
    for r in parts[1:]:
        total = total + r[...].astype(F32)
    out[:rows, :] = total
    own = group(ncol, rows, 0)
    mirror = jnp.transpose(out[:sub, own])[sub : 2 * sub, :]
    out[sub:rows, own] = jnp.concatenate([mirror, out[sub:rows, own][:, sub:]], axis=1)
    mass = jnp.zeros((1, 1), F32)
    for k, part in enumerate(parts):
        note = part[sub:, own].astype(F32)[:, :sub]
        mass = mass + note[sub // 2 : sub // 2 + 1, :1] + note[sub * 3 // 4 : sub * 3 // 4 + 1, :1]
        line = jnp.concatenate([note[n : n + 1, :] for n in range(2 * ncol)], axis=1)
        vectors[:, group(ncol, rows, k)] = jnp.broadcast_to(line, (8, ncol * rows))
    out[rows:, :] = jnp.broadcast_to(mass, (8, out.shape[1]))


def normalize(raw, squares, units):
    for at in range(0, raw.shape[0], 128):
        inverse = 1.0 / jnp.sqrt(column(squares[:1, at : at + 128]))
        units[at : at + 128, :] = (raw[at : at + 128, :].astype(F32) * inverse).astype(BF16)


def unit_gram_kernel(ncol, mine, other, *refs):
    rows = mine.shape[0] - 8
    gram, inverses, squares = refs[1:4] if len(refs) > 3 else refs
    squares[...] = mine[rows:, :] + other[rows:, :]
    at = pl.multiple_of(lax.axis_index("row") * ncol * rows, 2 * rows)
    inverse = 1.0 / jnp.sqrt(column(squares[:1, pl.ds(at, 2 * rows)][:, :rows]))
    inverses[...] = jnp.broadcast_to(inverse, inverses.shape)
    gram[...] = (mine[:rows, :] + other[:rows, :]) * (inverse * (1.0 / jnp.sqrt(squares[:1, :])))
    if len(refs) > 3:
        normalize(refs[0], squares, refs[4])


def final_kernel(nrow, ncol, keys, mine, other, vectors, gram, inverses, squares, stud, scale, *refs):
    rows = stud.shape[0]
    if keys:
        out, units = refs[-2:]
        assemble(nrow, ncol, rows, keys, refs[:-2], units)
        normalize(units, squares, units)
    else:
        units, out = refs
    inverse = inverses[:, :1]
    mass = (mine[rows : rows + 1, :1] + other[rows : rows + 1, :1]) / mine.shape[1]
    outer = (column(scale[...].astype(F32)) / mass) * vectors[:1, :]
    error_b = (gram[...] - outer * (mine[:rows, :] + other[:rows, :])).astype(BF16)
    grads = 4.0 * jnp.dot(error_b, units[...], preferred_element_type=F32)
    along = 4.0 * jnp.sum(error_b.astype(F32) * gram[...], axis=1, keepdims=True)
    unit = stud[...].astype(F32) * inverse
    out[...] = (grads - along * unit) * inverse


def shards(student, teacher, scale):
    rows, half = student.shape
    nrow, ncol = lax.axis_size("row"), lax.axis_size("col")
    batch = rows * nrow * ncol
    part = teacher.shape[1] // nrow
    small = batch <= 2048
    sds = jax.ShapeDtypeStruct
    scale = scale.reshape(1, rows)

    def along_row(x, k):
        return lax.ppermute(x, "row", [(i, i ^ k) for i in range(nrow)])

    def along_col(x, c):
        return lax.ppermute(x, "col", [(i, (i - c) % ncol) for i in range(ncol)])

    def other_core(x):
        return lax.ppermute(x, "sub", [(0, 1), (1, 0)])

    def pack(xs, spans, after=()):
        shape = (sum(last - first for first, last in spans), half)
        return call(functools.partial(pack_kernel, spans), sds(shape, BF16), xs, after=after)

    def with_columns(x):
        return [x if c == 0 else along_col(x, c) for c in range(ncol)]

    middle, high = nrow // 2, rows * part // half
    order = list(range(middle, nrow)) + list(range(middle))
    riders = (1, middle)
    cuts = call(functools.partial(cut_kernel, nrow), [sds((rows, part), BF16)] * (nrow - 1), [teacher])
    ridden = call(ride_kernel, [sds((rows + high, half), BF16)] * 2, [student] + [cuts[k - 1] for k in riders])
    leaving = dict(enumerate(cuts, 1)) | dict(zip(riders, ridden))
    came = {k: along_row(leaving[k], k) for k in order if k}
    own = call(
        functools.partial(own_kernel, nrow),
        sds((rows + TAIL + high, half), BF16),
        [teacher, student, scale],
        after=[came[nrow - 1]],
    )
    columns = {0: with_columns(own)}
    for k in range(1, nrow):
        piece = came[k]
        if k in riders:
            piece = call(functools.partial(take_kernel, rows), sds((rows, part), BF16), [piece])
        columns[k] = with_columns(piece)
    partial = call(
        functools.partial(gram_kernel, nrow, ncol, rows, order),
        [sds((rows, batch), BF16 if k else F32) for k in range(nrow)],
        [columns[k][c] for k in order for c in range(ncol)],
        scratch=[pltpu.VMEM((batch, part), BF16), pltpu.VMEM((nrow * rows, part), BF16)],
    )
    returned = {k: along_row(partial[k], k) if k else partial[0] for k in order}

    near, far = came[1], came[middle]
    stack, keys, k, spans, got, got_keys = [student, far], [0, middle], middle // 2, [(0, rows)] * 2, [], []
    while k:
        first = 1 if k == 1 else 0
        sent = pack(stack[first:], spans[first:])
        got.append(along_row(sent, k))
        got_keys += [n ^ k for n in keys[first:]]
        stack, spans, keys = stack + got[-1:], spans + [(0, len(keys) * rows)], keys + [n ^ k for n in keys]
        k //= 2
    rest = pack([near, far] + got, [(0, rows)] * 2 + [(0, g.shape[0]) for g in got], after=[partial[0]])
    raw_keys = [[0], [1, middle] + got_keys]
    sources = [columns[0], with_columns(rest)]
    raw_refs = [x[c] for c in range(ncol) for x in sources]
    raw_gram, *raw = call(
        functools.partial(raw_gram_kernel, nrow, ncol, rows, raw_keys),
        [sds((rows + 8, batch), F32)] + ([sds((batch, half), BF16)] if small else []),
        raw_refs,
        scratch=[] if small else [pltpu.VMEM((batch, half), BF16)],
    )
    gram, inverses, squares, *units = call(
        functools.partial(unit_gram_kernel, ncol),
        [sds((rows, batch), F32), sds((rows, 128), F32), sds((8, batch), F32)] + ([sds((batch, half), BF16)] if small else []),
        [raw_gram, other_core(raw_gram)] + raw,
    )
    message, vectors = call(
        functools.partial(sum_kernel, nrow, ncol, order),
        [sds((rows + 8, batch), F32), sds((8, batch), F32)],
        [returned[k] for k in order],
    )
    return call(
        functools.partial(final_kernel, nrow, ncol, None if small else raw_keys),
        sds((rows, half), F32),
        [message, other_core(message), vectors, gram, inverses, squares, student, scale] + (units if small else raw_refs),
        scratch=[] if small else [pltpu.VMEM((batch, half), BF16)],
    )


def solution(mesh):
    spec = P(("groups", "row", "col"), "sub")
    return jax.shard_map(
        shards,
        mesh=mesh,
        in_specs=(spec, spec, P(("groups", "row", "col"))),
        out_specs=spec,
        check_vma=False,
    )
```

```python
import functools

import jax
import jax.numpy as jnp
from jax import lax
from jax.experimental import pallas as pl
from jax.experimental.pallas import tpu as pltpu
from jax.sharding import PartitionSpec as P

F32, BF16 = jnp.float32, jnp.bfloat16
INNER = (((1,), (1,)), ((), ()))
TAIL = 16


def call(body, out_shape, operands, scratch=(), after=()):
    outs = out_shape if isinstance(out_shape, (list, tuple)) else [out_shape]
    moved = sum(x.size * x.dtype.itemsize for x in list(operands) + list(outs))

    def run(*refs):
        body(*refs[: len(operands)], *refs[len(operands) + len(after) :])

    return pl.pallas_call(
        run,
        out_shape=out_shape,
        in_specs=[pl.BlockSpec(memory_space=pltpu.VMEM)] * len(operands) + [pl.BlockSpec(memory_space=pl.ANY)] * len(after),
        out_specs=jax.tree.map(lambda _: pl.BlockSpec(memory_space=pltpu.VMEM), out_shape),
        scratch_shapes=list(scratch),
        cost_estimate=pl.CostEstimate(flops=0, bytes_accessed=0, transcendentals=0),
        compiler_params=pltpu.CompilerParams(vmem_limit_bytes=min(56 << 20, (8 << 20) + 3 * moved)),
    )(*operands, *after)


def column(row):
    shape = (row.shape[1], row.shape[1])
    eye = lax.broadcasted_iota(jnp.int32, shape, 0) == lax.broadcasted_iota(jnp.int32, shape, 1)
    return jnp.sum(jnp.where(eye, row, 0.0), axis=1, keepdims=True)


def tags_of(scales, mass):
    shape = (TAIL, scales.shape[1])
    at = lax.broadcasted_iota(jnp.int32, shape, 0)
    high = mass.astype(BF16).astype(F32)
    return jnp.where(at < 8, scales, jnp.where(at < 12, high, mass - high)).astype(BF16)


def read_tags(tags):
    tags = tags.astype(F32)
    return tags[0:1, :], tags[8:9, 0:1] + tags[12:13, 0:1]


def lane_row(col):
    shape = (col.shape[0], col.shape[0])
    eye = lax.broadcasted_iota(jnp.int32, shape, 0) == lax.broadcasted_iota(jnp.int32, shape, 1)
    return jnp.sum(jnp.where(eye, col, 0.0), axis=0, keepdims=True)


def wide(out, at, piece):
    rows, part = piece.shape
    width = out.shape[1]
    high = rows * part // width
    for n in range(width // part):
        out[at : at + high, n * part : (n + 1) * part] = piece[n * high : (n + 1) * high, :]


def put(held, spot, rows, ref, at):
    width = held.shape[1]
    high = rows * width // ref.shape[1]
    for n in range(ref.shape[1] // width):
        held[pl.ds(spot + n * high, high), :] = ref[at : at + high, n * width : (n + 1) * width]


def cut_kernel(nrow, teach, *outs):
    part = teach.shape[1] // nrow
    z = lax.axis_index("row")
    for k in range(1, nrow):
        at = pl.multiple_of((z ^ k) * part, part)
        outs[k - 1][...] = teach[:, pl.ds(at, part)]


def ride_kernel(stud, *refs):
    rows, count = stud.shape[0], len(refs) // 2
    for piece, out in zip(refs[:count], refs[count:]):
        out[:rows, :] = stud[...]
        wide(out, rows, piece)


def own_kernel(nrow, teach, stud, scale, out):
    rows, half = stud.shape
    part = teach.shape[1] // nrow
    ts = teach[...].astype(F32)
    s = scale[...].astype(F32)
    mass = jnp.sum(jnp.square(column(s)) * jnp.sum(ts * ts, axis=1, keepdims=True), keepdims=True)
    tags = tags_of(jnp.concatenate([s, s], axis=1), mass)
    out[:rows, :] = stud[...]
    out[rows : rows + TAIL, :] = jnp.concatenate([tags] * (half // (2 * rows)), axis=1)
    wide(out, rows + TAIL, teach[:, pl.ds(pl.multiple_of(lax.axis_index("row") * part, part), part)])


def take_kernel(rows, ref, out):
    put(out, 0, rows, ref, rows)


def pack_kernel(spans, *refs):
    out, at = refs[-1], 0
    for r, (first, last) in zip(refs[:-1], spans):
        out[at : at + last - first, :] = r[first:last, :]
        at += last - first


def place(nrow, ncol, rows, k, c):
    return pl.multiple_of(((lax.axis_index("row") ^ k) * ncol + c) * rows, rows)


def group(ncol, rows, k):
    at = (lax.axis_index("row") ^ k) * ncol * rows
    return pl.ds(pl.multiple_of(at, 2 * rows), ncol * rows)


def note_of(scales, mass):
    shape = (32, scales.shape[1])
    at = lax.broadcasted_iota(jnp.int32, shape, 0)
    high = mass.astype(BF16).astype(F32)
    return jnp.where(at < 16, scales, jnp.where(at < 24, high, mass - high))


def read_note(note):
    note = note.astype(F32)
    return note[0:1, :], note[16:17, :1] + note[24:25, :1]


def gram_kernel(nrow, ncol, rows, order, *refs):
    count = nrow * ncol
    kept, given, held, left = refs[count:]
    own = order.index(0) * ncol
    for n, k in enumerate(order):
        for c in range(ncol):
            put(held, place(nrow, ncol, rows, k, c), rows, refs[n * ncol + c], 0 if k else rows + TAIL)
    sub, batch = rows // 2, held.shape[0]
    total = nrow * sub
    core = lax.axis_index("sub")
    for n, k in enumerate(order):
        for first, which in ((0, 1 - core), (total, core)):
            at = pl.multiple_of(place(nrow, ncol, rows, k, 0) + which * sub, sub)
            left[first + n * sub : first + (n + 1) * sub, :] = held[pl.ds(at, sub), :]
    lane = lax.broadcasted_iota(jnp.int32, (1, 2 * rows), 1)
    line, mass = [], jnp.zeros((1, 1), F32)
    for c in range(0, ncol, 2):
        pair = [read_tags(refs[own + d][rows : rows + TAIL, : 2 * rows]) for d in (c, c + 1)]
        line.append(jnp.where(lane < rows, pair[0][0], pair[1][0]))
        mass = mass + pair[0][1] + pair[1][1]
    note = note_of(jnp.concatenate(line, axis=1) if len(line) > 1 else line[0], mass)
    given[:, :batch] = lax.dot_general(left[:total, :], held[...], INNER, preferred_element_type=F32).astype(BF16)
    given[:sub, batch:] = note.astype(BF16)
    given[sub:, batch:] = jnp.zeros((total - sub, ncol * rows), BF16)
    kept[:, :batch] = lax.dot_general(left[total:, :], held[...], INNER, preferred_element_type=F32).astype(kept.dtype)
    kept[:sub, batch:] = note.astype(kept.dtype)


def fold_kernel(order, batch, kept, came, *outs):
    sub = outs[0].shape[0]
    (scales, mass), (_, more) = read_note(kept[:sub, batch:]), read_note(came[:sub, batch:])
    note = note_of(scales, mass + more)
    for n, k in enumerate(order):
        at = slice(n * sub, (n + 1) * sub)
        outs[k][:, :batch] = (kept[at, :batch].astype(F32) + came[at, :batch].astype(F32)).astype(outs[k].dtype)
        outs[k][:, batch:] = note.astype(outs[k].dtype)


def teach_kernel(nrow, ncol, rows, *refs):
    parts, (scale, out, vectors) = refs[:nrow], refs[nrow:]
    sub, batch = out.shape
    total, mass = parts[0][:, :batch].astype(F32), jnp.zeros((1, 1), F32)
    for k, part in enumerate(parts):
        scales, more = read_note(part[:, batch:])
        mass = mass + more
        vectors[:, group(ncol, rows, k)] = jnp.broadcast_to(scales, (8, ncol * rows))
        if k:
            total = total + part[:, :batch].astype(F32)
    shape = (sub, rows)
    first = lax.axis_index("sub") * sub
    eye = lax.broadcasted_iota(jnp.int32, shape, 0) + first == lax.broadcasted_iota(jnp.int32, shape, 1)
    s = jnp.sum(jnp.where(eye, scale[...].astype(F32), 0.0), axis=1, keepdims=True)
    out[...] = (s / (mass / batch)) * vectors[:1, :] * total


def assemble(nrow, ncol, rows, keys, refs, held):
    each = len(keys)
    for c in range(ncol):
        for stack, ref in zip(keys, refs[c * each : (c + 1) * each]):
            for n, k in enumerate(stack):
                held[pl.ds(place(nrow, ncol, rows, k, c), rows), :] = ref[n * rows : (n + 1) * rows, :]


def raw_gram_kernel(nrow, ncol, rows, keys, *refs):
    count = len(keys) * ncol
    out, raw = refs[count:]
    assemble(nrow, ncol, rows, keys, refs, raw)
    out[:rows, :] = lax.dot_general(refs[0][:rows, :], raw[...], INNER, preferred_element_type=F32)
    for at in range(0, raw.shape[0], 128):
        squares = jnp.sum(jnp.square(raw[at : at + 128, :].astype(F32)), axis=1, keepdims=True)
        out[rows:, at : at + 128] = jnp.broadcast_to(lane_row(squares), (8, 128))


def normalize(raw, squares, units):
    for at in range(0, raw.shape[0], 128):
        inverse = 1.0 / jnp.sqrt(column(squares[:1, at : at + 128]))
        units[at : at + 128, :] = (raw[at : at + 128, :].astype(F32) * inverse).astype(BF16)


def unit_gram_kernel(ncol, mine, other, *refs):
    rows = mine.shape[0] - 8
    gram, inverses, squares = refs[1:4] if len(refs) > 3 else refs
    squares[...] = mine[rows:, :] + other[rows:, :]
    at = pl.multiple_of(lax.axis_index("row") * ncol * rows, 2 * rows)
    inverse = 1.0 / jnp.sqrt(column(squares[:1, pl.ds(at, 2 * rows)][:, :rows]))
    inverses[...] = jnp.broadcast_to(inverse, inverses.shape)
    gram[...] = (mine[:rows, :] + other[:rows, :]) * (inverse * (1.0 / jnp.sqrt(squares[:1, :])))
    if len(refs) > 3:
        normalize(refs[0], squares, refs[4])


def final_kernel(nrow, ncol, keys, mine, other, gram, inverses, squares, stud, *refs):
    rows = stud.shape[0]
    if keys:
        out, teach, units = refs[-3:]
        assemble(nrow, ncol, rows, keys, refs[:-3], units)
        normalize(units, squares, units)
    else:
        units, out, teach = refs
    sub = rows // 2
    core = lax.axis_index("sub")
    teach[pl.ds(pl.multiple_of(core * sub, sub), sub), :] = mine[...]
    teach[pl.ds(pl.multiple_of((1 - core) * sub, sub), sub), :] = other[...]
    error_b = (gram[...] - teach[...]).astype(BF16)
    inverse = inverses[:, :1]
    grads = 4.0 * jnp.dot(error_b, units[...], preferred_element_type=F32)
    along = 4.0 * jnp.sum(error_b.astype(F32) * gram[...], axis=1, keepdims=True)
    unit = stud[...].astype(F32) * inverse
    out[...] = (grads - along * unit) * inverse


def shards(student, teacher, scale):
    rows, half = student.shape
    nrow, ncol = lax.axis_size("row"), lax.axis_size("col")
    batch = rows * nrow * ncol
    part = teacher.shape[1] // nrow
    small = batch <= 2048
    sds = jax.ShapeDtypeStruct
    scale = scale.reshape(1, rows)

    def along_row(x, k):
        return lax.ppermute(x, "row", [(i, i ^ k) for i in range(nrow)])

    def along_col(x, c):
        return lax.ppermute(x, "col", [(i, (i - c) % ncol) for i in range(ncol)])

    def other_core(x):
        return lax.ppermute(x, "sub", [(0, 1), (1, 0)])

    def pack(xs, spans, after=()):
        shape = (sum(last - first for first, last in spans), half)
        return call(functools.partial(pack_kernel, spans), sds(shape, BF16), xs, after=after)

    def with_columns(x):
        return [x if c == 0 else along_col(x, c) for c in range(ncol)]

    middle, high = nrow // 2, rows * part // half
    order = list(range(middle, nrow)) + list(range(middle))
    riders = (1, middle)
    cuts = call(functools.partial(cut_kernel, nrow), [sds((rows, part), BF16)] * (nrow - 1), [teacher])
    ridden = call(ride_kernel, [sds((rows + high, half), BF16)] * 2, [student] + [cuts[k - 1] for k in riders])
    leaving = dict(enumerate(cuts, 1)) | dict(zip(riders, ridden))
    came = {k: along_row(leaving[k], k) for k in order if k}
    own = call(
        functools.partial(own_kernel, nrow),
        sds((rows + TAIL + high, half), BF16),
        [teacher, student, scale],
        after=[came[nrow - 1]],
    )
    columns = {0: with_columns(own)}
    for k in range(1, nrow):
        piece = came[k]
        if k in riders:
            piece = call(functools.partial(take_kernel, rows), sds((rows, part), BF16), [piece])
        columns[k] = with_columns(piece)
    extra = batch + ncol * rows
    kept, given = call(
        functools.partial(gram_kernel, nrow, ncol, rows, order),
        [sds((nrow * rows // 2, extra), F32 if small else BF16), sds((nrow * rows // 2, extra), BF16)],
        [columns[k][c] for k in order for c in range(ncol)],
        scratch=[pltpu.VMEM((batch, part), BF16), pltpu.VMEM((nrow * rows, part), BF16)],
    )
    partial = call(
        functools.partial(fold_kernel, order, batch),
        [sds((rows // 2, extra), BF16 if k else F32) for k in range(nrow)],
        [kept, other_core(given)],
    )
    returned = {k: along_row(partial[k], k) if k else partial[0] for k in order}

    near, far = came[1], came[middle]
    stack, keys, k, spans, got, got_keys = [student, far], [0, middle], middle // 2, [(0, rows)] * 2, [], []
    while k:
        first = 1 if k == 1 else 0
        sent = pack(stack[first:], spans[first:])
        got.append(along_row(sent, k))
        got_keys += [n ^ k for n in keys[first:]]
        stack, spans, keys = stack + got[-1:], spans + [(0, len(keys) * rows)], keys + [n ^ k for n in keys]
        k //= 2
    rest = pack([near, far] + got, [(0, rows)] * 2 + [(0, g.shape[0]) for g in got], after=[kept])
    raw_keys = [[0], [1, middle] + got_keys]
    sources = [columns[0], with_columns(rest)]
    raw_refs = [x[c] for c in range(ncol) for x in sources]
    raw_gram, *raw = call(
        functools.partial(raw_gram_kernel, nrow, ncol, rows, raw_keys),
        [sds((rows + 8, batch), F32)] + ([sds((batch, half), BF16)] if small else []),
        raw_refs,
        after=[returned[k] for k in order if k],
        scratch=[] if small else [pltpu.VMEM((batch, half), BF16)],
    )
    gram, inverses, squares, *units = call(
        functools.partial(unit_gram_kernel, ncol),
        [sds((rows, batch), F32), sds((rows, 128), F32), sds((8, batch), F32)] + ([sds((batch, half), BF16)] if small else []),
        [raw_gram, other_core(raw_gram)] + raw,
    )
    taught = call(
        functools.partial(teach_kernel, nrow, ncol, rows),
        sds((rows // 2, batch), F32),
        [returned[k] for k in range(nrow)] + [scale],
        scratch=[pltpu.VMEM((8, batch), F32)],
    )
    return call(
        functools.partial(final_kernel, nrow, ncol, None if small else raw_keys),
        sds((rows, half), F32),
        [taught, other_core(taught), gram, inverses, squares, student] + (units if small else raw_refs),
        scratch=[pltpu.VMEM((rows, batch), F32)] + ([] if small else [pltpu.VMEM((batch, half), BF16)]),
    )


def solution(mesh):
    spec = P(("groups", "row", "col"), "sub")
    return jax.shard_map(
        shards,
        mesh=mesh,
        in_specs=(spec, spec, P(("groups", "row", "col"))),
        out_specs=spec,
        check_vma=False,
    )
```

```python
import functools

import jax
import jax.numpy as jnp
from jax import lax
from jax.experimental import pallas as pl
from jax.experimental.pallas import tpu as pltpu
from jax.sharding import PartitionSpec as P

F32, BF16 = jnp.float32, jnp.bfloat16
INNER = (((1,), (1,)), ((), ()))
TAIL = 16


def call(body, out_shape, operands, scratch=(), after=()):
    outs = out_shape if isinstance(out_shape, (list, tuple)) else [out_shape]
    moved = sum(x.size * x.dtype.itemsize for x in list(operands) + list(outs))

    def run(*refs):
        body(*refs[: len(operands)], *refs[len(operands) + len(after) :])

    return pl.pallas_call(
        run,
        out_shape=out_shape,
        in_specs=[pl.BlockSpec(memory_space=pltpu.VMEM)] * len(operands) + [pl.BlockSpec(memory_space=pl.ANY)] * len(after),
        out_specs=jax.tree.map(lambda _: pl.BlockSpec(memory_space=pltpu.VMEM), out_shape),
        scratch_shapes=list(scratch),
        cost_estimate=pl.CostEstimate(flops=0, bytes_accessed=0, transcendentals=0),
        compiler_params=pltpu.CompilerParams(vmem_limit_bytes=min(56 << 20, (8 << 20) + 3 * moved)),
    )(*operands, *after)


def column(row):
    shape = (row.shape[1], row.shape[1])
    eye = lax.broadcasted_iota(jnp.int32, shape, 0) == lax.broadcasted_iota(jnp.int32, shape, 1)
    return jnp.sum(jnp.where(eye, row, 0.0), axis=1, keepdims=True)


def tags_of(scales, mass):
    shape = (TAIL, scales.shape[1])
    at = lax.broadcasted_iota(jnp.int32, shape, 0)
    high = mass.astype(BF16).astype(F32)
    return jnp.where(at < 8, scales, jnp.where(at < 12, high, mass - high)).astype(BF16)


def read_tags(tags):
    tags = tags.astype(F32)
    return tags[0:1, :], tags[8:9, 0:1] + tags[12:13, 0:1]


def lane_row(col):
    shape = (col.shape[0], col.shape[0])
    eye = lax.broadcasted_iota(jnp.int32, shape, 0) == lax.broadcasted_iota(jnp.int32, shape, 1)
    return jnp.sum(jnp.where(eye, col, 0.0), axis=0, keepdims=True)


def wide(out, at, piece):
    rows, part = piece.shape
    width = out.shape[1]
    high = rows * part // width
    for n in range(width // part):
        out[at : at + high, n * part : (n + 1) * part] = piece[n * high : (n + 1) * high, :]


def put(held, spot, rows, ref, at):
    width = held.shape[1]
    high = rows * width // ref.shape[1]
    for n in range(ref.shape[1] // width):
        held[pl.ds(spot + n * high, high), :] = ref[at : at + high, n * width : (n + 1) * width]


def cut_kernel(nrow, teach, *outs):
    part = teach.shape[1] // nrow
    z = lax.axis_index("row")
    for k in range(1, nrow):
        at = pl.multiple_of((z ^ k) * part, part)
        outs[k - 1][...] = teach[:, pl.ds(at, part)]


def ride_kernel(stud, *refs):
    rows, count = stud.shape[0], len(refs) // 2
    for piece, out in zip(refs[:count], refs[count:]):
        out[:rows, :] = stud[...]
        wide(out, rows, piece)


def own_kernel(nrow, teach, stud, scale, out):
    rows, half = stud.shape
    part = teach.shape[1] // nrow
    ts = teach[...].astype(F32)
    s = scale[...].astype(F32)
    mass = jnp.sum(jnp.square(column(s)) * jnp.sum(ts * ts, axis=1, keepdims=True), keepdims=True)
    tags = tags_of(jnp.concatenate([s, s], axis=1), mass)
    out[:rows, :] = stud[...]
    out[rows : rows + TAIL, :] = jnp.concatenate([tags] * (half // (2 * rows)), axis=1)
    wide(out, rows + TAIL, teach[:, pl.ds(pl.multiple_of(lax.axis_index("row") * part, part), part)])


def take_kernel(rows, ref, out):
    put(out, 0, rows, ref, rows)


def pack_kernel(spans, *refs):
    out, at = refs[-1], 0
    for r, (first, last) in zip(refs[:-1], spans):
        out[at : at + last - first, :] = r[first:last, :]
        at += last - first


def place(nrow, ncol, rows, k, c):
    return pl.multiple_of(((lax.axis_index("row") ^ k) * ncol + c) * rows, rows)


def group(ncol, rows, k):
    at = (lax.axis_index("row") ^ k) * ncol * rows
    return pl.ds(pl.multiple_of(at, 2 * rows), ncol * rows)


def gram_kernel(nrow, ncol, rows, order, *refs):
    count = nrow * ncol
    outs, held, left = refs[count : count + nrow], refs[-2], refs[-1]
    own = order.index(0) * ncol
    for n, k in enumerate(order):
        for c in range(ncol):
            put(held, place(nrow, ncol, rows, k, c), rows, refs[n * ncol + c], 0 if k else rows + TAIL)
    for n, k in enumerate(order):
        left[n * rows : (n + 1) * rows, :] = held[pl.ds(place(nrow, ncol, rows, k, 0), rows), :]
    sub = rows // 2
    at = lax.broadcasted_iota(jnp.int32, (sub, 2 * rows), 0)
    lane = lax.broadcasted_iota(jnp.int32, (sub, 2 * rows), 1)
    note, mass = jnp.zeros((sub, 2 * rows), F32), jnp.zeros((1, 1), F32)
    for c in range(ncol):
        scales, part = read_tags(refs[own + c][rows : rows + TAIL, : 2 * rows])
        turned = jnp.concatenate([scales[:, sub:], scales[:, :sub]], axis=1)
        note = jnp.where(at == 2 * c, scales, jnp.where(at == 2 * c + 1, turned, note))
        mass = mass + part
    high = mass.astype(BF16).astype(F32)
    note = jnp.where(at < sub // 2, note, jnp.where(at < sub * 3 // 4, high, mass - high))
    per = max(1, 2048 * rows * nrow // held.shape[0] // rows // 8)
    for first in range(0, nrow, per):
        last = min(first + per, nrow)
        gram = lax.dot_general(left[first * rows : last * rows, :], held[...], INNER, preferred_element_type=F32)
        for n in range(first, last):
            out = outs[order[n]]
            out[...] = gram[(n - first) * rows : (n - first + 1) * rows, :].astype(out.dtype)
            spot = pl.ds(pl.multiple_of(place(nrow, ncol, rows, order[n], 0), 2 * rows), 2 * rows)
            seen = out[sub:, spot].astype(F32)
            out[sub:, spot] = jnp.where(lane < sub, note, seen).astype(out.dtype)


def assemble(nrow, ncol, rows, keys, refs, held):
    each = len(keys)
    for c in range(ncol):
        for stack, ref in zip(keys, refs[c * each : (c + 1) * each]):
            for n, k in enumerate(stack):
                held[pl.ds(place(nrow, ncol, rows, k, c), rows), :] = ref[n * rows : (n + 1) * rows, :]


def raw_gram_kernel(nrow, ncol, rows, keys, *refs):
    count = len(keys) * ncol
    out, raw = refs[count:]
    assemble(nrow, ncol, rows, keys, refs, raw)
    out[:rows, :] = lax.dot_general(refs[0][:rows, :], raw[...], INNER, preferred_element_type=F32)
    for at in range(0, raw.shape[0], 128):
        squares = jnp.sum(jnp.square(raw[at : at + 128, :].astype(F32)), axis=1, keepdims=True)
        out[rows:, at : at + 128] = jnp.broadcast_to(lane_row(squares), (8, 128))


def sum_kernel(nrow, ncol, order, *refs):
    parts, (out, vectors) = [refs[order.index(k)] for k in range(nrow)], refs[-2:]
    rows = parts[0].shape[0]
    sub = rows // 2
    total = parts[0][...].astype(F32)
    for r in parts[1:]:
        total = total + r[...].astype(F32)
    out[:rows, :] = total
    own = group(ncol, rows, 0)
    mirror = jnp.transpose(out[:sub, own])[sub : 2 * sub, :]
    out[sub:rows, own] = jnp.concatenate([mirror, out[sub:rows, own][:, sub:]], axis=1)
    mass = jnp.zeros((1, 1), F32)
    for k, part in enumerate(parts):
        note = part[sub:, own].astype(F32)[:, :sub]
        mass = mass + note[sub // 2 : sub // 2 + 1, :1] + note[sub * 3 // 4 : sub * 3 // 4 + 1, :1]
        line = jnp.concatenate([note[n : n + 1, :] for n in range(2 * ncol)], axis=1)
        vectors[:, group(ncol, rows, k)] = jnp.broadcast_to(line, (8, ncol * rows))
    out[rows:, :] = jnp.broadcast_to(mass, (8, out.shape[1]))


def normalize(raw, squares, units):
    for at in range(0, raw.shape[0], 128):
        inverse = 1.0 / jnp.sqrt(column(squares[:1, at : at + 128]))
        units[at : at + 128, :] = (raw[at : at + 128, :].astype(F32) * inverse).astype(BF16)


def unit_gram_kernel(ncol, mine, other, *refs):
    rows = mine.shape[0] - 8
    gram, inverses, squares = refs[1:4] if len(refs) > 3 else refs
    squares[...] = mine[rows:, :] + other[rows:, :]
    at = pl.multiple_of(lax.axis_index("row") * ncol * rows, 2 * rows)
    inverse = 1.0 / jnp.sqrt(column(squares[:1, pl.ds(at, 2 * rows)][:, :rows]))
    inverses[...] = jnp.broadcast_to(inverse, inverses.shape)
    gram[...] = (mine[:rows, :] + other[:rows, :]) * (inverse * (1.0 / jnp.sqrt(squares[:1, :])))
    if len(refs) > 3:
        normalize(refs[0], squares, refs[4])


def final_kernel(nrow, ncol, keys, mine, other, vectors, gram, inverses, squares, stud, scale, *refs):
    rows = stud.shape[0]
    if keys:
        out, units = refs[-2:]
        assemble(nrow, ncol, rows, keys, refs[:-2], units)
        normalize(units, squares, units)
    else:
        units, out = refs
    inverse = inverses[:, :1]
    mass = (mine[rows : rows + 1, :1] + other[rows : rows + 1, :1]) / mine.shape[1]
    outer = (column(scale[...].astype(F32)) / mass) * vectors[:1, :]
    error_b = (gram[...] - outer * (mine[:rows, :] + other[:rows, :])).astype(BF16)
    grads = 4.0 * jnp.dot(error_b, units[...], preferred_element_type=F32)
    along = 4.0 * jnp.sum(error_b.astype(F32) * gram[...], axis=1, keepdims=True)
    unit = stud[...].astype(F32) * inverse
    out[...] = (grads - along * unit) * inverse


def shards(student, teacher, scale):
    rows, half = student.shape
    nrow, ncol = lax.axis_size("row"), lax.axis_size("col")
    batch = rows * nrow * ncol
    part = teacher.shape[1] // nrow
    small = batch <= 2048
    sds = jax.ShapeDtypeStruct
    scale = scale.reshape(1, rows)

    def along_row(x, k):
        return lax.ppermute(x, "row", [(i, i ^ k) for i in range(nrow)])

    def along_col(x, c):
        return lax.ppermute(x, "col", [(i, (i - c) % ncol) for i in range(ncol)])

    def other_core(x):
        return lax.ppermute(x, "sub", [(0, 1), (1, 0)])

    def pack(xs, spans, after=()):
        shape = (sum(last - first for first, last in spans), half)
        return call(functools.partial(pack_kernel, spans), sds(shape, BF16), xs, after=after)

    def with_columns(x):
        return [x if c == 0 else along_col(x, c) for c in range(ncol)]

    middle, high = nrow // 2, rows * part // half
    order = list(range(middle, nrow)) + list(range(middle))
    riders = (1, middle)
    cuts = call(functools.partial(cut_kernel, nrow), [sds((rows, part), BF16)] * (nrow - 1), [teacher])
    ridden = call(ride_kernel, [sds((rows + high, half), BF16)] * 2, [student] + [cuts[k - 1] for k in riders])
    leaving = dict(enumerate(cuts, 1)) | dict(zip(riders, ridden))
    came = {k: along_row(leaving[k], k) for k in order if k}
    own = call(
        functools.partial(own_kernel, nrow),
        sds((rows + TAIL + high, half), BF16),
        [teacher, student, scale],
        after=[came[nrow - 1]],
    )
    columns = {0: with_columns(own)}
    for k in range(1, nrow):
        piece = came[k]
        if k in riders:
            piece = call(functools.partial(take_kernel, rows), sds((rows, part), BF16), [piece])
        columns[k] = with_columns(piece)
    partial = call(
        functools.partial(gram_kernel, nrow, ncol, rows, order),
        [sds((rows, batch), BF16 if k else F32) for k in range(nrow)],
        [columns[k][c] for k in order for c in range(ncol)],
        scratch=[pltpu.VMEM((batch, part), BF16), pltpu.VMEM((nrow * rows, part), BF16)],
    )
    returned = {k: along_row(partial[k], k) if k else partial[0] for k in order}

    near, far = came[1], came[middle]
    stack, keys, k, spans, got, got_keys = [student, far], [0, middle], middle // 2, [(0, rows)] * 2, [], []
    while k:
        first = 1 if k == 1 else 0
        sent = pack(stack[first:], spans[first:])
        got.append(along_row(sent, k))
        got_keys += [n ^ k for n in keys[first:]]
        stack, spans, keys = stack + got[-1:], spans + [(0, len(keys) * rows)], keys + [n ^ k for n in keys]
        k //= 2
    two = pack([near, far], [(0, rows)] * 2)
    rest = pack(got, [(0, g.shape[0]) for g in got], after=[partial[0]])
    raw_keys = [[0], [1, middle], got_keys]
    sources = [columns[0], with_columns(two), with_columns(rest)]
    raw_refs = [x[c] for c in range(ncol) for x in sources]
    raw_gram, *raw = call(
        functools.partial(raw_gram_kernel, nrow, ncol, rows, raw_keys),
        [sds((rows + 8, batch), F32)] + ([sds((batch, half), BF16)] if small else []),
        raw_refs,
        after=[returned[k] for k in order if k],
        scratch=[] if small else [pltpu.VMEM((batch, half), BF16)],
    )
    gram, inverses, squares, *units = call(
        functools.partial(unit_gram_kernel, ncol),
        [sds((rows, batch), F32), sds((rows, 128), F32), sds((8, batch), F32)] + ([sds((batch, half), BF16)] if small else []),
        [raw_gram, other_core(raw_gram)] + raw,
    )
    message, vectors = call(
        functools.partial(sum_kernel, nrow, ncol, order),
        [sds((rows + 8, batch), F32), sds((8, batch), F32)],
        [returned[k] for k in order],
    )
    return call(
        functools.partial(final_kernel, nrow, ncol, None if small else raw_keys),
        sds((rows, half), F32),
        [message, other_core(message), vectors, gram, inverses, squares, student, scale] + (units if small else raw_refs),
        scratch=[] if small else [pltpu.VMEM((batch, half), BF16)],
    )


def solution(mesh):
    spec = P(("groups", "row", "col"), "sub")
    return jax.shard_map(
        shards,
        mesh=mesh,
        in_specs=(spec, spec, P(("groups", "row", "col"))),
        out_specs=spec,
        check_vma=False,
    )
```

```python
import functools

import jax
import jax.numpy as jnp
from jax import lax
from jax.experimental import pallas as pl
from jax.experimental.pallas import tpu as pltpu
from jax.sharding import PartitionSpec as P

F32, BF16 = jnp.float32, jnp.bfloat16
INNER = (((1,), (1,)), ((), ()))
TAIL = 16


def call(body, out_shape, operands, scratch=(), after=()):
    outs = out_shape if isinstance(out_shape, (list, tuple)) else [out_shape]
    moved = sum(x.size * x.dtype.itemsize for x in list(operands) + list(outs))

    def run(*refs):
        body(*refs[: len(operands)], *refs[len(operands) + len(after) :])

    return pl.pallas_call(
        run,
        out_shape=out_shape,
        in_specs=[pl.BlockSpec(memory_space=pltpu.VMEM)] * len(operands) + [pl.BlockSpec(memory_space=pl.ANY)] * len(after),
        out_specs=jax.tree.map(lambda _: pl.BlockSpec(memory_space=pltpu.VMEM), out_shape),
        scratch_shapes=list(scratch),
        cost_estimate=pl.CostEstimate(flops=0, bytes_accessed=0, transcendentals=0),
        compiler_params=pltpu.CompilerParams(vmem_limit_bytes=min(56 << 20, (8 << 20) + 3 * moved)),
    )(*operands, *after)


def column(row):
    shape = (row.shape[1], row.shape[1])
    eye = lax.broadcasted_iota(jnp.int32, shape, 0) == lax.broadcasted_iota(jnp.int32, shape, 1)
    return jnp.sum(jnp.where(eye, row, 0.0), axis=1, keepdims=True)


def tags_of(scales, mass):
    shape = (TAIL, scales.shape[1])
    at = lax.broadcasted_iota(jnp.int32, shape, 0)
    high = mass.astype(BF16).astype(F32)
    return jnp.where(at < 8, scales, jnp.where(at < 12, high, mass - high)).astype(BF16)


def read_tags(tags):
    tags = tags.astype(F32)
    return tags[0:1, :], tags[8:9, 0:1] + tags[12:13, 0:1]


def lane_row(col):
    shape = (col.shape[0], col.shape[0])
    eye = lax.broadcasted_iota(jnp.int32, shape, 0) == lax.broadcasted_iota(jnp.int32, shape, 1)
    return jnp.sum(jnp.where(eye, col, 0.0), axis=0, keepdims=True)


def wide(out, at, piece):
    rows, part = piece.shape
    width = out.shape[1]
    high = rows * part // width
    for n in range(width // part):
        out[at : at + high, n * part : (n + 1) * part] = piece[n * high : (n + 1) * high, :]


def put(held, spot, rows, ref, at):
    width = held.shape[1]
    high = rows * width // ref.shape[1]
    for n in range(ref.shape[1] // width):
        held[pl.ds(spot + n * high, high), :] = ref[at : at + high, n * width : (n + 1) * width]


def cut_kernel(nrow, teach, *outs):
    part = teach.shape[1] // nrow
    z = lax.axis_index("row")
    for k in range(1, nrow):
        at = pl.multiple_of((z ^ k) * part, part)
        outs[k - 1][...] = teach[:, pl.ds(at, part)]


def ride_kernel(stud, piece, out):
    rows = stud.shape[0]
    out[:rows, :] = stud[...]
    wide(out, rows, piece[...])


def own_kernel(nrow, teach, stud, scale, out):
    rows, half = stud.shape
    part = teach.shape[1] // nrow
    ts = teach[...].astype(F32)
    s = scale[...].astype(F32)
    mass = jnp.sum(jnp.square(column(s)) * jnp.sum(ts * ts, axis=1, keepdims=True), keepdims=True)
    tags = tags_of(jnp.concatenate([s, s], axis=1), mass)
    out[:rows, :] = stud[...]
    out[rows : rows + TAIL, :] = jnp.concatenate([tags] * (half // (2 * rows)), axis=1)
    wide(out, rows + TAIL, teach[:, pl.ds(pl.multiple_of(lax.axis_index("row") * part, part), part)])


def take_kernel(rows, ref, out):
    put(out, 0, rows, ref, rows)


def pack_kernel(spans, *refs):
    out, at = refs[-1], 0
    for r, (first, last) in zip(refs[:-1], spans):
        out[at : at + last - first, :] = r[first:last, :]
        at += last - first


def place(nrow, ncol, rows, k, c):
    return pl.multiple_of(((lax.axis_index("row") ^ k) * ncol + c) * rows, rows)


def group_spot(nrow, ncol, rows, k):
    return pl.multiple_of((lax.axis_index("row") ^ k) * ncol * rows, 2 * rows)


def gram_kernel(nrow, ncol, rows, order, *refs):
    count = nrow * ncol
    outs, held, left = refs[count : count + nrow], refs[-2], refs[-1]
    own = order.index(0) * ncol
    for n, k in enumerate(order):
        for c in range(ncol):
            put(held, place(nrow, ncol, rows, k, c), rows, refs[n * ncol + c], 0 if k else rows + TAIL)
    for n, k in enumerate(order):
        left[n * rows : (n + 1) * rows, :] = held[pl.ds(place(nrow, ncol, rows, k, 0), rows), :]
    sub = rows // 2
    at = lax.broadcasted_iota(jnp.int32, (sub, 2 * rows), 0)
    lane = lax.broadcasted_iota(jnp.int32, (sub, 2 * rows), 1)
    note, mass = jnp.zeros((sub, 2 * rows), F32), jnp.zeros((1, 1), F32)
    for c in range(ncol):
        scales, part = read_tags(refs[own + c][rows : rows + TAIL, : 2 * rows])
        turned = jnp.concatenate([scales[:, sub:], scales[:, :sub]], axis=1)
        note = jnp.where(at == 2 * c, scales, jnp.where(at == 2 * c + 1, turned, note))
        mass = mass + part
    high = mass.astype(BF16).astype(F32)
    note = jnp.where(at < sub // 2, note, jnp.where(at < sub * 3 // 4, high, mass - high))
    per = max(1, 2048 * rows * nrow // held.shape[0] // rows // 8)
    for first in range(0, nrow, per):
        last = min(first + per, nrow)
        gram = lax.dot_general(left[first * rows : last * rows, :], held[...], INNER, preferred_element_type=F32)
        for n in range(first, last):
            out = outs[order[n]]
            out[...] = gram[(n - first) * rows : (n - first + 1) * rows, :].astype(out.dtype)
            spot = pl.ds(group_spot(nrow, ncol, rows, order[n]), 2 * rows)
            seen = out[sub:, spot].astype(F32)
            out[sub:, spot] = jnp.where(lane < sub, note, seen).astype(out.dtype)


def assemble(nrow, ncol, rows, keys, refs, held):
    each = len(keys)
    for c in range(ncol):
        for stack, ref in zip(keys, refs[c * each : (c + 1) * each]):
            for n, k in enumerate(stack):
                held[pl.ds(place(nrow, ncol, rows, k, c), rows), :] = ref[n * rows : (n + 1) * rows, :]


def raw_gram_kernel(nrow, ncol, rows, keys, *refs):
    count = len(keys) * ncol
    out, raw = refs[count:]
    assemble(nrow, ncol, rows, keys, refs, raw)
    out[:rows, :] = lax.dot_general(refs[0][:rows, :], raw[...], INNER, preferred_element_type=F32)
    for at in range(0, raw.shape[0], 128):
        squares = jnp.sum(jnp.square(raw[at : at + 128, :].astype(F32)), axis=1, keepdims=True)
        out[rows:, at : at + 128] = jnp.broadcast_to(lane_row(squares), (8, 128))


def message_kernel(nrow, ncol, order, raw_gram, *refs):
    parts, (out, vectors) = [refs[order.index(k)] for k in range(nrow)], refs[-2:]
    rows = parts[0].shape[0]
    sub = rows // 2
    total = parts[0][...].astype(F32)
    for r in parts[1:]:
        total = total + r[...].astype(F32)
    out[:rows, :] = total
    own = pl.ds(group_spot(nrow, ncol, rows, 0), 2 * rows)
    mirror = jnp.transpose(out[:sub, own])[sub : 2 * sub, :]
    out[sub:rows, own] = jnp.concatenate([mirror, out[sub:rows, own][:, sub:]], axis=1)
    mass = jnp.zeros((1, 1), F32)
    for k, part in enumerate(parts):
        note = part[sub:, own].astype(F32)[:, :sub]
        mass = mass + note[sub // 2 : sub // 2 + 1, :1] + note[sub * 3 // 4 : sub * 3 // 4 + 1, :1]
        line = jnp.concatenate([note[n : n + 1, :] for n in range(2 * ncol)], axis=1)
        vectors[:, pl.ds(group_spot(nrow, ncol, rows, k), ncol * rows)] = jnp.broadcast_to(line, (8, ncol * rows))
    out[rows : 2 * rows + 8, :] = raw_gram[...]
    out[2 * rows + 8 :, :] = jnp.broadcast_to(mass, (8, out.shape[1]))


def final_kernel(nrow, ncol, keys, mine, other, vectors, stud, scale, *refs):
    rows = stud.shape[0]
    if keys:
        out, raw, units = refs[-3:]
        assemble(nrow, ncol, rows, keys, refs, raw)
    else:
        raw, out, units = refs
    batch = mine.shape[1]
    squares = mine[2 * rows : 2 * rows + 8, :] + other[2 * rows : 2 * rows + 8, :]
    for at in range(0, batch, 128):
        norm = jnp.sqrt(column(squares[:1, at : at + 128]))
        units[at : at + 128, :] = (raw[at : at + 128, :].astype(F32) / norm).astype(BF16)
    at = pl.ds(group_spot(nrow, ncol, rows, 0), 2 * rows)
    own = (mine[2 * rows : 2 * rows + 8, at] + other[2 * rows : 2 * rows + 8, at])[:1, :rows]
    norm = jnp.sqrt(column(own))
    mass = (mine[2 * rows + 8 : 2 * rows + 9, :1] + other[2 * rows + 8 : 2 * rows + 9, :1]) / batch
    gram = (mine[rows : 2 * rows, :] + other[rows : 2 * rows, :]) / (norm * jnp.sqrt(squares[:1, :]))
    outer = column(scale[...].astype(F32)) * vectors[:1, :]
    error_b = (gram - outer * (mine[:rows, :] + other[:rows, :]) / mass).astype(BF16)
    grads = 4.0 * jnp.dot(error_b, units[...], preferred_element_type=F32)
    along = 4.0 * jnp.sum(error_b.astype(F32) * gram, axis=1, keepdims=True)
    unit = stud[...].astype(F32) / norm
    out[...] = (grads - along * unit) / norm


def shards(student, teacher, scale):
    rows, half = student.shape
    nrow, ncol = lax.axis_size("row"), lax.axis_size("col")
    batch = rows * nrow * ncol
    part = teacher.shape[1] // nrow
    small = batch <= 2048
    sds = jax.ShapeDtypeStruct
    scale = scale.reshape(1, rows)

    def along_row(x, k):
        return lax.ppermute(x, "row", [(i, i ^ k) for i in range(nrow)])

    def along_col(x, c):
        return lax.ppermute(x, "col", [(i, (i - c) % ncol) for i in range(ncol)])

    def other_core(x):
        return lax.ppermute(x, "sub", [(0, 1), (1, 0)])

    def pack(xs, spans, after=()):
        shape = (sum(last - first for first, last in spans), half)
        return call(functools.partial(pack_kernel, spans), sds(shape, BF16), xs, after=after)

    def with_columns(x):
        return [x if c == 0 else along_col(x, c) for c in range(ncol)]

    middle, high = nrow // 2, rows * part // half
    order = list(range(middle, nrow)) + list(range(middle))
    riders = (1, middle)
    cuts = call(functools.partial(cut_kernel, nrow), [sds((rows, part), BF16)] * (nrow - 1), [teacher])
    came = {}
    for k in order:
        if k:
            leaving = cuts[k - 1]
            if k in riders:
                leaving = call(ride_kernel, sds((rows + high, half), BF16), [student, leaving])
            came[k] = along_row(leaving, k)
    own = call(
        functools.partial(own_kernel, nrow),
        sds((rows + TAIL + high, half), BF16),
        [teacher, student, scale],
        after=[came[nrow - 1]],
    )
    columns = {0: with_columns(own)}
    for k in range(1, nrow):
        piece = came[k]
        if k in riders:
            piece = call(functools.partial(take_kernel, rows), sds((rows, part), BF16), [piece])
        columns[k] = with_columns(piece)
    partial = call(
        functools.partial(gram_kernel, nrow, ncol, rows, order),
        [sds((rows, batch), BF16 if k else F32) for k in range(nrow)],
        [columns[k][c] for k in order for c in range(ncol)],
        scratch=[pltpu.VMEM((batch, part), BF16), pltpu.VMEM((nrow * rows, part), BF16)],
    )
    returned = {k: along_row(partial[k], k) if k else partial[0] for k in order}

    near, far = came[1], came[middle]
    stack, keys, k, spans, got, got_keys = [student, far], [0, middle], middle // 2, [(0, rows)] * 2, [], []
    while k:
        first = 1 if k == 1 else 0
        sent = pack(stack[first:], spans[first:])
        got.append(along_row(sent, k))
        got_keys += [n ^ k for n in keys[first:]]
        stack, spans, keys = stack + got[-1:], spans + [(0, len(keys) * rows)], keys + [n ^ k for n in keys]
        k //= 2
    rest = pack([near, far] + got, [(0, rows)] * 2 + [(0, g.shape[0]) for g in got], after=[partial[0]])
    raw_keys = [[0], [1, middle] + got_keys]
    sources = [columns[0], with_columns(rest)]
    raw_refs = [x[c] for c in range(ncol) for x in sources]
    raw_gram, *all_raw = call(
        functools.partial(raw_gram_kernel, nrow, ncol, rows, raw_keys),
        [sds((rows + 8, batch), F32)] + ([sds((batch, half), BF16)] if small else []),
        raw_refs,
        scratch=[] if small else [pltpu.VMEM((batch, half), BF16)],
    )
    message, vectors = call(
        functools.partial(message_kernel, nrow, ncol, order),
        [sds((2 * rows + 16, batch), F32), sds((8, batch), F32)],
        [raw_gram] + [returned[k] for k in order],
    )
    return call(
        functools.partial(final_kernel, nrow, ncol, None if small else raw_keys),
        sds((rows, half), F32),
        [message, other_core(message), vectors, student, scale] + (all_raw if small else raw_refs),
        scratch=([] if small else [pltpu.VMEM((batch, half), BF16)]) + [pltpu.VMEM((batch, half), BF16)],
    )


def solution(mesh):
    spec = P(("groups", "row", "col"), "sub")
    return jax.shard_map(
        shards,
        mesh=mesh,
        in_specs=(spec, spec, P(("groups", "row", "col"))),
        out_specs=spec,
        check_vma=False,
    )
```

```python
import functools

import jax
import jax.numpy as jnp
from jax import lax
from jax.experimental import pallas as pl
from jax.experimental.pallas import tpu as pltpu
from jax.sharding import PartitionSpec as P

F32, BF16 = jnp.float32, jnp.bfloat16
INNER = (((1,), (1,)), ((), ()))
TAIL = 16


def call(body, out_shape, operands, scratch=(), after=()):
    outs = out_shape if isinstance(out_shape, (list, tuple)) else [out_shape]
    moved = sum(x.size * x.dtype.itemsize for x in list(operands) + list(outs))

    def run(*refs):
        body(*refs[: len(operands)], *refs[len(operands) + len(after) :])

    return pl.pallas_call(
        run,
        out_shape=out_shape,
        in_specs=[pl.BlockSpec(memory_space=pltpu.VMEM)] * len(operands) + [pl.BlockSpec(memory_space=pl.ANY)] * len(after),
        out_specs=jax.tree.map(lambda _: pl.BlockSpec(memory_space=pltpu.VMEM), out_shape),
        scratch_shapes=list(scratch),
        cost_estimate=pl.CostEstimate(flops=0, bytes_accessed=0, transcendentals=0),
        compiler_params=pltpu.CompilerParams(vmem_limit_bytes=min(56 << 20, (8 << 20) + 3 * moved)),
    )(*operands, *after)


def column(row):
    shape = (row.shape[1], row.shape[1])
    eye = lax.broadcasted_iota(jnp.int32, shape, 0) == lax.broadcasted_iota(jnp.int32, shape, 1)
    return jnp.sum(jnp.where(eye, row, 0.0), axis=1, keepdims=True)


def tags_of(scales, mass):
    shape = (TAIL, scales.shape[1])
    at = lax.broadcasted_iota(jnp.int32, shape, 0)
    high = mass.astype(BF16).astype(F32)
    return jnp.where(at < 8, scales, jnp.where(at < 12, high, mass - high)).astype(BF16)


def read_tags(tags):
    tags = tags.astype(F32)
    return tags[0:1, :], tags[8:9, 0:1] + tags[12:13, 0:1]


def lane_row(col):
    shape = (col.shape[0], col.shape[0])
    eye = lax.broadcasted_iota(jnp.int32, shape, 0) == lax.broadcasted_iota(jnp.int32, shape, 1)
    return jnp.sum(jnp.where(eye, col, 0.0), axis=0, keepdims=True)


def wide(out, at, piece):
    rows, part = piece.shape
    width = out.shape[1]
    high = rows * part // width
    for n in range(width // part):
        out[at : at + high, n * part : (n + 1) * part] = piece[n * high : (n + 1) * high, :]


def put(held, spot, rows, ref, at):
    width = held.shape[1]
    high = rows * width // ref.shape[1]
    for n in range(ref.shape[1] // width):
        held[pl.ds(spot + n * high, high), :] = ref[at : at + high, n * width : (n + 1) * width]


def cut_kernel(nrow, teach, *outs):
    part = teach.shape[1] // nrow
    z = lax.axis_index("row")
    for k in range(1, nrow):
        at = pl.multiple_of((z ^ k) * part, part)
        outs[k - 1][...] = teach[:, pl.ds(at, part)]


def ride_kernel(stud, piece, out):
    rows = stud.shape[0]
    out[:rows, :] = stud[...]
    wide(out, rows, piece[...])


def own_kernel(nrow, teach, stud, scale, out):
    rows, half = stud.shape
    part = teach.shape[1] // nrow
    ts = teach[...].astype(F32)
    s = scale[...].astype(F32)
    mass = jnp.sum(jnp.square(column(s)) * jnp.sum(ts * ts, axis=1, keepdims=True), keepdims=True)
    tags = tags_of(jnp.concatenate([s, s], axis=1), mass)
    out[:rows, :] = stud[...]
    out[rows : rows + TAIL, :] = jnp.concatenate([tags] * (half // (2 * rows)), axis=1)
    wide(out, rows + TAIL, teach[:, pl.ds(pl.multiple_of(lax.axis_index("row") * part, part), part)])


def take_kernel(rows, ref, out):
    put(out, 0, rows, ref, rows)


def pack_kernel(spans, *refs):
    out, at = refs[-1], 0
    for r, (first, last) in zip(refs[:-1], spans):
        out[at : at + last - first, :] = r[first:last, :]
        at += last - first


def place(nrow, ncol, rows, k, c):
    return pl.multiple_of(((lax.axis_index("row") ^ k) * ncol + c) * rows, rows)


def group_spot(nrow, ncol, rows, k):
    return pl.multiple_of((lax.axis_index("row") ^ k) * ncol * rows, 2 * rows)


def gram_kernel(nrow, ncol, rows, order, *refs):
    count = nrow * ncol
    outs, held, left = refs[count : count + nrow], refs[-2], refs[-1]
    own = order.index(0) * ncol
    for n, k in enumerate(order):
        for c in range(ncol):
            put(held, place(nrow, ncol, rows, k, c), rows, refs[n * ncol + c], 0 if k else rows + TAIL)
    for n, k in enumerate(order):
        left[n * rows : (n + 1) * rows, :] = held[pl.ds(place(nrow, ncol, rows, k, 0), rows), :]
    sub = rows // 2
    at = lax.broadcasted_iota(jnp.int32, (sub, 2 * rows), 0)
    lane = lax.broadcasted_iota(jnp.int32, (sub, 2 * rows), 1)
    note, mass = jnp.zeros((sub, 2 * rows), F32), jnp.zeros((1, 1), F32)
    for c in range(ncol):
        scales, part = read_tags(refs[own + c][rows : rows + TAIL, : 2 * rows])
        turned = jnp.concatenate([scales[:, sub:], scales[:, :sub]], axis=1)
        note = jnp.where(at == 2 * c, scales, jnp.where(at == 2 * c + 1, turned, note))
        mass = mass + part
    high = mass.astype(BF16).astype(F32)
    note = jnp.where(at < sub // 2, note, jnp.where(at < sub * 3 // 4, high, mass - high))
    per = max(1, 2048 * rows * nrow // held.shape[0] // rows // 8)
    for first in range(0, nrow, per):
        last = min(first + per, nrow)
        gram = lax.dot_general(left[first * rows : last * rows, :], held[...], INNER, preferred_element_type=F32)
        for n in range(first, last):
            out = outs[order[n]]
            out[...] = gram[(n - first) * rows : (n - first + 1) * rows, :].astype(out.dtype)
            spot = pl.ds(group_spot(nrow, ncol, rows, order[n]), 2 * rows)
            seen = out[sub:, spot].astype(F32)
            out[sub:, spot] = jnp.where(lane < sub, note, seen).astype(out.dtype)


def assemble(nrow, ncol, rows, keys, refs, held):
    each = len(keys)
    for c in range(ncol):
        for stack, ref in zip(keys, refs[c * each : (c + 1) * each]):
            for n, k in enumerate(stack):
                held[pl.ds(place(nrow, ncol, rows, k, c), rows), :] = ref[n * rows : (n + 1) * rows, :]


def raw_gram_kernel(nrow, ncol, rows, keys, *refs):
    count = len(keys) * ncol
    out, raw = refs[count:]
    assemble(nrow, ncol, rows, keys, refs, raw)
    out[:rows, :] = lax.dot_general(refs[0][:rows, :], raw[...], INNER, preferred_element_type=F32)
    for at in range(0, raw.shape[0], 128):
        squares = jnp.sum(jnp.square(raw[at : at + 128, :].astype(F32)), axis=1, keepdims=True)
        out[rows:, at : at + 128] = jnp.broadcast_to(lane_row(squares), (8, 128))


def message_kernel(nrow, ncol, order, raw_gram, *refs):
    parts, (out, vectors) = [refs[order.index(k)] for k in range(nrow)], refs[-2:]
    rows = parts[0].shape[0]
    sub = rows // 2
    total = parts[0][...].astype(F32)
    for r in parts[1:]:
        total = total + r[...].astype(F32)
    out[:rows, :] = total
    own = pl.ds(group_spot(nrow, ncol, rows, 0), 2 * rows)
    mirror = jnp.transpose(out[:sub, own])[sub : 2 * sub, :]
    out[sub:rows, own] = jnp.concatenate([mirror, out[sub:rows, own][:, sub:]], axis=1)
    mass = jnp.zeros((1, 1), F32)
    for k, part in enumerate(parts):
        note = part[sub:, own].astype(F32)[:, :sub]
        mass = mass + note[sub // 2 : sub // 2 + 1, :1] + note[sub * 3 // 4 : sub * 3 // 4 + 1, :1]
        line = jnp.concatenate([note[n : n + 1, :] for n in range(2 * ncol)], axis=1)
        vectors[:, pl.ds(group_spot(nrow, ncol, rows, k), ncol * rows)] = jnp.broadcast_to(line, (8, ncol * rows))
    out[rows : 2 * rows + 8, :] = raw_gram[...]
    out[2 * rows + 8 :, :] = jnp.broadcast_to(mass, (8, out.shape[1]))


def final_kernel(nrow, ncol, keys, mine, other, vectors, stud, scale, *refs):
    rows = stud.shape[0]
    if keys:
        out, raw, units = refs[-3:]
        assemble(nrow, ncol, rows, keys, refs, raw)
    else:
        raw, out, units = refs
    batch = mine.shape[1]
    squares = mine[2 * rows : 2 * rows + 8, :] + other[2 * rows : 2 * rows + 8, :]
    for at in range(0, batch, 128):
        norm = jnp.sqrt(column(squares[:1, at : at + 128]))
        units[at : at + 128, :] = (raw[at : at + 128, :].astype(F32) / norm).astype(BF16)
    at = pl.ds(group_spot(nrow, ncol, rows, 0), 2 * rows)
    own = (mine[2 * rows : 2 * rows + 8, at] + other[2 * rows : 2 * rows + 8, at])[:1, :rows]
    norm = jnp.sqrt(column(own))
    mass = (mine[2 * rows + 8 : 2 * rows + 9, :1] + other[2 * rows + 8 : 2 * rows + 9, :1]) / batch
    gram = (mine[rows : 2 * rows, :] + other[rows : 2 * rows, :]) / (norm * jnp.sqrt(squares[:1, :]))
    outer = column(scale[...].astype(F32)) * vectors[:1, :]
    error_b = (gram - outer * (mine[:rows, :] + other[:rows, :]) / mass).astype(BF16)
    grads = 4.0 * jnp.dot(error_b, units[...], preferred_element_type=F32)
    along = 4.0 * jnp.sum(error_b.astype(F32) * gram, axis=1, keepdims=True)
    unit = stud[...].astype(F32) / norm
    out[...] = (grads - along * unit) / norm


def shards(student, teacher, scale):
    rows, half = student.shape
    nrow, ncol = lax.axis_size("row"), lax.axis_size("col")
    batch = rows * nrow * ncol
    part = teacher.shape[1] // nrow
    small = batch <= 2048
    sds = jax.ShapeDtypeStruct
    scale = scale.reshape(1, rows)

    def along_row(x, k):
        return lax.ppermute(x, "row", [(i, i ^ k) for i in range(nrow)])

    def along_col(x, c):
        return lax.ppermute(x, "col", [(i, (i - c) % ncol) for i in range(ncol)])

    def other_core(x):
        return lax.ppermute(x, "sub", [(0, 1), (1, 0)])

    def pack(xs, spans, after=()):
        shape = (sum(last - first for first, last in spans), half)
        return call(functools.partial(pack_kernel, spans), sds(shape, BF16), xs, after=after)

    def with_columns(x):
        return [x if c == 0 else along_col(x, c) for c in range(ncol)]

    middle, high = nrow // 2, rows * part // half
    order = list(range(middle, nrow)) + list(range(middle))
    riders = (1, middle)
    cuts = call(functools.partial(cut_kernel, nrow), [sds((rows, part), BF16)] * (nrow - 1), [teacher])
    came = {}
    for k in order:
        if k:
            leaving = cuts[k - 1]
            if k in riders:
                leaving = call(ride_kernel, sds((rows + high, half), BF16), [student, leaving])
            came[k] = along_row(leaving, k)
    own = call(
        functools.partial(own_kernel, nrow),
        sds((rows + TAIL + high, half), BF16),
        [teacher, student, scale],
        after=[came[nrow - 1]],
    )
    columns, taken = {0: with_columns(own)}, ()
    for k in range(1, nrow):
        piece = came[k]
        if k in riders:
            piece = call(functools.partial(take_kernel, rows), sds((rows, part), BF16), [piece], after=taken)
        columns[k] = with_columns(piece)
        if k == 1:
            taken = columns[k][1:2]
    partial = call(
        functools.partial(gram_kernel, nrow, ncol, rows, order),
        [sds((rows, batch), BF16 if k else F32) for k in range(nrow)],
        [columns[k][c] for k in order for c in range(ncol)],
        scratch=[pltpu.VMEM((batch, part), BF16), pltpu.VMEM((nrow * rows, part), BF16)],
    )
    returned = {k: along_row(partial[k], k) if k else partial[0] for k in order}

    near, far = came[1], came[middle]
    stack, keys, k, spans, got, got_keys = [student, far], [0, middle], middle // 2, [(0, rows)] * 2, [], []
    while k:
        first = 1 if k == 1 else 0
        sent = pack(stack[first:], spans[first:])
        got.append(along_row(sent, k))
        got_keys += [n ^ k for n in keys[first:]]
        stack, spans, keys = stack + got[-1:], spans + [(0, len(keys) * rows)], keys + [n ^ k for n in keys]
        k //= 2
    rest = pack([near, far] + got, [(0, rows)] * 2 + [(0, g.shape[0]) for g in got], after=[partial[0]])
    raw_keys = [[0], [1, middle] + got_keys]
    sources = [columns[0], with_columns(rest)]
    raw_refs = [x[c] for c in range(ncol) for x in sources]
    raw_gram, *all_raw = call(
        functools.partial(raw_gram_kernel, nrow, ncol, rows, raw_keys),
        [sds((rows + 8, batch), F32)] + ([sds((batch, half), BF16)] if small else []),
        raw_refs,
        scratch=[] if small else [pltpu.VMEM((batch, half), BF16)],
    )
    message, vectors = call(
        functools.partial(message_kernel, nrow, ncol, order),
        [sds((2 * rows + 16, batch), F32), sds((8, batch), F32)],
        [raw_gram] + [returned[k] for k in order],
    )
    return call(
        functools.partial(final_kernel, nrow, ncol, None if small else raw_keys),
        sds((rows, half), F32),
        [message, other_core(message), vectors, student, scale] + (all_raw if small else raw_refs),
        scratch=([] if small else [pltpu.VMEM((batch, half), BF16)]) + [pltpu.VMEM((batch, half), BF16)],
    )


def solution(mesh):
    spec = P(("groups", "row", "col"), "sub")
    return jax.shard_map(
        shards,
        mesh=mesh,
        in_specs=(spec, spec, P(("groups", "row", "col"))),
        out_specs=spec,
        check_vma=False,
    )
```

```python
import functools

import jax
import jax.numpy as jnp
from jax import lax
from jax.experimental import pallas as pl
from jax.experimental.pallas import tpu as pltpu
from jax.sharding import PartitionSpec as P

F32, BF16 = jnp.float32, jnp.bfloat16
INNER = (((1,), (1,)), ((), ()))
TAIL = 16


def call(body, out_shape, operands, scratch=(), after=()):
    outs = out_shape if isinstance(out_shape, (list, tuple)) else [out_shape]
    moved = sum(x.size * x.dtype.itemsize for x in list(operands) + list(outs))

    def run(*refs):
        body(*refs[: len(operands)], *refs[len(operands) + len(after) :])

    return pl.pallas_call(
        run,
        out_shape=out_shape,
        in_specs=[pl.BlockSpec(memory_space=pltpu.VMEM)] * len(operands) + [pl.BlockSpec(memory_space=pl.ANY)] * len(after),
        out_specs=jax.tree.map(lambda _: pl.BlockSpec(memory_space=pltpu.VMEM), out_shape),
        scratch_shapes=list(scratch),
        cost_estimate=pl.CostEstimate(flops=0, bytes_accessed=0, transcendentals=0),
        compiler_params=pltpu.CompilerParams(vmem_limit_bytes=min(56 << 20, (8 << 20) + 3 * moved)),
    )(*operands, *after)


def column(row):
    shape = (row.shape[1], row.shape[1])
    eye = lax.broadcasted_iota(jnp.int32, shape, 0) == lax.broadcasted_iota(jnp.int32, shape, 1)
    return jnp.sum(jnp.where(eye, row, 0.0), axis=1, keepdims=True)


def tags_of(scales, mass):
    shape = (TAIL, scales.shape[1])
    at = lax.broadcasted_iota(jnp.int32, shape, 0)
    high = mass.astype(BF16).astype(F32)
    return jnp.where(at < 8, scales, jnp.where(at < 12, high, mass - high)).astype(BF16)


def read_tags(tags):
    tags = tags.astype(F32)
    return tags[0:1, :], tags[8:9, 0:1] + tags[12:13, 0:1]


def lane_row(col):
    shape = (col.shape[0], col.shape[0])
    eye = lax.broadcasted_iota(jnp.int32, shape, 0) == lax.broadcasted_iota(jnp.int32, shape, 1)
    return jnp.sum(jnp.where(eye, col, 0.0), axis=0, keepdims=True)


def wide(out, at, piece):
    rows, part = piece.shape
    width = out.shape[1]
    high = rows * part // width
    for n in range(width // part):
        out[at : at + high, n * part : (n + 1) * part] = piece[n * high : (n + 1) * high, :]


def put(held, spot, rows, ref, at):
    width = held.shape[1]
    high = rows * width // ref.shape[1]
    for n in range(ref.shape[1] // width):
        held[pl.ds(spot + n * high, high), :] = ref[at : at + high, n * width : (n + 1) * width]


def cut_kernel(nrow, teach, *outs):
    part = teach.shape[1] // nrow
    z = lax.axis_index("row")
    for k in range(1, nrow):
        at = pl.multiple_of((z ^ k) * part, part)
        outs[k - 1][...] = teach[:, pl.ds(at, part)]


def ride_kernel(stud, *refs):
    rows, count = stud.shape[0], len(refs) // 2
    for piece, out in zip(refs[:count], refs[count:]):
        out[:rows, :] = stud[...]
        wide(out, rows, piece)


def own_kernel(nrow, teach, stud, scale, out):
    rows, half = stud.shape
    part = teach.shape[1] // nrow
    ts = teach[...].astype(F32)
    s = scale[...].astype(F32)
    mass = jnp.sum(jnp.square(column(s)) * jnp.sum(ts * ts, axis=1, keepdims=True), keepdims=True)
    tags = tags_of(jnp.concatenate([s, s], axis=1), mass)
    out[:rows, :] = stud[...]
    out[rows : rows + TAIL, :] = jnp.concatenate([tags] * (half // (2 * rows)), axis=1)
    wide(out, rows + TAIL, teach[:, pl.ds(pl.multiple_of(lax.axis_index("row") * part, part), part)])


def take_kernel(rows, near, far, out):
    put(out, 0, rows, near, rows)
    put(out, rows, rows, far, rows)


def pack_kernel(spans, *refs):
    out, at = refs[-1], 0
    for r, (first, last) in zip(refs[:-1], spans):
        out[at : at + last - first, :] = r[first:last, :]
        at += last - first


def place(nrow, ncol, rows, k, c):
    return pl.multiple_of(((lax.axis_index("row") ^ k) * ncol + c) * rows, rows)


def group_spot(nrow, ncol, rows, k):
    return pl.multiple_of((lax.axis_index("row") ^ k) * ncol * rows, 2 * rows)


def gram_kernel(nrow, ncol, rows, order, *refs):
    count = nrow * ncol
    outs, held, left = refs[count : count + nrow], refs[-2], refs[-1]
    own = order.index(0) * ncol
    for n, k in enumerate(order):
        for c in range(ncol):
            put(held, place(nrow, ncol, rows, k, c), rows, refs[n * ncol + c], {0: rows + TAIL, nrow // 2: rows}.get(k, 0))
    for n, k in enumerate(order):
        left[n * rows : (n + 1) * rows, :] = held[pl.ds(place(nrow, ncol, rows, k, 0), rows), :]
    sub = rows // 2
    at = lax.broadcasted_iota(jnp.int32, (sub, 2 * rows), 0)
    lane = lax.broadcasted_iota(jnp.int32, (sub, 2 * rows), 1)
    note, mass = jnp.zeros((sub, 2 * rows), F32), jnp.zeros((1, 1), F32)
    for c in range(ncol):
        scales, part = read_tags(refs[own + c][rows : rows + TAIL, : 2 * rows])
        turned = jnp.concatenate([scales[:, sub:], scales[:, :sub]], axis=1)
        note = jnp.where(at == 2 * c, scales, jnp.where(at == 2 * c + 1, turned, note))
        mass = mass + part
    high = mass.astype(BF16).astype(F32)
    note = jnp.where(at < sub // 2, note, jnp.where(at < sub * 3 // 4, high, mass - high))
    per = max(1, 2048 * rows * nrow // held.shape[0] // rows // 8)
    for first in range(0, nrow, per):
        last = min(first + per, nrow)
        gram = lax.dot_general(left[first * rows : last * rows, :], held[...], INNER, preferred_element_type=F32)
        for n in range(first, last):
            out = outs[order[n]]
            out[...] = gram[(n - first) * rows : (n - first + 1) * rows, :].astype(out.dtype)
            spot = pl.ds(group_spot(nrow, ncol, rows, order[n]), 2 * rows)
            seen = out[sub:, spot].astype(F32)
            out[sub:, spot] = jnp.where(lane < sub, note, seen).astype(out.dtype)


def assemble(nrow, ncol, rows, keys, refs, held):
    each = len(keys)
    for c in range(ncol):
        for stack, ref in zip(keys, refs[c * each : (c + 1) * each]):
            for n, k in enumerate(stack):
                held[pl.ds(place(nrow, ncol, rows, k, c), rows), :] = ref[n * rows : (n + 1) * rows, :]


def raw_gram_kernel(nrow, ncol, rows, keys, *refs):
    count = len(keys) * ncol
    out, raw = refs[count:]
    assemble(nrow, ncol, rows, keys, refs, raw)
    out[:rows, :] = lax.dot_general(refs[0][:rows, :], raw[...], INNER, preferred_element_type=F32)
    for at in range(0, raw.shape[0], 128):
        squares = jnp.sum(jnp.square(raw[at : at + 128, :].astype(F32)), axis=1, keepdims=True)
        out[rows:, at : at + 128] = jnp.broadcast_to(lane_row(squares), (8, 128))


def message_kernel(nrow, ncol, order, raw_gram, *refs):
    parts, (out, vectors) = [refs[order.index(k)] for k in range(nrow)], refs[-2:]
    rows = parts[0].shape[0]
    sub = rows // 2
    total = parts[0][...].astype(F32)
    for r in parts[1:]:
        total = total + r[...].astype(F32)
    out[:rows, :] = total
    own = pl.ds(group_spot(nrow, ncol, rows, 0), 2 * rows)
    mirror = jnp.transpose(out[:sub, own])[sub : 2 * sub, :]
    out[sub:rows, own] = jnp.concatenate([mirror, out[sub:rows, own][:, sub:]], axis=1)
    mass = jnp.zeros((1, 1), F32)
    for k, part in enumerate(parts):
        note = part[sub:, own].astype(F32)[:, :sub]
        mass = mass + note[sub // 2 : sub // 2 + 1, :1] + note[sub * 3 // 4 : sub * 3 // 4 + 1, :1]
        line = jnp.concatenate([note[n : n + 1, :] for n in range(2 * ncol)], axis=1)
        vectors[:, pl.ds(group_spot(nrow, ncol, rows, k), ncol * rows)] = jnp.broadcast_to(line, (8, ncol * rows))
    out[rows : 2 * rows + 8, :] = raw_gram[...]
    out[2 * rows + 8 :, :] = jnp.broadcast_to(mass, (8, out.shape[1]))


def final_kernel(nrow, ncol, keys, mine, other, vectors, stud, scale, *refs):
    rows = stud.shape[0]
    if keys:
        out, raw, units = refs[-3:]
        assemble(nrow, ncol, rows, keys, refs, raw)
    else:
        raw, out, units = refs
    batch = mine.shape[1]
    squares = mine[2 * rows : 2 * rows + 8, :] + other[2 * rows : 2 * rows + 8, :]
    for at in range(0, batch, 128):
        norm = jnp.sqrt(column(squares[:1, at : at + 128]))
        units[at : at + 128, :] = (raw[at : at + 128, :].astype(F32) / norm).astype(BF16)
    at = pl.ds(group_spot(nrow, ncol, rows, 0), 2 * rows)
    own = (mine[2 * rows : 2 * rows + 8, at] + other[2 * rows : 2 * rows + 8, at])[:1, :rows]
    norm = jnp.sqrt(column(own))
    mass = (mine[2 * rows + 8 : 2 * rows + 9, :1] + other[2 * rows + 8 : 2 * rows + 9, :1]) / batch
    gram = (mine[rows : 2 * rows, :] + other[rows : 2 * rows, :]) / (norm * jnp.sqrt(squares[:1, :]))
    outer = column(scale[...].astype(F32)) * vectors[:1, :]
    error_b = (gram - outer * (mine[:rows, :] + other[:rows, :]) / mass).astype(BF16)
    grads = 4.0 * jnp.dot(error_b, units[...], preferred_element_type=F32)
    along = 4.0 * jnp.sum(error_b.astype(F32) * gram, axis=1, keepdims=True)
    unit = stud[...].astype(F32) / norm
    out[...] = (grads - along * unit) / norm


def shards(student, teacher, scale):
    rows, half = student.shape
    nrow, ncol = lax.axis_size("row"), lax.axis_size("col")
    batch = rows * nrow * ncol
    part = teacher.shape[1] // nrow
    small = batch <= 2048
    sds = jax.ShapeDtypeStruct
    scale = scale.reshape(1, rows)

    def along_row(x, k):
        return lax.ppermute(x, "row", [(i, i ^ k) for i in range(nrow)])

    def along_col(x, c):
        return lax.ppermute(x, "col", [(i, (i - c) % ncol) for i in range(ncol)])

    def other_core(x):
        return lax.ppermute(x, "sub", [(0, 1), (1, 0)])

    def pack(xs, spans, after=()):
        shape = (sum(last - first for first, last in spans), half)
        return call(functools.partial(pack_kernel, spans), sds(shape, BF16), xs, after=after)

    def with_columns(x):
        return [x if c == 0 else along_col(x, c) for c in range(ncol)]

    middle, high = nrow // 2, rows * part // half
    order = list(range(middle, nrow)) + list(range(middle))
    riders = (1, middle)
    cuts = call(functools.partial(cut_kernel, nrow), [sds((rows, part), BF16)] * (nrow - 1), [teacher])
    ridden = call(ride_kernel, [sds((rows + high, half), BF16)] * 2, [student] + [cuts[k - 1] for k in riders])
    leaving = dict(enumerate(cuts, 1)) | dict(zip(riders, ridden))
    came = {k: along_row(leaving[k], k) for k in order if k}
    own = call(
        functools.partial(own_kernel, nrow),
        sds((rows + TAIL + high, half), BF16),
        [teacher, student, scale],
        after=[came[nrow - 1]],
    )
    columns = {0: with_columns(own)}
    pair = call(functools.partial(take_kernel, rows), sds((2 * rows, part), BF16), [came[k] for k in riders])
    pair = with_columns(pair)
    for k in range(1, nrow):
        columns[k] = pair if k in riders else with_columns(came[k])
    partial = call(
        functools.partial(gram_kernel, nrow, ncol, rows, order),
        [sds((rows, batch), BF16 if k else F32) for k in range(nrow)],
        [columns[k][c] for k in order for c in range(ncol)],
        scratch=[pltpu.VMEM((batch, part), BF16), pltpu.VMEM((nrow * rows, part), BF16)],
    )
    returned = {k: along_row(partial[k], k) if k else partial[0] for k in order}

    near, far = came[1], came[middle]
    stack, keys, k, spans, got, got_keys = [student, far], [0, middle], middle // 2, [(0, rows)] * 2, [], []
    while k:
        first = 1 if k == 1 else 0
        sent = pack(stack[first:], spans[first:])
        got.append(along_row(sent, k))
        got_keys += [n ^ k for n in keys[first:]]
        stack, spans, keys = stack + got[-1:], spans + [(0, len(keys) * rows)], keys + [n ^ k for n in keys]
        k //= 2
    rest = pack([near, far] + got, [(0, rows)] * 2 + [(0, g.shape[0]) for g in got], after=[partial[0]])
    raw_keys = [[0], [1, middle] + got_keys]
    sources = [columns[0], with_columns(rest)]
    raw_refs = [x[c] for c in range(ncol) for x in sources]
    raw_gram, *all_raw = call(
        functools.partial(raw_gram_kernel, nrow, ncol, rows, raw_keys),
        [sds((rows + 8, batch), F32)] + ([sds((batch, half), BF16)] if small else []),
        raw_refs,
        scratch=[] if small else [pltpu.VMEM((batch, half), BF16)],
    )
    message, vectors = call(
        functools.partial(message_kernel, nrow, ncol, order),
        [sds((2 * rows + 16, batch), F32), sds((8, batch), F32)],
        [raw_gram] + [returned[k] for k in order],
    )
    return call(
        functools.partial(final_kernel, nrow, ncol, None if small else raw_keys),
        sds((rows, half), F32),
        [message, other_core(message), vectors, student, scale] + (all_raw if small else raw_refs),
        scratch=([] if small else [pltpu.VMEM((batch, half), BF16)]) + [pltpu.VMEM((batch, half), BF16)],
    )


def solution(mesh):
    spec = P(("groups", "row", "col"), "sub")
    return jax.shard_map(
        shards,
        mesh=mesh,
        in_specs=(spec, spec, P(("groups", "row", "col"))),
        out_specs=spec,
        check_vma=False,
    )
```

```python
import functools

import jax
import jax.numpy as jnp
from jax import lax
from jax.experimental import pallas as pl
from jax.experimental.pallas import tpu as pltpu
from jax.sharding import PartitionSpec as P

F32, BF16 = jnp.float32, jnp.bfloat16
INNER = (((1,), (1,)), ((), ()))
TAIL = 16


def call(body, out_shape, operands, scratch=(), after=()):
    outs = out_shape if isinstance(out_shape, (list, tuple)) else [out_shape]
    moved = sum(x.size * x.dtype.itemsize for x in list(operands) + list(outs))

    def run(*refs):
        body(*refs[: len(operands)], *refs[len(operands) + len(after) :])

    return pl.pallas_call(
        run,
        out_shape=out_shape,
        in_specs=[pl.BlockSpec(memory_space=pltpu.VMEM)] * len(operands) + [pl.BlockSpec(memory_space=pl.ANY)] * len(after),
        out_specs=jax.tree.map(lambda _: pl.BlockSpec(memory_space=pltpu.VMEM), out_shape),
        scratch_shapes=list(scratch),
        cost_estimate=pl.CostEstimate(flops=0, bytes_accessed=0, transcendentals=0),
        compiler_params=pltpu.CompilerParams(vmem_limit_bytes=min(56 << 20, (8 << 20) + 3 * moved)),
    )(*operands, *after)


def column(row):
    shape = (row.shape[1], row.shape[1])
    eye = lax.broadcasted_iota(jnp.int32, shape, 0) == lax.broadcasted_iota(jnp.int32, shape, 1)
    return jnp.sum(jnp.where(eye, row, 0.0), axis=1, keepdims=True)


def tags_of(scales, mass):
    shape = (TAIL, scales.shape[1])
    at = lax.broadcasted_iota(jnp.int32, shape, 0)
    high = mass.astype(BF16).astype(F32)
    return jnp.where(at < 8, scales, jnp.where(at < 12, high, mass - high)).astype(BF16)


def read_tags(tags):
    tags = tags.astype(F32)
    return tags[0:1, :], tags[8:9, 0:1] + tags[12:13, 0:1]


def lane_row(col):
    shape = (col.shape[0], col.shape[0])
    eye = lax.broadcasted_iota(jnp.int32, shape, 0) == lax.broadcasted_iota(jnp.int32, shape, 1)
    return jnp.sum(jnp.where(eye, col, 0.0), axis=0, keepdims=True)


def wide(out, at, piece):
    rows, part = piece.shape
    width = out.shape[1]
    high = rows * part // width
    for n in range(width // part):
        out[at : at + high, n * part : (n + 1) * part] = piece[n * high : (n + 1) * high, :]


def put(held, spot, rows, ref, at):
    width = held.shape[1]
    high = rows * width // ref.shape[1]
    for n in range(ref.shape[1] // width):
        held[pl.ds(spot + n * high, high), :] = ref[at : at + high, n * width : (n + 1) * width]


def cut_kernel(nrow, teach, *outs):
    part = teach.shape[1] // nrow
    z = lax.axis_index("row")
    for k in range(1, nrow):
        at = pl.multiple_of((z ^ k) * part, part)
        outs[k - 1][...] = teach[:, pl.ds(at, part)]


def ride_kernel(stud, *refs):
    rows, count = stud.shape[0], len(refs) // 2
    for piece, out in zip(refs[:count], refs[count:]):
        out[:rows, :] = stud[...]
        wide(out, rows, piece)


def own_kernel(nrow, teach, stud, scale, out):
    rows, half = stud.shape
    part = teach.shape[1] // nrow
    ts = teach[...].astype(F32)
    s = scale[...].astype(F32)
    mass = jnp.sum(jnp.square(column(s)) * jnp.sum(ts * ts, axis=1, keepdims=True), keepdims=True)
    tags = tags_of(jnp.concatenate([s, s], axis=1), mass)
    out[:rows, :] = stud[...]
    out[rows : rows + TAIL, :] = jnp.concatenate([tags] * (half // (2 * rows)), axis=1)
    wide(out, rows + TAIL, teach[:, pl.ds(pl.multiple_of(lax.axis_index("row") * part, part), part)])


def take_kernel(rows, near, far, out):
    put(out, 0, rows, near, rows)
    put(out, rows, rows, far, rows)


def pack_kernel(spans, *refs):
    out, at = refs[-1], 0
    for r, (first, last) in zip(refs[:-1], spans):
        out[at : at + last - first, :] = r[first:last, :]
        at += last - first


def place(nrow, ncol, rows, k, c):
    return pl.multiple_of(((lax.axis_index("row") ^ k) * ncol + c) * rows, rows)


def group_spot(nrow, ncol, rows, k):
    return pl.multiple_of((lax.axis_index("row") ^ k) * ncol * rows, 2 * rows)


def gram_kernel(nrow, ncol, rows, order, *refs):
    count = nrow * ncol
    outs, held, left = refs[count : count + nrow], refs[-2], refs[-1]
    own = order.index(0) * ncol
    for n, k in enumerate(order):
        for c in range(ncol):
            put(held, place(nrow, ncol, rows, k, c), rows, refs[n * ncol + c], {0: rows + TAIL, nrow // 2: rows}.get(k, 0))
    for n, k in enumerate(order):
        left[n * rows : (n + 1) * rows, :] = held[pl.ds(place(nrow, ncol, rows, k, 0), rows), :]
    sub = rows // 2
    at = lax.broadcasted_iota(jnp.int32, (sub, 2 * rows), 0)
    lane = lax.broadcasted_iota(jnp.int32, (sub, 2 * rows), 1)
    note, mass = jnp.zeros((sub, 2 * rows), F32), jnp.zeros((1, 1), F32)
    for c in range(ncol):
        scales, part = read_tags(refs[own + c][rows : rows + TAIL, : 2 * rows])
        turned = jnp.concatenate([scales[:, sub:], scales[:, :sub]], axis=1)
        note = jnp.where(at == 2 * c, scales, jnp.where(at == 2 * c + 1, turned, note))
        mass = mass + part
    high = mass.astype(BF16).astype(F32)
    note = jnp.where(at < sub // 2, note, jnp.where(at < sub * 3 // 4, high, mass - high))
    per = max(1, 2048 * rows * nrow // held.shape[0] // rows // 8)
    for first in range(0, nrow, per):
        last = min(first + per, nrow)
        gram = lax.dot_general(left[first * rows : last * rows, :], held[...], INNER, preferred_element_type=F32)
        for n in range(first, last):
            out = outs[order[n]]
            out[...] = gram[(n - first) * rows : (n - first + 1) * rows, :].astype(out.dtype)
            spot = pl.ds(group_spot(nrow, ncol, rows, order[n]), 2 * rows)
            seen = out[sub:, spot].astype(F32)
            out[sub:, spot] = jnp.where(lane < sub, note, seen).astype(out.dtype)


def assemble(nrow, ncol, rows, keys, refs, held):
    each = len(keys)
    for c in range(ncol):
        for stack, ref in zip(keys, refs[c * each : (c + 1) * each]):
            for n, k in enumerate(stack):
                held[pl.ds(place(nrow, ncol, rows, k, c), rows), :] = ref[n * rows : (n + 1) * rows, :]


def raw_gram_kernel(nrow, ncol, rows, keys, *refs):
    count = len(keys) * ncol
    out, raw = refs[count:]
    assemble(nrow, ncol, rows, keys, refs, raw)
    out[:rows, :] = lax.dot_general(refs[0][:rows, :], raw[...], INNER, preferred_element_type=F32)
    for at in range(0, raw.shape[0], 128):
        squares = jnp.sum(jnp.square(raw[at : at + 128, :].astype(F32)), axis=1, keepdims=True)
        out[rows:, at : at + 128] = jnp.broadcast_to(lane_row(squares), (8, 128))


def message_kernel(nrow, ncol, order, raw_gram, *refs):
    parts, (out, vectors) = [refs[order.index(k)] for k in range(nrow)], refs[-2:]
    rows = parts[0].shape[0]
    sub = rows // 2
    total = parts[0][...].astype(F32)
    for r in parts[1:]:
        total = total + r[...].astype(F32)
    out[:rows, :] = total
    own = pl.ds(group_spot(nrow, ncol, rows, 0), 2 * rows)
    mirror = jnp.transpose(out[:sub, own])[sub : 2 * sub, :]
    out[sub:rows, own] = jnp.concatenate([mirror, out[sub:rows, own][:, sub:]], axis=1)
    mass = jnp.zeros((1, 1), F32)
    for k, part in enumerate(parts):
        note = part[sub:, own].astype(F32)[:, :sub]
        mass = mass + note[sub // 2 : sub // 2 + 1, :1] + note[sub * 3 // 4 : sub * 3 // 4 + 1, :1]
        line = jnp.concatenate([note[n : n + 1, :] for n in range(2 * ncol)], axis=1)
        vectors[:, pl.ds(group_spot(nrow, ncol, rows, k), ncol * rows)] = jnp.broadcast_to(line, (8, ncol * rows))
    out[rows : 2 * rows + 8, :] = raw_gram[...]
    out[2 * rows + 8 :, :] = jnp.broadcast_to(mass, (8, out.shape[1]))


def final_kernel(nrow, ncol, keys, mine, other, vectors, stud, scale, *refs):
    rows = stud.shape[0]
    if keys:
        out, raw, units = refs[-3:]
        assemble(nrow, ncol, rows, keys, refs, raw)
    else:
        raw, out, units = refs
    batch = mine.shape[1]
    squares = mine[2 * rows : 2 * rows + 8, :] + other[2 * rows : 2 * rows + 8, :]
    for at in range(0, batch, 128):
        norm = jnp.sqrt(column(squares[:1, at : at + 128]))
        units[at : at + 128, :] = (raw[at : at + 128, :].astype(F32) / norm).astype(BF16)
    at = pl.ds(group_spot(nrow, ncol, rows, 0), 2 * rows)
    own = (mine[2 * rows : 2 * rows + 8, at] + other[2 * rows : 2 * rows + 8, at])[:1, :rows]
    norm = jnp.sqrt(column(own))
    mass = (mine[2 * rows + 8 : 2 * rows + 9, :1] + other[2 * rows + 8 : 2 * rows + 9, :1]) / batch
    gram = (mine[rows : 2 * rows, :] + other[rows : 2 * rows, :]) / (norm * jnp.sqrt(squares[:1, :]))
    outer = column(scale[...].astype(F32)) * vectors[:1, :]
    error_b = (gram - outer * (mine[:rows, :] + other[:rows, :]) / mass).astype(BF16)
    grads = 4.0 * jnp.dot(error_b, units[...], preferred_element_type=F32)
    along = 4.0 * jnp.sum(error_b.astype(F32) * gram, axis=1, keepdims=True)
    unit = stud[...].astype(F32) / norm
    out[...] = (grads - along * unit) / norm


def shards(student, teacher, scale):
    rows, half = student.shape
    nrow, ncol = lax.axis_size("row"), lax.axis_size("col")
    batch = rows * nrow * ncol
    part = teacher.shape[1] // nrow
    small = batch <= 2048
    sds = jax.ShapeDtypeStruct
    scale = scale.reshape(1, rows)

    def along_row(x, k):
        return lax.ppermute(x, "row", [(i, i ^ k) for i in range(nrow)])

    def along_col(x, c):
        return lax.ppermute(x, "col", [(i, (i - c) % ncol) for i in range(ncol)])

    def other_core(x):
        return lax.ppermute(x, "sub", [(0, 1), (1, 0)])

    def pack(xs, spans, after=()):
        shape = (sum(last - first for first, last in spans), half)
        return call(functools.partial(pack_kernel, spans), sds(shape, BF16), xs, after=after)

    def with_columns(x):
        return [x if c == 0 else along_col(x, c) for c in range(ncol)]

    middle, high = nrow // 2, rows * part // half
    order = list(range(middle, nrow)) + list(range(middle))
    riders = (1, middle)
    cuts = call(functools.partial(cut_kernel, nrow), [sds((rows, part), BF16)] * (nrow - 1), [teacher])
    ridden = call(ride_kernel, [sds((rows + high, half), BF16)] * 2, [student] + [cuts[k - 1] for k in riders])
    leaving = dict(enumerate(cuts, 1)) | dict(zip(riders, ridden))
    came = {k: along_row(leaving[k], k) for k in order if k}
    own = call(
        functools.partial(own_kernel, nrow),
        sds((rows + TAIL + high, half), BF16),
        [teacher, student, scale],
        after=[],
    )
    columns = {0: with_columns(own)}
    pair = call(functools.partial(take_kernel, rows), sds((2 * rows, part), BF16), [came[k] for k in riders])
    pair = with_columns(pair)
    for k in range(1, nrow):
        columns[k] = pair if k in riders else with_columns(came[k])
    partial = call(
        functools.partial(gram_kernel, nrow, ncol, rows, order),
        [sds((rows, batch), BF16 if k else F32) for k in range(nrow)],
        [columns[k][c] for k in order for c in range(ncol)],
        scratch=[pltpu.VMEM((batch, part), BF16), pltpu.VMEM((nrow * rows, part), BF16)],
    )
    returned = {k: along_row(partial[k], k) if k else partial[0] for k in order}

    near, far = came[1], came[middle]
    stack, keys, k, spans, got, got_keys = [student, far], [0, middle], middle // 2, [(0, rows)] * 2, [], []
    while k:
        first = 1 if k == 1 else 0
        sent = pack(stack[first:], spans[first:])
        got.append(along_row(sent, k))
        got_keys += [n ^ k for n in keys[first:]]
        stack, spans, keys = stack + got[-1:], spans + [(0, len(keys) * rows)], keys + [n ^ k for n in keys]
        k //= 2
    rest = pack([near, far] + got, [(0, rows)] * 2 + [(0, g.shape[0]) for g in got], after=[partial[0]])
    raw_keys = [[0], [1, middle] + got_keys]
    sources = [columns[0], with_columns(rest)]
    raw_refs = [x[c] for c in range(ncol) for x in sources]
    raw_gram, *all_raw = call(
        functools.partial(raw_gram_kernel, nrow, ncol, rows, raw_keys),
        [sds((rows + 8, batch), F32)] + ([sds((batch, half), BF16)] if small else []),
        raw_refs,
        scratch=[] if small else [pltpu.VMEM((batch, half), BF16)],
    )
    message, vectors = call(
        functools.partial(message_kernel, nrow, ncol, order),
        [sds((2 * rows + 16, batch), F32), sds((8, batch), F32)],
        [raw_gram] + [returned[k] for k in order],
    )
    return call(
        functools.partial(final_kernel, nrow, ncol, None if small else raw_keys),
        sds((rows, half), F32),
        [message, other_core(message), vectors, student, scale] + (all_raw if small else raw_refs),
        scratch=([] if small else [pltpu.VMEM((batch, half), BF16)]) + [pltpu.VMEM((batch, half), BF16)],
    )


def solution(mesh):
    spec = P(("groups", "row", "col"), "sub")
    return jax.shard_map(
        shards,
        mesh=mesh,
        in_specs=(spec, spec, P(("groups", "row", "col"))),
        out_specs=spec,
        check_vma=False,
    )
```

```python
import functools

import jax
import jax.numpy as jnp
from jax import lax
from jax.experimental import pallas as pl
from jax.experimental.pallas import tpu as pltpu
from jax.sharding import PartitionSpec as P

F32, BF16 = jnp.float32, jnp.bfloat16
INNER = (((1,), (1,)), ((), ()))
TAIL = 16


def call(body, out_shape, operands, scratch=(), after=()):
    outs = out_shape if isinstance(out_shape, (list, tuple)) else [out_shape]
    moved = sum(x.size * x.dtype.itemsize for x in list(operands) + list(outs))

    def run(*refs):
        body(*refs[: len(operands)], *refs[len(operands) + len(after) :])

    return pl.pallas_call(
        run,
        out_shape=out_shape,
        in_specs=[pl.BlockSpec(memory_space=pltpu.VMEM)] * len(operands) + [pl.BlockSpec(memory_space=pl.ANY)] * len(after),
        out_specs=jax.tree.map(lambda _: pl.BlockSpec(memory_space=pltpu.VMEM), out_shape),
        scratch_shapes=list(scratch),
        cost_estimate=pl.CostEstimate(flops=0, bytes_accessed=0, transcendentals=0),
        compiler_params=pltpu.CompilerParams(vmem_limit_bytes=min(56 << 20, (8 << 20) + 3 * moved)),
    )(*operands, *after)


def column(row):
    shape = (row.shape[1], row.shape[1])
    eye = lax.broadcasted_iota(jnp.int32, shape, 0) == lax.broadcasted_iota(jnp.int32, shape, 1)
    return jnp.sum(jnp.where(eye, row, 0.0), axis=1, keepdims=True)


def tags_of(scales, mass):
    shape = (TAIL, scales.shape[1])
    at = lax.broadcasted_iota(jnp.int32, shape, 0)
    high = mass.astype(BF16).astype(F32)
    return jnp.where(at < 8, scales, jnp.where(at < 12, high, mass - high)).astype(BF16)


def read_tags(tags):
    tags = tags.astype(F32)
    return tags[0:1, :], tags[8:9, 0:1] + tags[12:13, 0:1]


def lane_row(col):
    shape = (col.shape[0], col.shape[0])
    eye = lax.broadcasted_iota(jnp.int32, shape, 0) == lax.broadcasted_iota(jnp.int32, shape, 1)
    return jnp.sum(jnp.where(eye, col, 0.0), axis=0, keepdims=True)


def wide(out, at, piece):
    rows, part = piece.shape
    width = out.shape[1]
    high = rows * part // width
    for n in range(width // part):
        out[at : at + high, n * part : (n + 1) * part] = piece[n * high : (n + 1) * high, :]


def put(held, spot, rows, ref, at):
    width = held.shape[1]
    high = rows * width // ref.shape[1]
    for n in range(ref.shape[1] // width):
        held[pl.ds(spot + n * high, high), :] = ref[at : at + high, n * width : (n + 1) * width]


def cut_kernel(nrow, teach, *outs):
    part = teach.shape[1] // nrow
    z = lax.axis_index("row")
    for k in range(1, nrow):
        at = pl.multiple_of((z ^ k) * part, part)
        outs[k - 1][...] = teach[:, pl.ds(at, part)]


def ride_kernel(stud, *refs):
    rows, count = stud.shape[0], len(refs) // 2
    for piece, out in zip(refs[:count], refs[count:]):
        out[:rows, :] = stud[...]
        wide(out, rows, piece)


def own_kernel(nrow, teach, stud, scale, out):
    rows, half = stud.shape
    part = teach.shape[1] // nrow
    ts = teach[...].astype(F32)
    s = scale[...].astype(F32)
    mass = jnp.sum(jnp.square(column(s)) * jnp.sum(ts * ts, axis=1, keepdims=True), keepdims=True)
    tags = tags_of(jnp.concatenate([s, s], axis=1), mass)
    out[:rows, :] = stud[...]
    out[rows : rows + TAIL, :] = jnp.concatenate([tags] * (half // (2 * rows)), axis=1)
    wide(out, rows + TAIL, teach[:, pl.ds(pl.multiple_of(lax.axis_index("row") * part, part), part)])


def take_kernel(rows, ref, out):
    put(out, 0, rows, ref, rows)


def pack_kernel(spans, *refs):
    out, at = refs[-1], 0
    for r, (first, last) in zip(refs[:-1], spans):
        out[at : at + last - first, :] = r[first:last, :]
        at += last - first


def place(nrow, ncol, rows, k, c):
    return pl.multiple_of(((lax.axis_index("row") ^ k) * ncol + c) * rows, rows)


def group_spot(nrow, ncol, rows, k):
    return pl.multiple_of((lax.axis_index("row") ^ k) * ncol * rows, 2 * rows)


def gram_kernel(nrow, ncol, rows, order, *refs):
    count = nrow * ncol
    outs, held, left = refs[count : count + nrow], refs[-2], refs[-1]
    own = order.index(0) * ncol
    for n, k in enumerate(order):
        for c in range(ncol):
            put(held, place(nrow, ncol, rows, k, c), rows, refs[n * ncol + c], 0 if k else rows + TAIL)
    for n, k in enumerate(order):
        left[n * rows : (n + 1) * rows, :] = held[pl.ds(place(nrow, ncol, rows, k, 0), rows), :]
    sub = rows // 2
    at = lax.broadcasted_iota(jnp.int32, (sub, 2 * rows), 0)
    lane = lax.broadcasted_iota(jnp.int32, (sub, 2 * rows), 1)
    note, mass = jnp.zeros((sub, 2 * rows), F32), jnp.zeros((1, 1), F32)
    for c in range(ncol):
        scales, part = read_tags(refs[own + c][rows : rows + TAIL, : 2 * rows])
        turned = jnp.concatenate([scales[:, sub:], scales[:, :sub]], axis=1)
        note = jnp.where(at == 2 * c, scales, jnp.where(at == 2 * c + 1, turned, note))
        mass = mass + part
    high = mass.astype(BF16).astype(F32)
    note = jnp.where(at < sub // 2, note, jnp.where(at < sub * 3 // 4, high, mass - high))
    per = max(1, 2048 * rows * nrow // held.shape[0] // rows // 8)
    for first in range(0, nrow, per):
        last = min(first + per, nrow)
        gram = lax.dot_general(left[first * rows : last * rows, :], held[...], INNER, preferred_element_type=F32)
        for n in range(first, last):
            out = outs[order[n]]
            out[...] = gram[(n - first) * rows : (n - first + 1) * rows, :].astype(out.dtype)
            spot = pl.ds(group_spot(nrow, ncol, rows, order[n]), 2 * rows)
            seen = out[sub:, spot].astype(F32)
            out[sub:, spot] = jnp.where(lane < sub, note, seen).astype(out.dtype)


def assemble(nrow, ncol, rows, keys, refs, held):
    each = len(keys)
    for c in range(ncol):
        for stack, ref in zip(keys, refs[c * each : (c + 1) * each]):
            for n, k in enumerate(stack):
                held[pl.ds(place(nrow, ncol, rows, k, c), rows), :] = ref[n * rows : (n + 1) * rows, :]


def raw_gram_kernel(nrow, ncol, rows, keys, *refs):
    count = len(keys) * ncol
    out, raw = refs[count:]
    assemble(nrow, ncol, rows, keys, refs, raw)
    out[:rows, :] = lax.dot_general(refs[0][:rows, :], raw[...], INNER, preferred_element_type=F32)
    for at in range(0, raw.shape[0], 128):
        squares = jnp.sum(jnp.square(raw[at : at + 128, :].astype(F32)), axis=1, keepdims=True)
        out[rows:, at : at + 128] = jnp.broadcast_to(lane_row(squares), (8, 128))


def message_kernel(nrow, ncol, order, raw_gram, *refs):
    parts, (out, vectors) = [refs[order.index(k)] for k in range(nrow)], refs[-2:]
    rows = parts[0].shape[0]
    sub = rows // 2
    total = parts[0][...].astype(F32)
    for r in parts[1:]:
        total = total + r[...].astype(F32)
    out[:rows, :] = total
    own = pl.ds(group_spot(nrow, ncol, rows, 0), 2 * rows)
    mirror = jnp.transpose(out[:sub, own])[sub : 2 * sub, :]
    out[sub:rows, own] = jnp.concatenate([mirror, out[sub:rows, own][:, sub:]], axis=1)
    mass = jnp.zeros((1, 1), F32)
    for k, part in enumerate(parts):
        note = part[sub:, own].astype(F32)[:, :sub]
        mass = mass + note[sub // 2 : sub // 2 + 1, :1] + note[sub * 3 // 4 : sub * 3 // 4 + 1, :1]
        line = jnp.concatenate([note[n : n + 1, :] for n in range(2 * ncol)], axis=1)
        vectors[:, pl.ds(group_spot(nrow, ncol, rows, k), ncol * rows)] = jnp.broadcast_to(line, (8, ncol * rows))
    out[rows : 2 * rows + 8, :] = raw_gram[...]
    out[2 * rows + 8 :, :] = jnp.broadcast_to(mass, (8, out.shape[1]))


def final_kernel(nrow, ncol, keys, mine, other, vectors, stud, scale, *refs):
    rows = stud.shape[0]
    if keys:
        out, raw, units = refs[-3:]
        assemble(nrow, ncol, rows, keys, refs, raw)
    else:
        raw, out, units = refs
    batch = mine.shape[1]
    squares = mine[2 * rows : 2 * rows + 8, :] + other[2 * rows : 2 * rows + 8, :]
    for at in range(0, batch, 128):
        inverse = 1.0 / jnp.sqrt(column(squares[:1, at : at + 128]))
        units[at : at + 128, :] = (raw[at : at + 128, :].astype(F32) * inverse).astype(BF16)
    at = pl.ds(group_spot(nrow, ncol, rows, 0), 2 * rows)
    own = (mine[2 * rows : 2 * rows + 8, at] + other[2 * rows : 2 * rows + 8, at])[:1, :rows]
    inverse = 1.0 / jnp.sqrt(column(own))
    mass = (mine[2 * rows + 8 : 2 * rows + 9, :1] + other[2 * rows + 8 : 2 * rows + 9, :1]) / batch
    gram = (mine[rows : 2 * rows, :] + other[rows : 2 * rows, :]) * (inverse * (1.0 / jnp.sqrt(squares[:1, :])))
    outer = (column(scale[...].astype(F32)) / mass) * vectors[:1, :]
    error_b = (gram - outer * (mine[:rows, :] + other[:rows, :])).astype(BF16)
    grads = 4.0 * jnp.dot(error_b, units[...], preferred_element_type=F32)
    along = 4.0 * jnp.sum(error_b.astype(F32) * gram, axis=1, keepdims=True)
    unit = stud[...].astype(F32) * inverse
    out[...] = (grads - along * unit) * inverse


def shards(student, teacher, scale):
    rows, half = student.shape
    nrow, ncol = lax.axis_size("row"), lax.axis_size("col")
    batch = rows * nrow * ncol
    part = teacher.shape[1] // nrow
    small = batch <= 2048
    sds = jax.ShapeDtypeStruct
    scale = scale.reshape(1, rows)

    def along_row(x, k):
        return lax.ppermute(x, "row", [(i, i ^ k) for i in range(nrow)])

    def along_col(x, c):
        return lax.ppermute(x, "col", [(i, (i - c) % ncol) for i in range(ncol)])

    def other_core(x):
        return lax.ppermute(x, "sub", [(0, 1), (1, 0)])

    def pack(xs, spans, after=()):
        shape = (sum(last - first for first, last in spans), half)
        return call(functools.partial(pack_kernel, spans), sds(shape, BF16), xs, after=after)

    def with_columns(x):
        return [x if c == 0 else along_col(x, c) for c in range(ncol)]

    middle, high = nrow // 2, rows * part // half
    order = list(range(middle, nrow)) + list(range(middle))
    riders = (1, middle)
    cuts = call(functools.partial(cut_kernel, nrow), [sds((rows, part), BF16)] * (nrow - 1), [teacher])
    ridden = call(ride_kernel, [sds((rows + high, half), BF16)] * 2, [student] + [cuts[k - 1] for k in riders])
    leaving = dict(enumerate(cuts, 1)) | dict(zip(riders, ridden))
    came = {k: along_row(leaving[k], k) for k in order if k}
    own = call(
        functools.partial(own_kernel, nrow),
        sds((rows + TAIL + high, half), BF16),
        [teacher, student, scale],
        after=[came[nrow - 1]],
    )
    columns = {0: with_columns(own)}
    for k in range(1, nrow):
        piece = came[k]
        if k in riders:
            piece = call(functools.partial(take_kernel, rows), sds((rows, part), BF16), [piece])
        columns[k] = with_columns(piece)
    partial = call(
        functools.partial(gram_kernel, nrow, ncol, rows, order),
        [sds((rows, batch), BF16 if k else F32) for k in range(nrow)],
        [columns[k][c] for k in order for c in range(ncol)],
        scratch=[pltpu.VMEM((batch, part), BF16), pltpu.VMEM((nrow * rows, part), BF16)],
    )
    returned = {k: along_row(partial[k], k) if k else partial[0] for k in order}

    near, far = came[1], came[middle]
    stack, keys, k, spans, got, got_keys = [student, far], [0, middle], middle // 2, [(0, rows)] * 2, [], []
    while k:
        first = 1 if k == 1 else 0
        sent = pack(stack[first:], spans[first:])
        got.append(along_row(sent, k))
        got_keys += [n ^ k for n in keys[first:]]
        stack, spans, keys = stack + got[-1:], spans + [(0, len(keys) * rows)], keys + [n ^ k for n in keys]
        k //= 2
    rest = pack([near, far] + got, [(0, rows)] * 2 + [(0, g.shape[0]) for g in got], after=[partial[0]])
    raw_keys = [[0], [1, middle] + got_keys]
    sources = [columns[0], with_columns(rest)]
    raw_refs = [x[c] for c in range(ncol) for x in sources]
    raw_gram, *all_raw = call(
        functools.partial(raw_gram_kernel, nrow, ncol, rows, raw_keys),
        [sds((rows + 8, batch), F32)] + ([sds((batch, half), BF16)] if small else []),
        raw_refs,
        scratch=[] if small else [pltpu.VMEM((batch, half), BF16)],
    )
    far_first = sorted(order, reverse=True)
    message, vectors = call(
        functools.partial(message_kernel, nrow, ncol, far_first),
        [sds((2 * rows + 16, batch), F32), sds((8, batch), F32)],
        [raw_gram] + [returned[k] for k in far_first],
    )
    return call(
        functools.partial(final_kernel, nrow, ncol, None if small else raw_keys),
        sds((rows, half), F32),
        [message, other_core(message), vectors, student, scale] + (all_raw if small else raw_refs),
        scratch=([] if small else [pltpu.VMEM((batch, half), BF16)]) + [pltpu.VMEM((batch, half), BF16)],
    )


def solution(mesh):
    spec = P(("groups", "row", "col"), "sub")
    return jax.shard_map(
        shards,
        mesh=mesh,
        in_specs=(spec, spec, P(("groups", "row", "col"))),
        out_specs=spec,
        check_vma=False,
    )
```
